32 devices in a mesh: dp: 8 (over z, x), chan: 4 (over y, core).
Axes of the slice: x: 2, y: 2, z: 4, core: 2. Of those that a mesh axis runs over, the one named last changes fastest.
Arguments:
- big_crops: bfloat16 [16, 32, 32, 512], P('dp', None, None, 'chan'), may hold values from -6 to 6
- small_crops: bfloat16 [32, 16, 16, 512], P('dp', None, None, 'chan'), may hold values from -6 to 6
- conv_down: bfloat16 [512, 3, 3, 1024], P(None, None, None, 'chan'), may hold values from -0.09375 to 0.09375
- split_a: bfloat16 [1024, 512], P(None, 'chan'), may hold values from -0.1875 to 0.1875
- split_b: bfloat16 [1024, 512], P(None, 'chan'), may hold values from -0.1875 to 0.1875
- neck_in: bfloat16 [512, 512], P(None, 'chan'), may hold values from -0.25 to 0.25
- neck_conv: bfloat16 [512, 3, 3, 512], P(None, None, None, 'chan'), may hold values from -0.09375 to 0.09375
- norm_wide: float32 [2, 1024], replicated, may hold values from 0.25 to 1.75
- norm_neck: float32 [2, 2, 512], replicated, may hold values from 0.25 to 1.75
- cot_big: bfloat16 [2, 16, 16, 16, 512], P(None, 'dp', None, None, 'chan'), may hold values from -6 to 6
- cot_small: bfloat16 [2, 32, 8, 8, 512], P(None, 'dp', None, None, 'chan'), may hold values from -6 to 6
- mom_down: float32 [512, 3, 3, 1024], P('dp', None, None, 'chan'), may hold values from -0.01171875 to 0.01171875
- mom_a: float32 [1024, 512], P('dp', 'chan'), may hold values from -0.0234375 to 0.0234375
- mom_b: float32 [1024, 512], P('dp', 'chan'), may hold values from -0.0234375 to 0.0234375
- mom_in: float32 [512, 512], P('dp', 'chan'), may hold values from -0.03125 to 0.03125
- mom_conv: float32 [512, 3, 3, 512], P('dp', None, None, 'chan'), may hold values from -0.01171875 to 0.01171875
Outputs:
- big_out: bfloat16 [2, 16, 16, 16, 512], P(None, 'dp', None, None, 'chan')
- small_out: bfloat16 [2, 32, 8, 8, 512], P(None, 'dp', None, None, 'chan')
- grad_big: float32 [16, 32, 32, 512], P('dp', None, None, 'chan')
- grad_small: float32 [32, 16, 16, 512], P('dp', None, None, 'chan')
- new_down: float32 [512, 3, 3, 1024], P('dp', None, None, 'chan')
- new_a: float32 [1024, 512], P('dp', 'chan')
- new_b: float32 [1024, 512], P('dp', 'chan')
- new_in: float32 [512, 512], P('dp', 'chan')
- new_conv: float32 [512, 3, 3, 512], P('dp', None, None, 'chan')
- next_down: float32 [512, 3, 3, 1024], P('dp', None, None, 'chan')
- next_a: float32 [1024, 512], P('dp', 'chan')
- next_b: float32 [1024, 512], P('dp', 'chan')
- next_in: float32 [512, 512], P('dp', 'chan')
- next_conv: float32 [512, 3, 3, 512], P('dp', None, None, 'chan')
- wide_norm_grad: float32 [2, 1024], P(None, 'chan')
- neck_norm_grad: float32 [2, 2, 512], P(None, None, 'chan')
- layer_norms: float32 [2, 5], replicated
The draws below stay inside these ranges and needn't reach their ends.
All inputs are finite; a program needn't handle non-finite values.
Results may differ from the reference program's by a relative error of at most 0.02.
Values may be sent and summed in bfloat16 or wider, within the bound.
A program may use at most 192 MiB of HBM per device.

```python
import jax
import jax.numpy as jnp
from jax import lax

CH = 512
WIDE = 1024
BIG_SIDE = 32
SMALL_SIDE = 16
BIG = 16
SMALL = 32


def levels(stream_key, dims, shards, smallest, largest):
    loudness, own = 1.0, jax.random.fold_in(stream_key, 6)
    for dim, blocks in shards:
        heights = jnp.exp(jax.random.uniform(jax.random.fold_in(own, dim), (blocks,), jnp.float32, smallest / len(shards), largest / len(shards)))
        loudness = loudness * jnp.repeat(heights, dims[dim] // blocks).reshape([-1 if axis == dim else 1 for axis in range(len(dims))])
    return loudness


def gaussian(own_key, dims, scale, bound, cuts=(), kind=jnp.bfloat16):
    values = jax.random.normal(own_key, dims, jnp.float32) * scale
    if len(cuts) > 0:
        values = levels(own_key, dims, cuts, -0.22, 0.18) * values
    return jnp.clip(values, min=-bound, max=bound).astype(kind)


def setup_inputs(seed: int = 0) -> dict:
    splits = jax.random.split(jax.random.key(seed), 17)
    return {
        "big_crops": gaussian(splits[0], (BIG, BIG_SIDE, BIG_SIDE, CH), 1.0, 6.0, ((0, 8), (3, 4))),
        "small_crops": gaussian(splits[1], (SMALL, SMALL_SIDE, SMALL_SIDE, CH), 1.0, 6.0, ((0, 8), (3, 4))),
        "conv_down": gaussian(splits[2], (CH, 3, 3, WIDE), (9 * CH) ** -0.5, 0.09375, ((3, 4),)),
        "split_a": gaussian(splits[3], (WIDE, CH), WIDE ** -0.5, 0.1875, ((1, 4),)),
        "split_b": gaussian(splits[4], (WIDE, CH), WIDE ** -0.5, 0.1875, ((1, 4),)),
        "neck_in": gaussian(splits[5], (CH, CH), CH ** -0.5, 0.25, ((1, 4),)),
        "neck_conv": gaussian(splits[6], (CH, 3, 3, CH), (9 * CH) ** -0.5, 0.09375, ((3, 4),)),
        "norm_wide": jnp.clip(1.0 + 0.15 * jax.random.normal(splits[7], (2, WIDE), jnp.float32), 0.25, 1.75),
        "norm_neck": jnp.clip(1.0 + 0.15 * jax.random.normal(splits[8], (2, 2, CH), jnp.float32), 0.25, 1.75),
        "cot_big": gaussian(splits[9], (2, BIG, BIG_SIDE // 2, BIG_SIDE // 2, CH), 1.0, 6.0, ((1, 8), (4, 4))),
        "cot_small": gaussian(splits[10], (2, SMALL, SMALL_SIDE // 2, SMALL_SIDE // 2, CH), 1.0, 6.0, ((1, 8), (4, 4))),
        "mom_down": gaussian(splits[11], (CH, 3, 3, WIDE), 0.002, 0.01171875, ((0, 8), (3, 4)), jnp.float32),
        "mom_a": gaussian(splits[12], (WIDE, CH), 0.004, 0.0234375, ((0, 8), (1, 4)), jnp.float32),
        "mom_b": gaussian(splits[13], (WIDE, CH), 0.004, 0.0234375, ((0, 8), (1, 4)), jnp.float32),
        "mom_in": gaussian(splits[14], (CH, CH), 0.005, 0.03125, ((0, 8), (1, 4)), jnp.float32),
        "mom_conv": gaussian(splits[15], (CH, 3, 3, CH), 0.002, 0.01171875, ((0, 8), (3, 4)), jnp.float32),
    }


@jax.custom_vjp
def low(v):
    return lax.optimization_barrier(v.astype(jnp.bfloat16)).astype(jnp.float32)

@jax.custom_vjp
def low_back(v):
    return v

def low_keep(v):
    return (low(v), None)

def low_pass(kept, grad):
    return (grad,)

def back_keep(v):
    return (v, None)

def back_low(kept, grad):
    return (low(grad),)
low.defvjp(low_keep, low_pass)
low_back.defvjp(back_keep, back_low)
EPSILON = 1e-05
MOMENTUM = 0.9
DECAY = 0.0005
TRUST = 0.1

def convolve(images, kernel, stride):
    return lax.conv_general_dilated(images, kernel, (stride, stride), ((1, 1), (1, 1)), dimension_numbers=('NHWC', 'IHWO', 'NHWC'), precision=lax.Precision.HIGHEST)

def mish(values):
    return values * jnp.tanh(jax.nn.softplus(values))

def batch_norm(values, params):
    average = lax.optimization_barrier(jnp.mean(values, axis=0))
    variance = lax.optimization_barrier(jnp.mean((values - average) ** 2, axis=0))
    return (values - average) * lax.rsqrt(variance + EPSILON) * params[0] + params[1]

def product(left, right):
    return jnp.dot(left, right, precision=lax.Precision.HIGHEST)

def forward(big_crops, small_crops, conv_down, split_a, split_b, neck_in, neck_conv, norm_wide, norm_neck):
    big_count, big_half = (big_crops.shape[0], big_crops.shape[1] // 2)
    small_count, small_half = (small_crops.shape[0], small_crops.shape[1] // 2)
    split_row = big_count * big_half * big_half
    big_rows = convolve(big_crops, conv_down, 2).reshape(split_row, -1)
    small_rows = convolve(small_crops, conv_down, 2).reshape(small_count * small_half * small_half, -1)
    down_rows = low_back(jnp.concatenate([big_rows, small_rows], 0))
    wide_act = low(mish(batch_norm(down_rows, norm_wide)))
    split_out = product(wide_act, split_a)
    part_b = low_back(low(product(wide_act, split_b)))
    neck_rows = low_back(product(part_b, neck_in))
    first_act = low(mish(batch_norm(neck_rows, norm_neck[0])))
    big_conv = convolve(first_act[:split_row].reshape(big_count, big_half, big_half, -1), neck_conv, 1)
    small_conv = convolve(first_act[split_row:].reshape(small_count, small_half, small_half, -1), neck_conv, 1)
    conv_rows = low_back(jnp.concatenate([big_conv.reshape(split_row, -1), small_conv.reshape(small_count * small_half * small_half, -1)], 0))
    block_out = part_b + mish(batch_norm(conv_rows, norm_neck[1]))
    return (split_out, block_out)

def lars(weight, gradient, moment):
    weight_norm = jnp.sqrt(jnp.sum(weight * weight))
    grad_norm = jnp.sqrt(jnp.sum(gradient * gradient))
    step_rate = TRUST * weight_norm / (grad_norm + DECAY * weight_norm)
    next_moment = MOMENTUM * moment + step_rate * (gradient + DECAY * weight)
    return (weight - next_moment, next_moment, weight_norm, grad_norm)

def reference(big_crops, small_crops, conv_down, split_a, split_b, neck_in, neck_conv, norm_wide, norm_neck, cot_big, cot_small, mom_down, mom_a, mom_b, mom_in, mom_conv):
    weights = [conv_down.astype(jnp.float32), split_a.astype(jnp.float32), split_b.astype(jnp.float32), neck_in.astype(jnp.float32), neck_conv.astype(jnp.float32)]
    outputs, pullback = jax.vjp(forward, big_crops.astype(jnp.float32), small_crops.astype(jnp.float32), weights[0], weights[1], weights[2], weights[3], weights[4], norm_wide, norm_neck)
    split_out, block_out = outputs
    big_count, big_half = (cot_big.shape[1], cot_big.shape[2])
    small_count, small_half = (cot_small.shape[1], cot_small.shape[2])
    split_row = big_count * big_half * big_half
    small_row = small_count * small_half * small_half
    grad_a = jnp.concatenate([cot_big[0].reshape(split_row, -1), cot_small[0].reshape(small_row, -1)], 0).astype(jnp.float32)
    grad_blk = jnp.concatenate([cot_big[1].reshape(split_row, -1), cot_small[1].reshape(small_row, -1)], 0).astype(jnp.float32)
    grads = pullback((grad_a, grad_blk))
    big_out = jnp.stack([split_out[:split_row].reshape(big_count, big_half, big_half, -1), block_out[:split_row].reshape(big_count, big_half, big_half, -1)]).astype(jnp.bfloat16)
    small_out = jnp.stack([split_out[split_row:].reshape(small_count, small_half, small_half, -1), block_out[split_row:].reshape(small_count, small_half, small_half, -1)]).astype(jnp.bfloat16)
    moments = [mom_down, mom_a, mom_b, mom_in, mom_conv]
    updated = [lars(weights[layer], grads[2 + layer], moments[layer]) for layer in range(5)]
    layer_norms = jnp.stack([jnp.stack([item[2] for item in updated]), jnp.stack([item[3] for item in updated])])
    return (big_out, small_out, grads[0], grads[1], updated[0][0], updated[1][0], updated[2][0], updated[3][0], updated[4][0], updated[0][1], updated[1][1], updated[2][1], updated[3][1], updated[4][1], grads[7], grads[8], layer_norms)
```

```python
import functools

import jax
import jax.numpy as jnp
from jax import lax
from jax.experimental import pallas as pl
from jax.experimental.pallas import tpu as pltpu
from jax.sharding import PartitionSpec as P

EPSILON = 1e-05
MOMENTUM = 0.9
DECAY = 0.0005
TRUST = 0.1
F32 = jnp.float32
BF16 = jnp.bfloat16
MESH = pl.DeviceIdType.MESH
PLANES = (3, 1, 2, 0)


def dot_nn(left, right):
    return lax.dot_general(left, right, (((1,), (0,)), ((), ())), preferred_element_type=F32)


def dot_nt(left, right):
    return lax.dot_general(left, right, (((1,), (1,)), ((), ())), preferred_element_type=F32)


def dot_tn(left, right):
    return lax.dot_general(left, right, (((0,), (0,)), ((), ())), preferred_element_type=F32)


def mish_parts(v):
    u = jnp.exp(-jnp.abs(v))
    pos = v >= 0
    num = jnp.where(pos, 1.0 + 2.0 * u, u * (u + 2.0))
    rest = jnp.where(pos, 2.0 * u * u, 2.0)
    den = num + rest
    inv = 1.0 / den
    tangent = num * inv
    slope = tangent + v * (rest * (den + num) * inv * inv) * (jnp.where(pos, 1.0, u) / (1.0 + u))
    return v * tangent, slope


def plane_taps(p):
    rows = ((0, -1), (2, 0)) if p // 2 else ((1, 0),)
    cols = ((0, -1), (2, 0)) if p % 2 else ((1, 0),)
    return [(r * 3 + s, di, dj) for r, di in rows for s, dj in cols]


def group_of(di, dj):
    return (2 if di else 0) + (1 if dj else 0)


class Geometry:
    def __init__(self, big, small, down, neck, n_dp):
        self.nb, self.hb = big[0], big[1] // 2
        self.ns, self.hs = small[0], small[1] // 2
        self.cb = big[3]
        self.ch = down[0]
        self.wc = down[3]
        self.nc = neck[3]
        self.n = n_dp
        self.big_rows = self.nb * self.hb * self.hb
        self.small_rows = self.ns * self.hs * self.hs
        self.rows = self.big_rows + self.small_rows
        self.total_rows = self.rows * n_dp
        self.tiles = [
            (i * self.hb * self.hb, self.hb * self.hb, 1, self.hb) for i in range(self.nb)
        ] + [(self.big_rows, self.small_rows, self.ns, self.hs)]


def shift_tile(value, tile, di, dj):
    _, rows, images, side = tile
    cols = value.shape[-1]
    if di:
        v = value.reshape(images, side, side, cols)
        blank = jnp.zeros((images, 1, side, cols), value.dtype)
        if di < 0:
            v = jnp.concatenate([blank, v[:, :-1]], axis=1)
        else:
            v = jnp.concatenate([v[:, 1:], blank], axis=1)
        value = v.reshape(rows, cols)
    if dj:
        v = pltpu.roll(value, 1 if dj < 0 else rows - 1, 0).reshape(rows // side, side, cols)
        at = lax.broadcasted_iota(jnp.int32, (1, side, cols), 1)
        keep = at >= 1 if dj < 0 else at < side - 1
        value = jnp.where(keep, v, 0.0).reshape(rows, cols)
    return value


def bits_of(n):
    return n.bit_length() - 1


def halving_plan(n, order):
    left = list(range(bits_of(n)))
    plan = []
    for bit in order:
        at = left.index(bit)
        plan.append((bit, 1 << (len(left) - 1 - at), 1 << at))
        left.remove(bit)
    return plan


def scratch_plan(g):
    n = g.n
    R = g.rows
    s = {}
    s["raw_big"] = ((g.nb * g.hb * 2, 2 * g.hb, g.cb), BF16)
    s["raw_small"] = ((g.ns * g.hs * 2, 2 * g.hs, g.cb), BF16)
    s["wide_big"] = ((g.nb * g.hb, 2, 2 * g.hb, g.cb), F32)
    s["wide_small"] = ((g.ns * g.hs, 2, 2 * g.hs, g.cb), F32)
    s["xg"] = ((4, 4, R, g.cb), BF16)
    s["wv"] = ((9, g.ch, g.wc), BF16)
    s["wn"] = ((g.ch, 9 * g.nc), BF16)
    s["ab"] = ((2 * g.ch, 2 * g.nc), BF16)
    s["nin"] = ((4, g.ch, g.nc), BF16)
    s["sar"] = ((4, g.wc, g.nc), BF16)
    s["sbr"] = ((4, g.wc, g.nc), BF16)
    s["cmat"] = ((4, g.wc, g.nc), BF16)
    s["pw"] = ((2, 4 * g.wc), F32)
    s["pn"] = ((2, 2, 4 * g.nc), F32)
    s["acc"] = ((4, R, g.wc), F32)
    s["n1"] = ((R, g.wc), F32)
    s["s1"] = ((R, g.wc), F32)
    s["wg"] = ((4, R, g.wc), BF16)
    for k in ("f", "b"):
        s["rs_send" + k] = ((2, R, g.nc), BF16)
        s["rs_recv" + k] = ((2, R, g.nc), BF16)
        s["rs_ys" + k] = ((R, g.nc), BF16)
        s["rs_yr" + k] = ((R, g.nc), BF16)
    s["rs_keep"] = ((2, R, g.nc), F32)
    s["n2"] = ((R, g.nc), F32)
    s["s2"] = ((R, g.nc), F32)
    s["fg"] = ((4, R, g.nc), BF16)
    s["yb"] = ((R, 9 * g.nc), F32)
    s["n3"] = ((R, g.nc), F32)
    s["s3"] = ((R, g.nc), F32)
    s["cg"] = ((R, 9 * g.nc), BF16)
    s["ga"] = ((4, R, g.nc), BF16)
    s["gb"] = ((4, R, g.nc), BF16)
    s["pb"] = ((4, R, g.nc), BF16)
    s["ng"] = ((4, R, g.nc), BF16)
    s["abg"] = ((R, 2 * g.nc), BF16)
    s["u"] = ((R, g.wc), F32)
    s["gsh"] = ((4, R, g.wc), BF16)
    s["so"] = ((2, R, g.nc), BF16)
    s["cs"] = ((4, 2, R, g.cb), BF16)
    s["cr"] = ((4, 2, R, g.cb), BF16)
    s["cys"] = ((4, R, g.cb), BF16)
    s["cyr"] = ((4, R, g.cb), BF16)
    s["ckeep"] = ((4, 2, R, g.cb), F32)
    s["st"] = ((6, n, 8, g.wc), F32)
    s["nm"] = ((n, 16, 128), F32)
    s["nq"] = ((4, 16, 128), F32)
    rc = {
        "down": (9, g.ch // n, g.wc),
        "conv": (1, g.ch // n, 9 * g.nc),
        "ab": (1, 2 * g.ch // n, 2 * g.nc),
        "in": (1, g.ch // n, g.nc),
    }
    for name, (count, rows, cols) in rc.items():
        for stage, (_, high, low) in enumerate(halving_plan(n, tuple(range(bits_of(n))))):
            s[f"h_{name}_s{stage}"] = ((count, high, 2, low, rows, cols), BF16)
            s[f"h_{name}_r{stage}"] = ((count, high, low, rows, cols), BF16)
        s[f"g_{name}"] = ((count, rows, cols), F32)
    s["m_down"] = ((9, g.ch // n, g.wc), F32)
    s["m_a"] = ((2 * g.ch // n, g.nc), F32)
    s["m_b"] = ((2 * g.ch // n, g.nc), F32)
    s["m_in"] = ((g.ch // n, g.nc), F32)
    s["m_conv"] = ((9, g.ch // n, g.nc), F32)
    s["o_down"] = ((2, 9, g.ch // n, g.wc), F32)
    s["o_a"] = ((2, 2 * g.ch // n, g.nc), F32)
    s["o_b"] = ((2, 2 * g.ch // n, g.nc), F32)
    s["o_in"] = ((2, g.ch // n, g.nc), F32)
    s["o_conv"] = ((2, 9, g.ch // n, g.nc), F32)
    s["k_down"] = ((9, g.ch // n, g.wc), BF16)
    s["k_a"] = ((2 * g.ch // n, g.nc), BF16)
    s["k_b"] = ((2 * g.ch // n, g.nc), BF16)
    s["k_in"] = ((g.ch // n, g.nc), BF16)
    s["k_conv"] = ((9, g.ch // n, g.nc), BF16)
    return s


N_SEMS = 400


def mega(g, names, *refs):
    (
        big, small, w_down, w_a, w_b, w_in, w_conv, p_wide, p_neck, c_big, c_small,
        m_down, m_a, m_b, m_in, m_conv,
    ) = refs[:16]
    (
        o_big, o_small, o_gbig, o_gsmall, o_ndown, o_na, o_nb, o_nin, o_nconv,
        o_mdown, o_ma, o_mb, o_min, o_mconv, o_wn, o_nn, o_ln,
    ) = refs[16:33]
    S = dict(zip(names, refs[33:-1], strict=True))
    sems = refs[-1]
    n, R, nc, wc, cb = g.n, g.rows, g.nc, g.wc, g.cb
    dp = lax.axis_index("dp")
    ch = lax.axis_index("chan")
    core = lax.rem(ch, 2)
    half = lax.div(ch, 2)
    sib = half * 2 + (1 - core)
    yp = (1 - half) * 2 + core
    diag = (1 - half) * 2 + (1 - core)
    other = 1 - half

    used = [0]
    pending = []

    def sem():
        used[0] += 1
        return sems.at[used[0] - 1]

    def local(src, dst):
        copy = pltpu.make_async_copy(src, dst, sem())
        copy.start()
        return copy

    def remote(src, dst, device):
        copy = pltpu.make_async_remote_copy(
            src_ref=src, dst_ref=dst, send_sem=sem(), recv_sem=sem(),
            device_id=device, device_id_type=MESH,
        )
        pending.append(copy)
        return copy

    ld_big = local(big, S["raw_big"])
    ld_small = local(small, S["raw_small"])
    ld_wv = local(w_down, S["wv"])
    ld_ab = [
        local(w_a, S["ab"].at[:, pl.ds(0, nc)]),
        local(w_b, S["ab"].at[:, pl.ds(nc, nc)]),
    ]
    ld_in = local(w_in, S["nin"].at[ch])
    ld_p = [local(p_wide, S["pw"]), local(p_neck, S["pn"])]
    ld_wn = [local(w_conv.at[t], S["wn"].at[:, pl.ds(t * nc, nc)]) for t in range(9)]
    br, sr = g.big_rows, g.small_rows
    ld_c = [
        local(c_big.at[k], S[nm].at[ch, pl.ds(0, br)]) for k, nm in ((0, "ga"), (1, "gb"))
    ] + [
        local(c_small.at[k], S[nm].at[ch, pl.ds(br, sr)]) for k, nm in ((0, "ga"), (1, "gb"))
    ]
    ld_m = [
        local(m_down, S["m_down"]), local(m_a, S["m_a"]), local(m_b, S["m_b"]),
        local(m_in, S["m_in"]), local(m_conv, S["m_conv"]),
        local(w_down.at[:, pl.ds(dp * (g.ch // n), g.ch // n)], S["k_down"]),
        local(w_a.at[pl.ds(dp * (2 * g.ch // n), 2 * g.ch // n)], S["k_a"]),
        local(w_b.at[pl.ds(dp * (2 * g.ch // n), 2 * g.ch // n)], S["k_b"]),
        local(w_in.at[pl.ds(dp * (g.ch // n), g.ch // n)], S["k_in"]),
        local(w_conv.at[:, pl.ds(dp * (g.ch // n), g.ch // n)], S["k_conv"]),
    ]

    peers = [(dp, sib), (dp, yp), (dp, diag)] + [
        (lax.rem(dp + k, n), ch) for k in range(1, n)
    ]
    bar = pltpu.get_barrier_semaphore()
    for peer in peers:
        pl.semaphore_signal(bar, inc=1, device_id=peer, device_id_type=MESH)

    xg = S["xg"]
    ld_big.wait()
    S["wide_big"][...] = S["raw_big"][...].astype(F32).reshape(S["wide_big"].shape)
    ld_small.wait()
    S["wide_small"][...] = S["raw_small"][...].astype(F32).reshape(S["wide_small"].shape)

    def split_plane(p):
        pr, pc = p // 2, p % 2
        xg[ch, p, 0:br] = (
            S["wide_big"][:, pr, pl.ds(pc, g.hb, stride=2), :].reshape(br, cb).astype(BF16)
        )
        xg[ch, p, br:R] = (
            S["wide_small"][:, pr, pl.ds(pc, g.hs, stride=2), :].reshape(sr, cb).astype(BF16)
        )

    class Gather:
        def __init__(self, block):
            self.to_sib = remote(block(ch), block(ch), (dp, sib))
            self.to_far = remote(block(ch), block(ch), (dp, yp))
            self.onward = remote(block(yp), block(yp), (dp, sib))

        def start(self):
            self.to_far.start()
            self.to_sib.start()

        def forward(self):
            self.to_far.wait_recv()
            self.onward.start()

        def near(self):
            self.to_sib.wait_recv()

        def far(self):
            self.onward.wait_recv()

    crops = {p: Gather(lambda c, p=p: xg.at[c, p]) for p in PLANES}
    split_plane(PLANES[0])
    pl.semaphore_wait(bar, len(peers))
    crops[PLANES[0]].start()
    for p in PLANES[1:]:
        split_plane(p)
        crops[p].start()

    ld_in.wait()
    neck_in = Gather(lambda c: S["nin"].at[c])
    for c in ld_ab:
        c.wait()

    def rows_to(buf, lane):
        out = []
        for dev in (yp, diag, sib):
            out.append(
                remote(
                    S["ab"].at[pl.ds(dev * wc, wc), pl.ds(lane, nc)], S[buf].at[ch], (dp, dev)
                )
            )
        S[buf][ch] = S["ab"][pl.ds(ch * wc, wc), lane : lane + nc]
        return out

    b_rows = rows_to("sbr", nc)
    a_rows = rows_to("sar", 0)
    for c in b_rows:
        c.start()
    neck_in.start()

    ld_wv.wait()
    wv, acc = S["wv"], S["acc"]

    def conv_part(side, p, first):
        x = jnp.concatenate([xg[2 * side, p], xg[2 * side + 1, p]], axis=1)
        for tap, di, dj in plane_taps(p):
            res = dot_nn(x, wv[tap, pl.ds(side * 2 * cb, 2 * cb), :])
            k = group_of(di, dj)
            if first:
                acc[k] = res
            else:
                acc[k] += res

    for p in PLANES:
        crops[p].near()
        conv_part(half, p, p == PLANES[0])
    for p in PLANES[:-1]:
        crops[p].forward()
        crops[p].far()
        conv_part(other, p, False)
    for tile in g.tiles:
        at = pl.ds(tile[0], tile[1])
        inner = acc[1, at] + shift_tile(acc[3, at], tile, -1, 0)
        acc[2, at] = shift_tile(acc[2, at], tile, -1, 0) + shift_tile(inner, tile, 0, -1)
    p = PLANES[-1]
    crops[p].forward()
    crops[p].far()
    conv_part(other, p, False)
    acc[0] = acc[0] + acc[2]

    st = S["st"]

    def exchange(phase, first, second, cols):
        st[phase, dp] = jnp.zeros((8, wc), F32)
        st[phase, dp, 0:1, 0:cols] = first
        st[phase, dp, 1:2, 0:cols] = second
        ssem, rsem = sem(), sem()
        mine = st.at[phase, dp, :, pl.ds(0, cols)]
        for k in range(1, n):
            pltpu.make_async_remote_copy(
                src_ref=mine, dst_ref=mine, send_sem=ssem, recv_sem=rsem,
                device_id=(lax.rem(dp + k, n), ch), device_id_type=MESH,
            ).start()
        some = st.at[phase, pl.ds(0, n - 1), :, pl.ds(0, cols)]

        def finish():
            pltpu.make_async_copy(some, some, rsem).wait()
            pltpu.make_async_copy(some, some, ssem).wait()
            return st[phase, :, :, 0:cols]

        return finish

    def norm_start(phase, ref):
        cols = ref.shape[-1]
        mean = jnp.sum(ref[...], axis=0, keepdims=True) * (1.0 / R)
        dev = ref[...] - mean
        return exchange(phase, mean, jnp.sum(dev * dev, axis=0, keepdims=True), cols)

    def norm_finish(finish):
        v = finish()
        tot = jnp.sum(v, axis=0)
        mean = tot[0:1] * (1.0 / n)
        off = v - mean[None]
        spread = jnp.sum(off * off, axis=0)[0:1]
        var = (tot[1:2] + R * spread) * (1.0 / g.total_rows)
        return mean, lax.rsqrt(var + EPSILON)

    def sums_finish(finish):
        tot = jnp.sum(finish(), axis=0)
        return tot[0:1], tot[1:2]

    fin = norm_start(0, acc.at[0])
    for c in ld_p:
        c.wait()
    gain1 = S["pw"][0:1, pl.ds(ch * wc, wc)]
    bias1 = S["pw"][1:2, pl.ds(ch * wc, wc)]

    neck_in.forward()
    neck_in.near()
    neck_in.far()
    for c in b_rows:
        c.wait_recv()
    rows_b = jnp.concatenate([S["sbr"][k] for k in range(4)], axis=1)
    for k in range(4):
        S["cmat"][k] = dot_nn(rows_b, S["nin"][k]).astype(BF16)

    mean1, inv1 = norm_finish(fin)
    wg = S["wg"]
    for t0 in range(0, R, 256):
        at = pl.ds(t0, 256)
        normed = (acc[0, at] - mean1) * inv1
        S["n1"][at] = normed
        act, slope = mish_parts(normed * gain1 + bias1)
        wg[ch, at] = act.astype(BF16)
        S["s1"][at] = slope

    def reduce_chan(k, pair):
        send, recv = S["rs_send" + k], S["rs_recv" + k]
        ys, yr, keep = S["rs_ys" + k], S["rs_yr" + k], S["rs_keep"]
        c0 = remote(send.at[0], recv.at[0], (dp, sib))
        c1 = remote(send.at[1], recv.at[1], (dp, sib))
        cy = remote(ys, yr, (dp, yp))
        part = pair(diag, sib)
        send[0] = part[:, :nc].astype(BF16)
        c0.start()
        send[1] = part[:, nc:].astype(BF16)
        c1.start()
        part = pair(yp, ch)
        keep[0] = part[:, :nc]
        keep[1] = part[:, nc:]
        c0.wait_recv()
        ys[...] = (keep[0] + recv[0].astype(F32)).astype(BF16)
        cy.start()
        c1.wait_recv()
        keep[1] += recv[1].astype(F32)

        def finish():
            cy.wait_recv()
            keep[1] += yr[...].astype(F32)

        return finish

    def neck_pair(d0, d1):
        return dot_nn(
            wg[ch], jnp.concatenate([S["cmat"][d0], S["cmat"][d1]], axis=1)
        )

    rs_fin = reduce_chan("f", neck_pair)
    for c in ld_c:
        c.wait()
    gb_g = Gather(lambda c: S["gb"].at[c])
    ga_g = Gather(lambda c: S["ga"].at[c])
    wide_g = Gather(lambda c: wg.at[c])
    gb_g.start()
    rs_fin()
    z2 = S["rs_keep"].at[1]
    fin = norm_start(1, z2)
    gain2 = S["pn"][0, 0:1, pl.ds(ch * nc, nc)]
    bias2 = S["pn"][0, 1:2, pl.ds(ch * nc, nc)]
    gain3 = S["pn"][1, 0:1, pl.ds(ch * nc, nc)]
    bias3 = S["pn"][1, 1:2, pl.ds(ch * nc, nc)]
    mean2, inv2 = norm_finish(fin)
    fg = S["fg"]
    for t0 in range(0, R, 256):
        at = pl.ds(t0, 256)
        normed = (z2[at] - mean2) * inv2
        S["n2"][at] = normed
        act, slope = mish_parts(normed * gain2 + bias2)
        fg[ch, at] = act.astype(BF16)
        S["s2"][at] = slope
    first_g = Gather(lambda c: fg.at[c])
    first_g.start()
    gb_g.forward()
    wide_g.start()

    for c in ld_wn:
        c.wait()
    wn, yb = S["wn"], S["yb"]

    def neck_part(side, first):
        x = jnp.concatenate([fg[2 * side], fg[2 * side + 1]], axis=1)
        w = wn[pl.ds(side * 2 * nc, 2 * nc), :]
        if first:
            yb[...] = dot_nn(x, w)
        else:
            yb[...] += dot_nn(x, w)

    first_g.near()
    neck_part(half, True)
    first_g.forward()
    first_g.far()
    neck_part(other, False)
    z3 = S["n3"]
    for tile in g.tiles:
        at = pl.ds(tile[0], tile[1])
        cols = []
        for s in range(3):
            cols.append(
                yb[at, (3 + s) * nc : (4 + s) * nc]
                + shift_tile(yb[at, s * nc : (s + 1) * nc], tile, -1, 0)
                + shift_tile(yb[at, (6 + s) * nc : (7 + s) * nc], tile, 1, 0)
            )
        z3[at] = (
            cols[1] + shift_tile(cols[0], tile, 0, -1) + shift_tile(cols[2], tile, 0, 1)
        )
    fin = norm_start(2, z3)
    mean3, inv3 = norm_finish(fin)
    q_tot = jnp.zeros((1, nc), F32)
    qn_tot = jnp.zeros((1, nc), F32)
    for t0 in range(0, R, 256):
        at = pl.ds(t0, 256)
        normed = (z3[at] - mean3) * inv3
        act, slope = mish_parts(normed * gain3 + bias3)
        q = S["gb"][ch, at].astype(F32) * slope
        z3[at] = normed
        S["s3"][at] = q
        S["yb"][at, 0:nc] = act
        q_tot += jnp.sum(q, axis=0, keepdims=True)
        qn_tot += jnp.sum(q * normed, axis=0, keepdims=True)
    fin = exchange(3, qn_tot, q_tot, nc)

    wide_g.near()
    wide_g.forward()
    for c in a_rows:
        c.start()
    wide_g.far()
    ga_g.start()
    so, pb = S["so"], S["pb"]
    split = dot_nn(
        jnp.concatenate([wg[k] for k in range(4)], axis=1), S["ab"][...]
    )
    so[0] = split[:, :nc].astype(BF16)
    part = split[:, nc:].astype(BF16)
    pb[ch] = part
    so[1] = (part.astype(F32) + yb[:, 0:nc]).astype(BF16)
    outs = []
    for k in range(2):
        outs.append(local(so.at[k, pl.ds(0, br)], o_big.at[k]))
        outs.append(local(so.at[k, pl.ds(br, sr)], o_small.at[k]))
    part_g = Gather(lambda c: pb.at[c])

    def grad_in(q, normed, gain, inv, qn_sum, q_sum):
        return gain * inv * (
            q - q_sum * (1.0 / g.total_rows) - normed * (qn_sum * (1.0 / g.total_rows))
        )

    qn3, q3 = sums_finish(fin)
    cg = S["cg"]
    for tile in g.tiles:
        at = pl.ds(tile[0], tile[1])
        v = grad_in(S["s3"][at], z3[at], gain3, inv3, qn3, q3)
        v = v.astype(BF16).astype(F32)
        for r in range(3):
            vi = shift_tile(v, tile, 1 - r, 0)
            for s in range(3):
                t = r * 3 + s
                cg[at, t * nc : (t + 1) * nc] = shift_tile(vi, tile, 0, 1 - s).astype(BF16)

    def back_pair(d0, d1):
        w = jnp.concatenate([wn[pl.ds(d0 * nc, nc), :], wn[pl.ds(d1 * nc, nc), :]], axis=0)
        return dot_nt(cg[...], w)

    rs_fin = reduce_chan("b", back_pair)

    class Halving:
        def __init__(self, name, item, order):
            self.name, self.item = name, item
            self.plan = halving_plan(n, order)
            self.copies = []
            for i, (bit, high, low) in enumerate(self.plan):
                own = lax.rem(lax.div(dp, 1 << bit), 2)
                peer = dp + (1 - 2 * own) * (1 << bit)
                send = S[f"h_{name}_s{i}"]
                recv = S[f"h_{name}_r{i}"]
                self.copies.append(remote(send.at[item, :, 1 - own], recv.at[item], (peer, ch)))

        def start(self, stage=0):
            self.copies[stage].start()

        def step(self, stage):
            bit, high, low = self.plan[stage]
            own = lax.rem(lax.div(dp, 1 << bit), 2)
            send = S[f"h_{self.name}_s{stage}"]
            recv = S[f"h_{self.name}_r{stage}"]
            self.copies[stage].wait_recv()
            total = send[self.item, :, own].astype(F32) + recv[self.item].astype(F32)
            if stage + 1 < len(self.plan):
                after = S[f"h_{self.name}_s{stage + 1}"]
                after[self.item] = total.astype(BF16).reshape(after.shape[1:])
                self.start(stage + 1)
            else:
                S[f"g_{self.name}"][self.item] = total[0, 0]

    n_bits = bits_of(n)
    x_first = tuple(range(n_bits))
    z_first = tuple(range(1, n_bits)) + (0,)

    def put(name, item, first_block, value):
        ref = S[f"h_{name}_s0"]
        _, high, _, low, rows, cols = ref.shape
        at = first_block // (2 * low)
        count = value.shape[0] // (rows * 2 * low)
        ref[item, at : at + count] = value.astype(BF16).reshape(count, 2, low, rows, cols)

    h_conv = Halving("conv", 0, x_first)
    for s in range(2):
        x = jnp.concatenate([fg[2 * s], fg[2 * s + 1]], axis=1)
        put("conv", 0, s * (n // 2), dot_tn(x, cg[...]))
    h_conv.start()

    rs_fin()
    part_g.start()
    ga_g.forward()
    q_tot = jnp.zeros((1, nc), F32)
    qn_tot = jnp.zeros((1, nc), F32)
    q2r = S["rs_keep"].at[1]
    for t0 in range(0, R, 256):
        at = pl.ds(t0, 256)
        q = q2r[at] * S["s2"][at]
        q2r[at] = q
        q_tot += jnp.sum(q, axis=0, keepdims=True)
        qn_tot += jnp.sum(q * S["n2"][at], axis=0, keepdims=True)
    fin = exchange(4, qn_tot, q_tot, nc)

    ga_g.near()
    ga_g.far()
    gb_g.near()
    gb_g.far()
    for c in a_rows:
        c.wait_recv()
    u = S["u"]
    u[...] = dot_nt(
        jnp.concatenate([S["ga"][k] for k in range(4)], axis=1),
        jnp.concatenate([S["sar"][k] for k in range(4)], axis=1),
    )
    u[...] += dot_nt(
        jnp.concatenate([S["gb"][k] for k in range(4)], axis=1),
        jnp.concatenate([S["sbr"][k] for k in range(4)], axis=1),
    )
    qn2, q2 = sums_finish(fin)
    ng = S["ng"]
    for t0 in range(0, R, 256):
        at = pl.ds(t0, 256)
        ng[ch, at] = grad_in(q2r[at], S["n2"][at], gain2, inv2, qn2, q2).astype(BF16)
    neck_g = Gather(lambda c: ng.at[c])
    neck_g.start()
    h_conv.step(0)

    def wide_part(side):
        return dot_nt(
            jnp.concatenate([ng[2 * side], ng[2 * side + 1]], axis=1),
            jnp.concatenate([S["cmat"][2 * side], S["cmat"][2 * side + 1]], axis=1),
        )

    neck_g.near()
    u[...] += wide_part(half)
    neck_g.forward()
    neck_g.far()
    u[...] += wide_part(other)
    q_tot = jnp.zeros((1, wc), F32)
    qn_tot = jnp.zeros((1, wc), F32)
    for t0 in range(0, R, 256):
        at = pl.ds(t0, 256)
        q = u[at] * S["s1"][at]
        u[at] = q
        q_tot += jnp.sum(q, axis=0, keepdims=True)
        qn_tot += jnp.sum(q * S["n1"][at], axis=0, keepdims=True)
    fin = exchange(5, qn_tot, q_tot, wc)

    h_conv.step(1)
    back = dot_nt(
        jnp.concatenate([ng[k] for k in range(4)], axis=1),
        jnp.concatenate([S["nin"][k, pl.ds(ch * nc, nc)] for k in range(4)], axis=1),
    )
    S["abg"][:, 0:nc] = S["ga"][ch]
    S["abg"][:, nc:] = (S["gb"][ch].astype(F32) + back).astype(BF16)
    h_ab = Halving("ab", 0, x_first)
    for k in range(4):
        put("ab", 0, k * (n // 4), dot_tn(wg[k], S["abg"][...]))
    part_g.forward()
    part_g.near()
    part_g.far()
    h_in = Halving("in", 0, x_first)
    for s in range(2):
        x = jnp.concatenate([pb[2 * s], pb[2 * s + 1]], axis=1)
        put("in", 0, s * (n // 2), dot_tn(x, ng[ch]))
    for stage in range(2, n_bits):
        h_conv.step(stage)

    qn1, q1 = sums_finish(fin)
    h_ab.start()
    h_in.start()
    gsh = S["gsh"]
    for tile in g.tiles:
        at = pl.ds(tile[0], tile[1])
        v = grad_in(u[at], S["n1"][at], gain1, inv1, qn1, q1)
        v = v.astype(BF16).astype(F32)
        gsh[0, at] = v.astype(BF16)
        gsh[1, at] = shift_tile(v, tile, 0, 1).astype(BF16)
        v = shift_tile(v, tile, 1, 0)
        gsh[2, at] = v.astype(BF16)
        gsh[3, at] = shift_tile(v, tile, 0, 1).astype(BF16)

    taps = [(tap, p, group_of(di, dj)) for p in PLANES for tap, di, dj in plane_taps(p)]
    h_down = {tap: Halving("down", tap, x_first) for tap, _, _ in taps}

    def down_tap(tap, p, k):
        for s in range(2):
            x = jnp.concatenate([xg[2 * s, p], xg[2 * s + 1, p]], axis=1)
            put("down", tap, s * (n // 2), dot_tn(x, gsh[k]))
        h_down[tap].start()

    cs, cr, cys, cyr, ckeep = S["cs"], S["cr"], S["cys"], S["cyr"], S["ckeep"]
    c_sib = {p: [remote(cs.at[p, k], cr.at[p, k], (dp, sib)) for k in range(2)] for p in PLANES}
    c_far = {p: remote(cys.at[p], cyr.at[p], (dp, yp)) for p in PLANES}

    def crop_pair(p, d0, d1):
        total = None
        for tap, di, dj in plane_taps(p):
            w = jnp.concatenate(
                [wv[tap, pl.ds(d0 * cb, cb), :], wv[tap, pl.ds(d1 * cb, cb), :]], axis=0
            )
            res = dot_nt(gsh[group_of(di, dj)], w)
            total = res if total is None else total + res
        return total

    def crop_start(p):
        part = crop_pair(p, diag, sib)
        cs[p, 0] = part[:, :cb].astype(BF16)
        c_sib[p][0].start()
        cs[p, 1] = part[:, cb:].astype(BF16)
        c_sib[p][1].start()
        part = crop_pair(p, yp, ch)
        ckeep[p, 0] = part[:, :cb]
        ckeep[p, 1] = part[:, cb:]

    def crop_send(p):
        c_sib[p][0].wait_recv()
        cys[p] = (ckeep[p, 0] + cr[p, 0].astype(F32)).astype(BF16)
        c_far[p].start()
        c_sib[p][1].wait_recv()
        ckeep[p, 1] += cr[p, 1].astype(F32)

    def crop_end(p):
        pr, pc = p // 2, p % 2
        c_far[p].wait_recv()
        v = ckeep[p, 1] + cyr[p].astype(F32)
        S["wide_big"][:, pr, pl.ds(pc, g.hb, stride=2), :] = v[:br].reshape(-1, g.hb, cb)
        S["wide_small"][:, pr, pl.ds(pc, g.hs, stride=2), :] = v[br:].reshape(-1, g.hs, cb)

    down_tap(*taps[0])
    down_tap(*taps[1])
    order = [PLANES[3], PLANES[1], PLANES[2], PLANES[0]]
    crop_start(order[0])
    down_tap(*taps[2])
    crop_send(order[0])
    crop_start(order[1])
    down_tap(*taps[3])
    crop_send(order[1])
    crop_start(order[2])
    down_tap(*taps[4])
    crop_send(order[2])
    crop_start(order[3])
    down_tap(*taps[5])
    crop_send(order[3])
    for k in range(6, 9):
        down_tap(*taps[k])

    for stage in range(n_bits):
        h_ab.step(stage)
        h_in.step(stage)
    events = []
    for i, (tap, _, _) in enumerate(taps):
        for stage in range(n_bits):
            events.append((3.0 + 2.7 * (i + 1) + 3.0 * stage, "d", tap, stage))
    for i, p in enumerate(order):
        events.append((3.0 + 4.2 * (i + 1), "c", p, 0))
    for _, kind, key, stage in sorted(events, key=lambda e: e[0]):
        if kind == "d":
            h_down[key].step(stage)
        else:
            crop_end(key)
            if key == order[-1]:
                outs.append(local(S["wide_big"], o_gbig))
                outs.append(local(S["wide_small"], o_gsmall))

    for c in ld_m:
        c.wait()

    def sq(value):
        v = value * value
        while v.ndim > 2:
            v = jnp.sum(v, axis=0)
        v = jnp.sum(v, axis=0, keepdims=True)
        out = v[:, 0:128]
        for k in range(128, v.shape[1], 128):
            out = out + v[:, k : k + 128]
        return out

    grads = {
        "down": S["g_down"][...],
        "a": S["g_ab"][0, :, 0:nc],
        "b": S["g_ab"][0, :, nc:],
        "in": S["g_in"][0],
    }
    g_conv = S["g_conv"]
    layers = ("down", "a", "b", "in", "conv")
    nm, nq = S["nm"], S["nq"]
    nm[dp] = jnp.zeros((16, 128), F32)
    for i, name in enumerate(layers):
        nm[dp, i : i + 1] = sq(S["k_" + name][...].astype(F32))
        nm[dp, 5 + i : 6 + i] = sq(g_conv[0]) if name == "conv" else sq(grads[name])
    ssem, rsem = sem(), sem()
    mine = nm.at[dp]
    for k in range(1, n):
        pltpu.make_async_remote_copy(
            src_ref=mine, dst_ref=mine, send_sem=ssem, recv_sem=rsem,
            device_id=(lax.rem(dp + k, n), ch), device_id_type=MESH,
        ).start()
    some = nm.at[pl.ds(0, n - 1)]
    pltpu.make_async_copy(some, some, rsem).wait()
    pltpu.make_async_copy(some, some, ssem).wait()
    nq[ch] = jnp.sum(nm[...], axis=0)
    last = [remote(nq.at[ch], nq.at[ch], (dp, d)) for d in (yp, diag, sib)]
    for c in last:
        c.start()
    for c in last:
        c.wait_recv()
    norms = jnp.sqrt(jnp.sum(jnp.sum(nq[...], axis=0), axis=1, keepdims=True))
    row = lax.broadcasted_iota(jnp.int32, (2, 5), 0)
    col = lax.broadcasted_iota(jnp.int32, (2, 5), 1)
    table = jnp.zeros((2, 5), F32)
    for k in range(10):
        table = jnp.where((row == k // 5) & (col == k % 5), norms[k : k + 1], table)
    o_ln[...] = table
    o_wn[0:1] = qn1
    o_wn[1:2] = q1
    o_nn[0, 0:1] = qn2
    o_nn[0, 1:2] = q2
    o_nn[1, 0:1] = qn3
    o_nn[1, 1:2] = q3

    def update(rate, weight, grad, moment):
        after = MOMENTUM * moment + rate * (grad + DECAY * weight)
        return weight - after, after

    for i, name in enumerate(layers):
        wnorm = norms[i : i + 1]
        rate = TRUST * wnorm / (norms[5 + i : 6 + i] + DECAY * wnorm)
        dst = S["o_" + name]
        if name == "down":
            for t in range(9):
                new, after = update(
                    rate, S["k_down"][t].astype(F32), S["g_down"][t], S["m_down"][t]
                )
                dst[0, t] = new
                dst[1, t] = after
        elif name == "conv":
            for t in range(9):
                new, after = update(
                    rate,
                    S["k_conv"][t].astype(F32),
                    g_conv[0, :, t * nc : (t + 1) * nc],
                    S["m_conv"][t],
                )
                dst[0, t] = new
                dst[1, t] = after
        else:
            new, after = update(rate, S["k_" + name][...].astype(F32), grads[name], S["m_" + name][...])
            dst[0] = new
            dst[1] = after
        targets = {
            "down": (o_ndown, o_mdown), "a": (o_na, o_ma), "b": (o_nb, o_mb),
            "in": (o_nin, o_min), "conv": (o_nconv, o_mconv),
        }[name]
        outs.append(local(dst.at[0], targets[0]))
        outs.append(local(dst.at[1], targets[1]))
    for c in outs:
        c.wait()
    for c in pending:
        c.wait_send()
    assert used[0] <= sems.shape[0], used[0]


def per_device(
    big_crops, small_crops, conv_down, split_a, split_b, neck_in, neck_conv, norm_wide, norm_neck,
    cot_big, cot_small, mom_down, mom_a, mom_b, mom_in, mom_conv,
):
    n = lax.axis_size("dp")
    g = Geometry(big_crops.shape, small_crops.shape, conv_down.shape, neck_conv.shape, n)

    def taps_first(w):
        return jnp.transpose(w, (1, 2, 0, 3)).reshape(9, w.shape[0], w.shape[3])

    def taps_back(w):
        return jnp.transpose(w.reshape(3, 3, w.shape[1], w.shape[2]), (2, 0, 1, 3))

    args = (
        big_crops.reshape(g.nb * g.hb * 2, 2 * g.hb, g.cb),
        small_crops.reshape(g.ns * g.hs * 2, 2 * g.hs, g.cb),
        taps_first(conv_down), split_a, split_b, neck_in, taps_first(neck_conv),
        norm_wide, norm_neck,
        cot_big.reshape(2, g.big_rows, g.nc), cot_small.reshape(2, g.small_rows, g.nc),
        taps_first(mom_down), mom_a, mom_b, mom_in, taps_first(mom_conv),
    )
    sds = jax.ShapeDtypeStruct
    up = [
        sds((9, g.ch // n, g.wc), F32), sds(mom_a.shape, F32), sds(mom_b.shape, F32),
        sds(mom_in.shape, F32), sds((9, g.ch // n, g.nc), F32),
    ]
    out_shape = [
        sds((2, g.big_rows, g.nc), BF16), sds((2, g.small_rows, g.nc), BF16),
        sds((g.nb * g.hb, 2, 2 * g.hb, g.cb), F32), sds((g.ns * g.hs, 2, 2 * g.hs, g.cb), F32),
        *up, *up,
        sds((2, g.wc), F32), sds((2, 2, g.nc), F32), sds((2, 5), F32),
    ]
    anywhere = pl.BlockSpec(memory_space=pl.ANY)
    vmem = pl.BlockSpec(memory_space=pltpu.VMEM)
    plan = scratch_plan(g)
    res = pl.pallas_call(
        functools.partial(mega, g, tuple(plan)),
        out_shape=out_shape,
        in_specs=[anywhere] * 16,
        out_specs=[anywhere] * 14 + [vmem] * 3,
        scratch_shapes=[pltpu.VMEM(shape, dtype) for shape, dtype in plan.values()]
        + [pltpu.SemaphoreType.DMA((N_SEMS,))],
        compiler_params=pltpu.CompilerParams(
            collective_id=0, has_side_effects=True, vmem_limit_bytes=60 * 2**20
        ),
    )(*args)
    res = list(res)
    res[0] = res[0].reshape(cot_big.shape)
    res[1] = res[1].reshape(cot_small.shape)
    res[2] = res[2].reshape(big_crops.shape)
    res[3] = res[3].reshape(small_crops.shape)
    for k in (4, 8, 9, 13):
        res[k] = taps_back(res[k])
    return tuple(res)


def solution(mesh):
    in_specs = (
        P("dp", None, None, "chan"),
        P("dp", None, None, "chan"),
        P(None, None, None, "chan"),
        P(None, "chan"),
        P(None, "chan"),
        P(None, "chan"),
        P(None, None, None, "chan"),
        P(),
        P(),
        P(None, "dp", None, None, "chan"),
        P(None, "dp", None, None, "chan"),
        P("dp", None, None, "chan"),
        P("dp", "chan"),
        P("dp", "chan"),
        P("dp", "chan"),
        P("dp", None, None, "chan"),
    )
    out_specs = (
        P(None, "dp", None, None, "chan"),
        P(None, "dp", None, None, "chan"),
        P("dp", None, None, "chan"),
        P("dp", None, None, "chan"),
        P("dp", None, None, "chan"),
        P("dp", "chan"),
        P("dp", "chan"),
        P("dp", "chan"),
        P("dp", None, None, "chan"),
        P("dp", None, None, "chan"),
        P("dp", "chan"),
        P("dp", "chan"),
        P("dp", "chan"),
        P("dp", None, None, "chan"),
        P(None, "chan"),
        P(None, None, "chan"),
        P(),
    )
    return jax.shard_map(
        per_device, mesh=mesh, in_specs=in_specs, out_specs=out_specs, check_vma=False
    )
```

```python
import functools

import jax
import jax.numpy as jnp
from jax import lax
from jax.experimental import pallas as pl
from jax.experimental.pallas import tpu as pltpu
from jax.sharding import PartitionSpec as P

EPSILON = 1e-05
MOMENTUM = 0.9
DECAY = 0.0005
TRUST = 0.1
F32 = jnp.float32
BF16 = jnp.bfloat16
MESH = pl.DeviceIdType.MESH
PLANES = (3, 1, 2, 0)


def dot_nn(left, right):
    return lax.dot_general(left, right, (((1,), (0,)), ((), ())), preferred_element_type=F32)


def dot_nt(left, right):
    return lax.dot_general(left, right, (((1,), (1,)), ((), ())), preferred_element_type=F32)


def dot_tn(left, right):
    return lax.dot_general(left, right, (((0,), (0,)), ((), ())), preferred_element_type=F32)


def mish_parts(v):
    u = jnp.exp(-jnp.abs(v))
    pos = v >= 0
    num = jnp.where(pos, 1.0 + 2.0 * u, u * (u + 2.0))
    rest = jnp.where(pos, 2.0 * u * u, 2.0)
    den = num + rest
    inv = 1.0 / den
    tangent = num * inv
    slope = tangent + v * (rest * (den + num) * inv * inv) * (jnp.where(pos, 1.0, u) / (1.0 + u))
    return v * tangent, slope


def plane_taps(p):
    rows = ((0, -1), (2, 0)) if p // 2 else ((1, 0),)
    cols = ((0, -1), (2, 0)) if p % 2 else ((1, 0),)
    return [(r * 3 + s, di, dj) for r, di in rows for s, dj in cols]


def group_of(di, dj):
    return (2 if di else 0) + (1 if dj else 0)


class Geometry:
    def __init__(self, big, small, down, neck, n_dp):
        self.nb, self.hb = big[0], big[1] // 2
        self.ns, self.hs = small[0], small[1] // 2
        self.cb = big[3]
        self.ch = down[0]
        self.wc = down[3]
        self.nc = neck[3]
        self.n = n_dp
        self.big_rows = self.nb * self.hb * self.hb
        self.small_rows = self.ns * self.hs * self.hs
        self.rows = self.big_rows + self.small_rows
        self.total_rows = self.rows * n_dp
        self.tiles = [
            (i * self.hb * self.hb, self.hb * self.hb, 1, self.hb) for i in range(self.nb)
        ] + [(self.big_rows, self.small_rows, self.ns, self.hs)]


def shift_tile(value, tile, di, dj):
    _, rows, images, side = tile
    cols = value.shape[-1]
    if di:
        v = value.reshape(images, side, side, cols)
        blank = jnp.zeros((images, 1, side, cols), value.dtype)
        if di < 0:
            v = jnp.concatenate([blank, v[:, :-1]], axis=1)
        else:
            v = jnp.concatenate([v[:, 1:], blank], axis=1)
        value = v.reshape(rows, cols)
    if dj:
        v = pltpu.roll(value, 1 if dj < 0 else rows - 1, 0).reshape(rows // side, side, cols)
        at = lax.broadcasted_iota(jnp.int32, (1, side, cols), 1)
        keep = at >= 1 if dj < 0 else at < side - 1
        value = jnp.where(keep, v, 0.0).reshape(rows, cols)
    return value


def bits_of(n):
    return n.bit_length() - 1


def halving_plan(n, order):
    left = list(range(bits_of(n)))
    plan = []
    for bit in order:
        at = left.index(bit)
        plan.append((bit, 1 << (len(left) - 1 - at), 1 << at))
        left.remove(bit)
    return plan


def halving_orders(n):
    bits = tuple(range(bits_of(n)))
    return bits, bits[1:] + bits[:1]


Z_TAPS = 1


def scratch_plan(g):
    n = g.n
    R = g.rows
    s = {}
    s["raw_big"] = ((g.nb * g.hb * 2, 2 * g.hb, g.cb), BF16)
    s["raw_small"] = ((g.ns * g.hs * 2, 2 * g.hs, g.cb), BF16)
    s["xg"] = ((4, 4, R, g.cb), BF16)
    s["wv"] = ((9, g.ch, g.wc), BF16)
    s["wn"] = ((g.ch, 9 * g.nc), BF16)
    s["ab"] = ((2 * g.ch, 2 * g.nc), BF16)
    s["nin"] = ((4, g.ch, g.nc), BF16)
    s["sar"] = ((4, g.wc, g.nc), BF16)
    s["sbr"] = ((4, g.wc, g.nc), BF16)
    s["cmat"] = ((4, g.wc, g.nc), BF16)
    s["pw"] = ((2, 4 * g.wc), F32)
    s["pn"] = ((2, 2, 4 * g.nc), F32)
    s["acc"] = ((4, R, g.wc), F32)
    s["n1"] = ((R, g.wc), F32)
    s["s1"] = ((R, g.wc), F32)
    s["wg"] = ((4, R, g.wc), BF16)
    for k in ("f", "b"):
        s["rs_send" + k] = ((2, R, g.nc), BF16)
        s["rs_recv" + k] = ((2, R, g.nc), BF16)
        s["rs_ys" + k] = ((R, g.nc), BF16)
        s["rs_yr" + k] = ((R, g.nc), BF16)
    s["rs_keep"] = ((2, R, g.nc), F32)
    s["n2"] = ((R, g.nc), F32)
    s["s2"] = ((R, g.nc), F32)
    s["fg"] = ((4, R, g.nc), BF16)
    s["yb"] = ((R, 9 * g.nc), F32)
    s["n3"] = ((R, g.nc), F32)
    s["s3"] = ((R, g.nc), F32)
    s["cg"] = ((R, 9 * g.nc), BF16)
    s["ga"] = ((4, R, g.nc), BF16)
    s["gb"] = ((4, R, g.nc), BF16)
    s["pb"] = ((R, g.nc), BF16)
    s["ng"] = ((4, R, g.nc), BF16)
    s["u"] = ((R, g.wc), F32)
    s["gsh"] = ((4, R, g.wc), BF16)
    s["cs"] = ((4, 2, R, g.cb), BF16)
    s["cr"] = ((4, 2, R, g.cb), BF16)
    s["cys"] = ((4, R, g.cb), BF16)
    s["cyr"] = ((4, R, g.cb), BF16)
    s["st"] = ((6, n, 2, g.wc), F32)
    s["nm"] = ((4 * n, 1, 128), F32)
    near, far = halving_orders(n)
    rc = {
        "dx": (9 - Z_TAPS, g.ch // n, g.wc, near),
        "dz": (Z_TAPS, g.ch // n, g.wc, far),
        "c0": (1, g.ch // n, 3 * g.nc, near),
        "c1": (1, g.ch // n, 3 * g.nc, near),
        "c2": (1, g.ch // n, 3 * g.nc, near),
        "a": (1, 2 * g.ch // n, g.nc, far),
        "b": (1, 2 * g.ch // n, g.nc, near),
        "in": (1, g.ch // n, g.nc, near),
    }
    for name, (count, rows, cols, order) in rc.items():
        for stage, (_, high, low) in enumerate(halving_plan(n, order)):
            s[f"h_{name}_s{stage}"] = ((count, high, 2, low, rows, cols), BF16)
            s[f"h_{name}_r{stage}"] = ((count, high, low, rows, cols), BF16)
    s["g_down"] = ((9, g.ch // n, g.wc), F32)
    s["g_conv"] = ((g.ch // n, 9 * g.nc), F32)
    s["p_a"] = ((2 * g.ch // n, g.nc), F32)
    s["p_b"] = ((2 * g.ch // n, g.nc), F32)
    s["p_in"] = ((g.ch // n, g.nc), F32)
    s["g_a"] = ((2 * g.ch // n, g.nc), F32)
    s["g_b"] = ((2 * g.ch // n, g.nc), F32)
    s["g_in"] = ((g.ch // n, g.nc), F32)
    s["m_down"] = ((9, g.ch // n, g.wc), F32)
    s["m_a"] = ((2 * g.ch // n, g.nc), F32)
    s["m_b"] = ((2 * g.ch // n, g.nc), F32)
    s["m_in"] = ((g.ch // n, g.nc), F32)
    s["m_conv"] = ((9, g.ch // n, g.nc), F32)
    s["k_down"] = ((9, g.ch // n, g.wc), BF16)
    s["k_a"] = ((2 * g.ch // n, g.nc), BF16)
    s["k_b"] = ((2 * g.ch // n, g.nc), BF16)
    s["k_in"] = ((g.ch // n, g.nc), BF16)
    s["k_conv"] = ((9, g.ch // n, g.nc), BF16)
    return s


def count_sems(n):
    return 99 + 16 * bits_of(n)


def mega(g, names, *refs):
    (
        big, small, w_down, w_a, w_b, w_in, w_conv, p_wide, p_neck, c_big, c_small,
        m_down, m_a, m_b, m_in, m_conv,
    ) = refs[:16]
    (
        o_big, o_small, o_gbig, o_gsmall, o_ndown, o_na, o_nb, o_nin, o_nconv,
        o_mdown, o_ma, o_mb, o_min, o_mconv, o_wn, o_nn, o_ln,
    ) = refs[16:33]
    S = dict(zip(names, refs[33:-1], strict=True))
    sems = refs[-1]
    n, R, nc, wc, cb = g.n, g.rows, g.nc, g.wc, g.cb
    dp = lax.axis_index("dp")
    ch = lax.axis_index("chan")
    core = lax.rem(ch, 2)
    half = lax.div(ch, 2)
    sib = half * 2 + (1 - core)
    yp = (1 - half) * 2 + core
    diag = (1 - half) * 2 + (1 - core)
    other = 1 - half

    used = [0]
    pending = []
    drain = []

    def sem():
        used[0] += 1
        return sems.at[used[0] - 1]

    load_sems = []

    def local(src, dst, own=None):
        if own is None:
            own = sem()
            load_sems.append(own)
        copy = pltpu.make_async_copy(src, dst, own)
        copy.start()
        return copy

    def remote(src, dst, device, ssem=None, rsem=None):
        copy = pltpu.make_async_remote_copy(
            src_ref=src, dst_ref=dst,
            send_sem=sem() if ssem is None else ssem,
            recv_sem=sem() if rsem is None else rsem,
            device_id=device, device_id_type=MESH,
        )
        if ssem is None:
            pending.append(copy)
        return copy

    def total(view, one):
        return pltpu.make_async_copy(view, view, one)

    def shared(view):
        one = sem()
        drain.append(total(view, one))
        return one
    ld_big = local(big, S["raw_big"])
    ld_small = local(small, S["raw_small"])
    ld_wv = local(w_down, S["wv"])
    ab_sem, wn_sem, ga_sem, gb_sem = sem(), sem(), sem(), sem()
    local(w_a, S["ab"].at[:, pl.ds(0, nc)], ab_sem)
    local(w_b, S["ab"].at[:, pl.ds(nc, nc)], ab_sem)
    ld_ab = total(S["ab"], ab_sem)
    ld_in = local(w_in, S["nin"].at[ch])
    ld_p = [local(p_wide, S["pw"]), local(p_neck, S["pn"])]
    for t in range(9):
        local(w_conv.at[t], S["wn"].at[:, pl.ds(t * nc, nc)], wn_sem)
    ld_wn = total(S["wn"], wn_sem)
    br, sr = g.big_rows, g.small_rows
    ld_c = []
    for k, name, one in ((0, "ga", ga_sem), (1, "gb", gb_sem)):
        local(c_big.at[k], S[name].at[ch, pl.ds(0, br)], one)
        local(c_small.at[k], S[name].at[ch, pl.ds(br, sr)], one)
        ld_c.append(total(S[name].at[ch], one))
    bar = pltpu.get_barrier_semaphore()

    def everyone(act):
        def one(k):
            act((lax.rem(dp + lax.div(k, 4), n), lax.rem(ch + lax.rem(k, 4), 4)))

        if n <= 8:
            for k in range(1, 4 * n):
                one(k)
        else:
            lax.fori_loop(1, 4 * n, lambda k, c: (one(k), c)[1], 0)

    peers = [(dp, yp), (dp, sib), (dp, diag)]
    peers += [(lax.rem(dp + k, n), ch) for k in range(1, n)]
    for peer in peers:
        pl.semaphore_signal(bar, inc=1, device_id=peer, device_id_type=MESH)
    xg = S["xg"]
    ld_big.wait()
    o_gbig[...] = S["raw_big"][...].astype(F32).reshape(o_gbig.shape)
    ld_small.wait()
    o_gsmall[...] = S["raw_small"][...].astype(F32).reshape(o_gsmall.shape)

    def split_plane(p):
        pr, pc = p // 2, p % 2
        xg[ch, p, 0:br] = (
            o_gbig[:, pr, pl.ds(pc, g.hb, stride=2), :].reshape(br, cb).astype(BF16)
        )
        xg[ch, p, br:R] = (
            o_gsmall[:, pr, pl.ds(pc, g.hs, stride=2), :].reshape(sr, cb).astype(BF16)
        )

    class Gather:
        def __init__(self, ref, plane=None, ssems=None):
            def block(c):
                return ref.at[c] if plane is None else ref.at[c, plane]

            if ssems is None:
                ssems = [shared(ref.at[pl.ds(0, 3)])] * 3
            self.to_sib = remote(block(ch), block(ch), (dp, sib), ssems[0])
            self.to_far = remote(block(ch), block(ch), (dp, yp), ssems[1])
            self.onward = remote(block(yp), block(yp), (dp, sib), ssems[2])

        def start(self):
            self.to_sib.start()
            self.to_far.start()

        def forward(self):
            self.to_far.wait_recv()
            self.onward.start()

        def near(self):
            self.to_sib.wait_recv()

        def far(self):
            self.onward.wait_recv()

    crop_sems = [shared(xg.at[0]) for _ in range(3)]
    crops = {p: Gather(xg, p, crop_sems) for p in PLANES}
    split_plane(PLANES[0])
    pl.semaphore_wait(bar, len(peers))
    crops[PLANES[0]].start()
    for p in PLANES[1:]:
        split_plane(p)
        crops[p].start()
    ld_in.wait()
    neck_in = Gather(S["nin"])
    ld_ab.wait()

    class Rows:
        def __init__(self, buf, lane):
            ref = S[buf]
            ssem, rsem = shared(ref.at[pl.ds(0, 3)]), sem()
            self.copies = [
                remote(
                    S["ab"].at[pl.ds(dev * wc, wc), pl.ds(lane, nc)], ref.at[ch], (dp, dev),
                    ssem, rsem,
                )
                for dev in (yp, diag, sib)
            ]
            self.arrived = total(ref.at[pl.ds(0, 3)], rsem)
            ref[ch] = S["ab"][pl.ds(ch * wc, wc), lane : lane + nc]

        def start(self):
            for c in self.copies:
                c.start()

        def wait(self):
            self.arrived.wait()

    b_rows = Rows("sbr", nc)
    a_rows = Rows("sar", 0)
    b_rows.start()
    neck_in.start()
    ld_wv.wait()
    wv, acc = S["wv"], S["acc"]

    def conv_part(side, p, first):
        x = jnp.concatenate([xg[2 * side, p], xg[2 * side + 1, p]], axis=1)
        for tap, di, dj in plane_taps(p):
            res = dot_nn(x, wv[tap, pl.ds(side * 2 * cb, 2 * cb), :])
            k = group_of(di, dj)
            if first:
                acc[k] = res
            else:
                acc[k] += res
    for p in PLANES:
        crops[p].near()
        conv_part(half, p, p == PLANES[0])
    for p in PLANES[:-1]:
        crops[p].forward()
        crops[p].far()
        conv_part(other, p, False)
    for tile in g.tiles:
        at = pl.ds(tile[0], tile[1])
        inner = acc[1, at] + shift_tile(acc[3, at], tile, -1, 0)
        acc[2, at] = shift_tile(acc[2, at], tile, -1, 0) + shift_tile(inner, tile, 0, -1)
    p = PLANES[-1]
    crops[p].forward()
    crops[p].far()
    conv_part(other, p, False)
    acc[0] = acc[0] + acc[2]

    st = S["st"]
    st_send, st_recv = sem(), [sem(), sem()]

    def exchange(phase, first, second, cols):
        st[phase, dp, 0:1, 0:cols] = first
        st[phase, dp, 1:2, 0:cols] = second
        ssem, rsem = st_send, st_recv[phase % 2]
        mine = st.at[phase, dp, :, pl.ds(0, cols)]
        for k in range(1, n):
            pltpu.make_async_remote_copy(
                src_ref=mine, dst_ref=mine, send_sem=ssem, recv_sem=rsem,
                device_id=(lax.rem(dp + k, n), ch), device_id_type=MESH,
            ).start()
        some = st.at[phase, pl.ds(0, n - 1), :, pl.ds(0, cols)]

        def finish():
            total(some, rsem).wait()
            total(some, ssem).wait()
            return st[phase, :, :, 0:cols]

        return finish

    def norm_start(phase, ref):
        cols = ref.shape[-1]
        mean = jnp.sum(ref[...], axis=0, keepdims=True) * (1.0 / R)
        dev = ref[...] - mean
        return exchange(phase, mean, jnp.sum(dev * dev, axis=0, keepdims=True), cols)

    def norm_finish(finish):
        v = finish()
        tot = jnp.sum(v, axis=0)
        mean = tot[0:1] * (1.0 / n)
        off = v - mean[None]
        spread = jnp.sum(off * off, axis=0)[0:1]
        var = (tot[1:2] + R * spread) * (1.0 / g.total_rows)
        return mean, lax.rsqrt(var + EPSILON)

    def sums_finish(finish):
        tot = jnp.sum(finish(), axis=0)
        return tot[0:1], tot[1:2]
    fin = norm_start(0, acc.at[0])
    for c in ld_p:
        c.wait()
    gain1 = S["pw"][0:1, pl.ds(ch * wc, wc)]
    bias1 = S["pw"][1:2, pl.ds(ch * wc, wc)]
    neck_in.forward()
    neck_in.near()
    neck_in.far()
    b_rows.wait()
    rows_b = jnp.concatenate([S["sbr"][k] for k in range(4)], axis=1)
    for k in range(4):
        S["cmat"][k] = dot_nn(rows_b, S["nin"][k]).astype(BF16)
    mean1, inv1 = norm_finish(fin)
    wg = S["wg"]
    for t0 in range(0, R, 256):
        at = pl.ds(t0, 256)
        normed = (acc[0, at] - mean1) * inv1
        S["n1"][at] = normed
        act, slope = mish_parts(normed * gain1 + bias1)
        wg[ch, at] = act.astype(BF16)
        S["s1"][at] = slope

    def reduce_chan(k, pair):
        send, recv = S["rs_send" + k], S["rs_recv" + k]
        ys, yr, keep = S["rs_ys" + k], S["rs_yr" + k], S["rs_keep"]
        parts = [pl.ds(0, R // 2), pl.ds(R // 2, R // 2)]
        s0, sy, r1 = shared(send), shared(ys), sem()
        c0 = [remote(send.at[0, at], recv.at[0, at], (dp, sib), s0) for at in parts]
        c1 = [remote(send.at[1, at], recv.at[1, at], (dp, sib), s0, r1) for at in parts]
        cy = [remote(ys.at[at], yr.at[at], (dp, yp), sy) for at in parts]
        for at, far, near in zip(parts, c0, c1, strict=True):
            part = pair(at, diag, sib).astype(BF16)
            send[0, at] = part[:, :nc]
            far.start()
            send[1, at] = part[:, nc:]
            near.start()
        for at, near, far in zip(parts, c0, cy, strict=True):
            part = pair(at, yp, ch)
            keep[1, at] = part[:, nc:]
            near.wait_recv()
            ys[at] = (part[:, :nc] + recv[0, at].astype(F32)).astype(BF16)
            far.start()
        total(recv.at[1], r1).wait()
        keep[1] += recv[1].astype(F32)

        def finish():
            for at, far in zip(parts, cy, strict=True):
                far.wait_recv()
                keep[1, at] += yr[at].astype(F32)

        return finish

    def neck_pair(at, d0, d1):
        return dot_nn(
            wg[ch, at], jnp.concatenate([S["cmat"][d0], S["cmat"][d1]], axis=1)
        )
    rs_fin = reduce_chan("f", neck_pair)
    for c in ld_c:
        c.wait()
    gb_g = Gather(S["gb"])
    ga_g = Gather(S["ga"])
    wide_g = Gather(wg)
    rs_fin()
    a_rows.start()
    z2 = S["rs_keep"].at[1]
    fin = norm_start(1, z2)
    gain2 = S["pn"][0, 0:1, pl.ds(ch * nc, nc)]
    bias2 = S["pn"][0, 1:2, pl.ds(ch * nc, nc)]
    gain3 = S["pn"][1, 0:1, pl.ds(ch * nc, nc)]
    bias3 = S["pn"][1, 1:2, pl.ds(ch * nc, nc)]
    mean2, inv2 = norm_finish(fin)
    fg = S["fg"]
    for t0 in range(0, R, 256):
        at = pl.ds(t0, 256)
        normed = (z2[at] - mean2) * inv2
        S["n2"][at] = normed
        act, slope = mish_parts(normed * gain2 + bias2)
        fg[ch, at] = act.astype(BF16)
        S["s2"][at] = slope
    first_g = Gather(fg)
    first_g.start()
    ld_wn.wait()
    wn, yb = S["wn"], S["yb"]

    def neck_part(side, first):
        x = jnp.concatenate([fg[2 * side], fg[2 * side + 1]], axis=1)
        w = wn[pl.ds(side * 2 * nc, 2 * nc), :]
        if first:
            yb[...] = dot_nn(x, w)
        else:
            yb[...] += dot_nn(x, w)

    first_g.near()
    neck_part(half, True)
    first_g.forward()
    first_g.far()
    gb_g.start()
    ga_g.start()
    neck_part(other, False)
    z3 = S["n3"]
    for tile in g.tiles:
        at = pl.ds(tile[0], tile[1])
        cols = []
        for s in range(3):
            cols.append(
                yb[at, (3 + s) * nc : (4 + s) * nc]
                + shift_tile(yb[at, s * nc : (s + 1) * nc], tile, -1, 0)
                + shift_tile(yb[at, (6 + s) * nc : (7 + s) * nc], tile, 1, 0)
            )
        z3[at] = (
            cols[1] + shift_tile(cols[0], tile, 0, -1) + shift_tile(cols[2], tile, 0, 1)
        )
    fin = norm_start(2, z3)
    mean3, inv3 = norm_finish(fin)
    q_tot = jnp.zeros((1, nc), F32)
    qn_tot = jnp.zeros((1, nc), F32)
    for t0 in range(0, R, 256):
        at = pl.ds(t0, 256)
        normed = (z3[at] - mean3) * inv3
        act, slope = mish_parts(normed * gain3 + bias3)
        q = S["gb"][ch, at].astype(F32) * slope
        z3[at] = normed
        S["s3"][at] = q
        S["yb"][at, 0:nc] = act
        q_tot += jnp.sum(q, axis=0, keepdims=True)
        qn_tot += jnp.sum(q * normed, axis=0, keepdims=True)
    fin = exchange(3, qn_tot, q_tot, nc)

    def grad_in(q, normed, gain, inv, qn_sum, q_sum):
        return gain * inv * (
            q - q_sum * (1.0 / g.total_rows) - normed * (qn_sum * (1.0 / g.total_rows))
        )

    stage_sems = {}

    class Halving:
        def __init__(self, name, item, order, result):
            self.name, self.item, self.result = name, item, result
            self.plan = halving_plan(n, order)
            self.copies = []
            self.alone = S[f"h_{name}_s0"].shape[0] == 1
            if name not in stage_sems:
                stages = range(len(self.plan))
                stage_sems[name] = (
                    [sem()] * len(self.plan)
                    if self.alone
                    else [shared(S[f"h_{name}_s{i}"].at[:, :, 0]) for i in stages]
                )
            for i, (bit, high, low) in enumerate(self.plan):
                own = lax.rem(lax.div(dp, 1 << bit), 2)
                peer = dp + (1 - 2 * own) * (1 << bit)
                send = S[f"h_{name}_s{i}"]
                recv = S[f"h_{name}_r{i}"]
                self.copies.append(
                    remote(
                        send.at[item, :, 1 - own], recv.at[item], (peer, ch), stage_sems[name][i]
                    )
                )

        def start(self, stage=0):
            self.copies[stage].start()

        def step(self, stage):
            bit, high, low = self.plan[stage]
            own = lax.rem(lax.div(dp, 1 << bit), 2)
            send = S[f"h_{self.name}_s{stage}"]
            recv = S[f"h_{self.name}_r{stage}"]
            self.copies[stage].wait_recv()
            if self.alone:
                self.copies[stage].wait_send()
            both = send[self.item, :, own].astype(F32) + recv[self.item].astype(F32)
            if stage + 1 < len(self.plan):
                after = S[f"h_{self.name}_s{stage + 1}"]
                after[self.item] = both.astype(BF16).reshape(after.shape[1:])
                self.start(stage + 1)
            else:
                self.result[...] = both[0, 0]

    n_bits = bits_of(n)
    x_first, z_first = halving_orders(n)

    def put_rows(name, value):
        ref = S[f"h_{name}_s0"]
        _, high, _, low, rows, cols = ref.shape
        value = value.astype(BF16)
        for e in range(n):
            r, c = e % (n // 4), e // (n // 4)
            ref[0, e // (2 * low), e // low % 2, e % low] = value[
                r * rows : (r + 1) * rows, c * cols : (c + 1) * cols
            ]

    quarter = n // 4
    at_home = lax.div(dp, quarter) == ch

    class Deliver:
        def __init__(self, name):
            self.src, self.dst = S[f"p_{name}"], S[f"g_{name}"]
            target = (ch * quarter + lax.rem(dp, quarter), lax.div(dp, quarter))
            self.copy = pltpu.make_async_remote_copy(
                src_ref=self.src, dst_ref=self.dst, send_sem=sem(), recv_sem=sem(),
                device_id=target, device_id_type=MESH,
            )

        def start(self):
            @pl.when(at_home)
            def _():
                self.dst[...] = self.src[...]

            @pl.when(jnp.logical_not(at_home))
            def _():
                self.copy.start()

        def finish(self):
            @pl.when(jnp.logical_not(at_home))
            def _():
                self.copy.wait_recv()
                self.copy.wait_send()

    def put(name, item, first_block, value):
        ref = S[f"h_{name}_s0"]
        _, high, _, low, rows, cols = ref.shape
        at = first_block // (2 * low)
        count = value.shape[0] // (rows * 2 * low)
        ref[item, at : at + count] = value.astype(BF16).reshape(count, 2, low, rows, cols)
    gb_g.forward()
    gb_g.near()
    gb_g.far()
    u = S["u"]
    u[...] = dot_nt(
        jnp.concatenate([S["gb"][k] for k in range(4)], axis=1),
        jnp.concatenate([S["sbr"][k] for k in range(4)], axis=1),
    )
    qn3, q3 = sums_finish(fin)
    cg = S["cg"]
    for tile in g.tiles:
        at = pl.ds(tile[0], tile[1])
        v = grad_in(S["s3"][at], z3[at], gain3, inv3, qn3, q3)
        v = v.astype(BF16).astype(F32)
        for r in range(3):
            vi = shift_tile(v, tile, 1 - r, 0)
            for s in range(3):
                t = r * 3 + s
                cg[at, t * nc : (t + 1) * nc] = shift_tile(vi, tile, 0, 1 - s).astype(BF16)

    rows = g.ch // n
    reuse = [*load_sems, ab_sem, wn_sem, ga_sem, gb_sem]
    ld_m = [
        local(src, S[name], one)
        for (src, name), one in zip(
            (
                (m_down, "m_down"), (m_a, "m_a"), (m_b, "m_b"), (m_in, "m_in"),
                (m_conv, "m_conv"),
                (w_down.at[:, pl.ds(dp * rows, rows)], "k_down"),
                (w_a.at[pl.ds(dp * 2 * rows, 2 * rows)], "k_a"),
                (w_b.at[pl.ds(dp * 2 * rows, 2 * rows)], "k_b"),
                (w_in.at[pl.ds(dp * rows, rows)], "k_in"),
                (w_conv.at[:, pl.ds(dp * rows, rows)], "k_conv"),
            ),
            reuse,
            strict=True,
        )
    ]

    def back_pair(at, d0, d1):
        w = jnp.concatenate([wn[pl.ds(d0 * nc, nc), :], wn[pl.ds(d1 * nc, nc), :]], axis=0)
        return dot_nt(cg[at], w)
    rs_fin = reduce_chan("b", back_pair)
    h_conv = [
        Halving(f"c{k}", 0, x_first, S["g_conv"].at[:, pl.ds(3 * k * nc, 3 * nc)])
        for k in range(3)
    ]
    for k in range(3):
        for s in range(2):
            x = jnp.concatenate([fg[2 * s], fg[2 * s + 1]], axis=1)
            put(f"c{k}", 0, s * (n // 2), dot_tn(x, cg[:, 3 * k * nc : 3 * (k + 1) * nc]))
        if k == 0:
            h_conv[k].start()
    ga_g.forward()
    ga_g.near()
    ga_g.far()
    a_rows.wait()
    u[...] += dot_nt(
        jnp.concatenate([S["ga"][k] for k in range(4)], axis=1),
        jnp.concatenate([S["sar"][k] for k in range(4)], axis=1),
    )
    h_a = Halving("a", 0, z_first, S["p_a"])
    put_rows("a", dot_tn(wg[ch], jnp.concatenate([S["ga"][k] for k in range(4)], axis=1)))
    rs_fin()
    q_tot = jnp.zeros((1, nc), F32)
    qn_tot = jnp.zeros((1, nc), F32)
    q2r = S["rs_keep"].at[1]
    for t0 in range(0, R, 256):
        at = pl.ds(t0, 256)
        q = q2r[at] * S["s2"][at]
        q2r[at] = q
        q_tot += jnp.sum(q, axis=0, keepdims=True)
        qn_tot += jnp.sum(q * S["n2"][at], axis=0, keepdims=True)
    fin = exchange(4, qn_tot, q_tot, nc)
    h_conv[1].start()
    h_conv[0].step(0)
    h_a.start()
    h_conv[2].start()
    qn2, q2 = sums_finish(fin)
    ng = S["ng"]
    for t0 in range(0, R, 256):
        at = pl.ds(t0, 256)
        ng[ch, at] = grad_in(q2r[at], S["n2"][at], gain2, inv2, qn2, q2).astype(BF16)
    neck_g = Gather(ng)
    neck_g.start()
    def wide_part(side):
        return dot_nt(
            jnp.concatenate([ng[2 * side], ng[2 * side + 1]], axis=1),
            jnp.concatenate([S["cmat"][2 * side], S["cmat"][2 * side + 1]], axis=1),
        )
    neck_g.near()
    u[...] += wide_part(half)
    h_a.step(0)
    h_conv[1].step(0)
    neck_g.forward()
    neck_g.far()
    wide_g.start()
    u[...] += wide_part(other)
    q_tot = jnp.zeros((1, wc), F32)
    qn_tot = jnp.zeros((1, wc), F32)
    for t0 in range(0, R, 256):
        at = pl.ds(t0, 256)
        q = u[at] * S["s1"][at]
        u[at] = q
        q_tot += jnp.sum(q, axis=0, keepdims=True)
        qn_tot += jnp.sum(q * S["n1"][at], axis=0, keepdims=True)
    fin = exchange(5, qn_tot, q_tot, wc)

    ng_whole = jnp.concatenate([ng[k] for k in range(4)], axis=1)
    h_b = Halving("b", 0, x_first, S["p_b"])
    cols = []
    for k in range(4):
        back = dot_nt(
            ng_whole,
            jnp.concatenate([S["nin"][c, k * nc : (k + 1) * nc] for c in range(4)], axis=1),
        )
        cols.append((S["gb"][k].astype(F32) + back).astype(BF16))
    put_rows("b", dot_tn(wg[ch], jnp.concatenate(cols, axis=1)))
    h_conv[2].step(0)
    h_b.start()
    h_conv[0].step(1)
    h_a.step(1)
    h_conv[1].step(1)
    h_in = Halving("in", 0, x_first, S["p_in"])
    qn1, q1 = sums_finish(fin)
    gsh = S["gsh"]
    for tile in g.tiles:
        at = pl.ds(tile[0], tile[1])
        v = grad_in(u[at], S["n1"][at], gain1, inv1, qn1, q1)
        v = v.astype(BF16).astype(F32)
        gsh[0, at] = v.astype(BF16)
        gsh[1, at] = shift_tile(v, tile, 0, 1).astype(BF16)
        v = shift_tile(v, tile, 1, 0)
        gsh[2, at] = v.astype(BF16)
        gsh[3, at] = shift_tile(v, tile, 0, 1).astype(BF16)

    where = {tap: (tap, p, k) for tap, p, k in
             ((t, p, group_of(di, dj)) for p in PLANES for t, di, dj in plane_taps(p))}

    def split_job():
        pb = S["pb"]
        split = dot_nn(
            jnp.concatenate([wg[k] for k in range(4)], axis=1), S["ab"][...]
        )
        o_big[0] = split[:br, :nc].astype(BF16)
        o_small[0] = split[br:, :nc].astype(BF16)
        part = split[:, nc:].astype(BF16)
        pb[...] = part
        block = (part.astype(F32) + yb[:, 0:nc]).astype(BF16)
        o_big[1] = block[:br]
        o_small[1] = block[br:]

    def in_job():
        put_rows("in", dot_tn(S["pb"][...], jnp.concatenate([ng[k] for k in range(4)], axis=1)))
        h_in.start()

    taps = [(tap, p, group_of(di, dj)) for p in PLANES for tap, di, dj in plane_taps(p)]
    h_down = {}
    for i, (tap, _, _) in enumerate(taps):
        result = S["g_down"].at[tap]
        if 1 <= i <= Z_TAPS:
            h_down[tap] = Halving("dz", i - 1, z_first, result)
        else:
            h_down[tap] = Halving("dx", i if i < 1 else i - Z_TAPS, x_first, result)

    def down_tap(tap, p, k):
        h = h_down[tap]
        for s in range(2):
            x = jnp.concatenate([xg[2 * s, p], xg[2 * s + 1, p]], axis=1)
            put(h.name, h.item, s * (n // 2), dot_tn(x, gsh[k]))
        h.start()

    cs, cr, cys, cyr = S["cs"], S["cr"], S["cys"], S["cyr"]
    cs_sem, cys_sem = shared(cs), shared(cys)
    c_sib = {
        p: [remote(cs.at[p, k], cr.at[p, k], (dp, sib), cs_sem) for k in range(2)] for p in PLANES
    }
    c_far = {p: remote(cys.at[p], cyr.at[p], (dp, yp), cys_sem) for p in PLANES}

    def crop_pair(p, d0, d1):
        part = None
        for tap, di, dj in plane_taps(p):
            w = jnp.concatenate(
                [wv[tap, pl.ds(d0 * cb, cb), :], wv[tap, pl.ds(d1 * cb, cb), :]], axis=0
            )
            res = dot_nt(gsh[group_of(di, dj)], w)
            part = res if part is None else part + res
        return part

    def crop_near(p):
        part = crop_pair(p, diag, sib).astype(BF16)
        cs[p, 0] = part[:, :cb]
        c_sib[p][0].start()
        cs[p, 1] = part[:, cb:]
        c_sib[p][1].start()

    def crop_own(p):
        acc[p] = crop_pair(p, yp, ch)

    def crop_send(p):
        c_sib[p][0].wait_recv()
        cys[p] = (acc[p, :, :cb] + cr[p, 0].astype(F32)).astype(BF16)
        c_far[p].start()
        c_sib[p][1].wait_recv()
        acc[p, :, cb:] += cr[p, 1].astype(F32)

    def crop_end(p):
        pr, pc = p // 2, p % 2
        c_far[p].wait_recv()
        v = acc[p, :, cb:] + cyr[p].astype(F32)
        o_gbig[:, pr, pl.ds(pc, g.hb, stride=2), :] = v[:br].reshape(-1, g.hb, cb)
        o_gsmall[:, pr, pl.ds(pc, g.hs, stride=2), :] = v[br:].reshape(-1, g.hs, cb)

    down = [t[0] for t in taps]
    z_taps = down[1 : 1 + Z_TAPS]
    x_taps = [t for t in down if t not in z_taps]
    deliveries = []

    def step(what, stage):
        h = what if isinstance(what, Halving) else h_down[what]
        if stage >= n_bits:
            return
        h.step(stage)
        if h.name in ("a", "b", "in") and stage == n_bits - 1:
            deliveries.append(Deliver(h.name))
            deliveries[-1].start()

    def job(kind, key=None):
        if kind == "d":
            down_tap(*where[key])
        elif kind == "near":
            crop_near(key)
        elif kind == "own":
            crop_own(key)
        elif kind == "send":
            crop_send(key)
        elif kind == "end":
            crop_end(key)
        elif kind == "wide":
            wide_g.forward()
            wide_g.near()
        else:
            wide_g.far()
            split_job()
            in_job()

    def early():
        job("d", x_taps[0])
        for t in z_taps:
            job("d", t)
        job("near", 0)
        job("d", x_taps[1])
        job("own", 0)
        job("near", 1)
        job("own", 1)
        job("send", 0)
        job("send", 1)
        job("d", x_taps[2])
        job("wide")

    def after(k):
        if k == 0:
            step(h_b, 0)
            for t in z_taps:
                step(t, 0)
            job("near", 2)
            job("own", 2)
            job("d", x_taps[3])
        elif k == 1:
            step(h_conv[2], 1)
            step(h_conv[0], 2)
            job("split")
            job("send", 2)
            job("d", x_taps[4])
        elif k == 2:
            step(h_conv[1], 2)
            step(h_a, 2)
            step(h_b, 1)
            job("near", 3)
            job("d", x_taps[5])
        elif k == 3:
            for t in z_taps:
                step(t, 1)
            job("own", 3)
            job("send", 3)
            job("end", 0)
        elif k == 4:
            job("d", x_taps[6])
            step(h_conv[2], 2)
            step(h_in, 0)
        elif k == 5:
            job("end", 1)
            for t in x_taps[7:]:
                job("d", t)
            step(h_b, 2)
        elif k == 6:
            step(h_in, 1)
            job("end", 2)
        elif k == 7:
            job("end", 3)

    early()
    last = len(x_taps) - 1
    for k in range(last + n_bits + 1):
        for stage in range(n_bits):
            j = k - stage - (1 if stage >= 2 else 0)
            if 0 <= j <= last:
                step(x_taps[j], stage)
        after(k)
        if k == last + 1:
            step(h_in, 2)
            for h in (h_a, h_b, h_in, *h_conv):
                for stage in range(3, n_bits):
                    step(h, stage)
            for t in z_taps:
                for stage in range(2, n_bits):
                    step(t, stage)

    for d in deliveries:
        d.finish()
    for c in ld_m:
        c.wait()

    def sq(value):
        v = value * value
        while v.ndim > 2:
            v = jnp.sum(v, axis=0)
        v = jnp.sum(v, axis=0, keepdims=True)
        out = v[:, 0:128]
        for k in range(128, v.shape[1], 128):
            out = out + v[:, k : k + 128]
        return out

    grads = {
        "down": S["g_down"][...],
        "a": S["g_a"][...],
        "b": S["g_b"][...],
        "in": S["g_in"][...],
    }
    g_conv = S["g_conv"]
    layers = ("down", "a", "b", "in", "conv")
    nm = S["nm"]
    lane = lax.broadcasted_iota(jnp.int32, (1, 128), 1)
    mine = jnp.zeros((1, 128), F32)
    for i, name in enumerate(layers):
        weight = S["k_" + name][...].astype(F32)
        grad = g_conv[...] if name == "conv" else grads[name]
        mine = jnp.where(lane == i, jnp.sum(sq(weight), axis=1, keepdims=True), mine)
        mine = jnp.where(lane == 5 + i, jnp.sum(sq(grad), axis=1, keepdims=True), mine)
    place = nm.at[dp * 4 + ch]
    place[...] = mine
    ssem, rsem = sem(), sem()
    everyone(
        lambda peer: pltpu.make_async_remote_copy(
            src_ref=place, dst_ref=place, send_sem=ssem, recv_sem=rsem,
            device_id=peer, device_id_type=MESH,
        ).start()
    )
    some = nm.at[pl.ds(0, 4 * n - 1)]
    total(some, rsem).wait()
    total(some, ssem).wait()
    roots = jnp.sqrt(jnp.sum(nm[...], axis=0))
    norms = [jnp.sum(jnp.where(lane == k, roots, 0.0), axis=1, keepdims=True) for k in range(10)]
    row = lax.broadcasted_iota(jnp.int32, (2, 5), 0)
    col = lax.broadcasted_iota(jnp.int32, (2, 5), 1)
    table = jnp.zeros((2, 5), F32)
    for k in range(10):
        table = jnp.where((row == k // 5) & (col == k % 5), norms[k], table)
    o_ln[...] = table
    o_wn[0:1] = qn1
    o_wn[1:2] = q1
    o_nn[0, 0:1] = qn2
    o_nn[0, 1:2] = q2
    o_nn[1, 0:1] = qn3
    o_nn[1, 1:2] = q3

    def update(rate, weight, grad, moment):
        after = MOMENTUM * moment + rate * (grad + DECAY * weight)
        return weight - after, after

    for i, name in enumerate(layers):
        wnorm = norms[i]
        rate = TRUST * wnorm / (norms[5 + i] + DECAY * wnorm)
        o_new, o_next = {
            "down": (o_ndown, o_mdown), "a": (o_na, o_ma), "b": (o_nb, o_mb),
            "in": (o_nin, o_min), "conv": (o_nconv, o_mconv),
        }[name]
        if name == "down":
            for t in range(9):
                new, after = update(
                    rate, S["k_down"][t].astype(F32), S["g_down"][t], S["m_down"][t]
                )
                o_new[t] = new
                o_next[t] = after
        elif name == "conv":
            for t in range(9):
                new, after = update(
                    rate,
                    S["k_conv"][t].astype(F32),
                    g_conv[:, t * nc : (t + 1) * nc],
                    S["m_conv"][t],
                )
                o_new[t] = new
                o_next[t] = after
        else:
            new, after = update(rate, S["k_" + name][...].astype(F32), grads[name], S["m_" + name][...])
            o_new[...] = new
            o_next[...] = after
    for c in pending:
        c.wait_send()
    for c in drain:
        c.wait()
    assert used[0] == sems.shape[0], used[0]


def hand_over(*refs):
    count = len(refs) // 2
    copies = [
        pltpu.make_async_copy(refs[k], refs[count + k], refs[-1].at[k]) for k in range(count)
    ]
    for c in copies:
        c.start()
    for c in copies:
        c.wait()


def per_device(
    big_crops, small_crops, conv_down, split_a, split_b, neck_in, neck_conv, norm_wide, norm_neck,
    cot_big, cot_small, mom_down, mom_a, mom_b, mom_in, mom_conv,
):
    n = lax.axis_size("dp")
    g = Geometry(big_crops.shape, small_crops.shape, conv_down.shape, neck_conv.shape, n)

    def taps_first(w):
        return jnp.transpose(w, (1, 2, 0, 3)).reshape(9, w.shape[0], w.shape[3])

    def taps_back(w):
        return jnp.transpose(w.reshape(3, 3, w.shape[1], w.shape[2]), (2, 0, 1, 3))

    args = (
        big_crops.reshape(g.nb * g.hb * 2, 2 * g.hb, g.cb),
        small_crops.reshape(g.ns * g.hs * 2, 2 * g.hs, g.cb),
        taps_first(conv_down), split_a, split_b, neck_in, taps_first(neck_conv),
        norm_wide, norm_neck,
        cot_big.reshape(2, g.big_rows, g.nc), cot_small.reshape(2, g.small_rows, g.nc),
        taps_first(mom_down), mom_a, mom_b, mom_in, taps_first(mom_conv),
    )
    sds = jax.ShapeDtypeStruct
    up = [
        sds((9, g.ch // n, g.wc), F32), sds(mom_a.shape, F32), sds(mom_b.shape, F32),
        sds(mom_in.shape, F32), sds((9, g.ch // n, g.nc), F32),
    ]
    out_shape = [
        sds((2, g.big_rows, g.nc), BF16), sds((2, g.small_rows, g.nc), BF16),
        sds((g.nb * g.hb, 2, 2 * g.hb, g.cb), F32), sds((g.ns * g.hs, 2, 2 * g.hs, g.cb), F32),
        *up, *up,
        sds((2, g.wc), F32), sds((2, 2, g.nc), F32), sds((2, 5), F32),
    ]
    anywhere = pl.BlockSpec(memory_space=pl.ANY)
    vmem = pl.BlockSpec(memory_space=pltpu.VMEM)
    plan = scratch_plan(g)
    res = pl.pallas_call(
        functools.partial(mega, g, tuple(plan)),
        out_shape=[pltpu.VMEM(o.shape, o.dtype) for o in out_shape],
        in_specs=[anywhere] * 16,
        out_specs=[vmem] * 17,
        scratch_shapes=[pltpu.VMEM(shape, dtype) for shape, dtype in plan.values()]
        + [pltpu.SemaphoreType.DMA((count_sems(n),))],
        compiler_params=pltpu.CompilerParams(
            collective_id=0, has_side_effects=True, vmem_limit_bytes=58 * 2**20
        ),
    )(*args)
    res = pl.pallas_call(
        hand_over,
        out_shape=out_shape,
        in_specs=[anywhere] * 17,
        out_specs=[anywhere] * 17,
        scratch_shapes=[pltpu.SemaphoreType.DMA((17,))],
        compiler_params=pltpu.CompilerParams(vmem_limit_bytes=2**20),
    )(*res)
    res = list(res)
    res[0] = res[0].reshape(cot_big.shape)
    res[1] = res[1].reshape(cot_small.shape)
    res[2] = res[2].reshape(big_crops.shape)
    res[3] = res[3].reshape(small_crops.shape)
    for k in (4, 8, 9, 13):
        res[k] = taps_back(res[k])
    return tuple(res)


def solution(mesh):
    in_specs = (
        P("dp", None, None, "chan"),
        P("dp", None, None, "chan"),
        P(None, None, None, "chan"),
        P(None, "chan"),
        P(None, "chan"),
        P(None, "chan"),
        P(None, None, None, "chan"),
        P(),
        P(),
        P(None, "dp", None, None, "chan"),
        P(None, "dp", None, None, "chan"),
        P("dp", None, None, "chan"),
        P("dp", "chan"),
        P("dp", "chan"),
        P("dp", "chan"),
        P("dp", None, None, "chan"),
    )
    out_specs = (
        P(None, "dp", None, None, "chan"),
        P(None, "dp", None, None, "chan"),
        P("dp", None, None, "chan"),
        P("dp", None, None, "chan"),
        P("dp", None, None, "chan"),
        P("dp", "chan"),
        P("dp", "chan"),
        P("dp", "chan"),
        P("dp", None, None, "chan"),
        P("dp", None, None, "chan"),
        P("dp", "chan"),
        P("dp", "chan"),
        P("dp", "chan"),
        P("dp", None, None, "chan"),
        P(None, "chan"),
        P(None, None, "chan"),
        P(),
    )
    return jax.shard_map(
        per_device, mesh=mesh, in_specs=in_specs, out_specs=out_specs, check_vma=False
    )
```

```python
import functools

import jax
import jax.numpy as jnp
from jax import lax
from jax.experimental import pallas as pl
from jax.experimental.pallas import tpu as pltpu
from jax.sharding import PartitionSpec as P

EPSILON = 1e-05
MOMENTUM = 0.9
DECAY = 0.0005
TRUST = 0.1
F32 = jnp.float32
BF16 = jnp.bfloat16
MESH = pl.DeviceIdType.MESH
PLANES = (3, 1, 2, 0)


def dot_nn(left, right):
    return lax.dot_general(left, right, (((1,), (0,)), ((), ())), preferred_element_type=F32)


def dot_nt(left, right):
    return lax.dot_general(left, right, (((1,), (1,)), ((), ())), preferred_element_type=F32)


def dot_tn(left, right):
    return lax.dot_general(left, right, (((0,), (0,)), ((), ())), preferred_element_type=F32)


def mish_parts(v):
    u = jnp.exp(-jnp.abs(v))
    pos = v >= 0
    num = jnp.where(pos, 1.0 + 2.0 * u, u * (u + 2.0))
    rest = jnp.where(pos, 2.0 * u * u, 2.0)
    den = num + rest
    inv = 1.0 / den
    tangent = num * inv
    slope = tangent + v * (rest * (den + num) * inv * inv) * (jnp.where(pos, 1.0, u) / (1.0 + u))
    return v * tangent, slope


def plane_taps(p):
    rows = ((0, -1), (2, 0)) if p // 2 else ((1, 0),)
    cols = ((0, -1), (2, 0)) if p % 2 else ((1, 0),)
    return [(r * 3 + s, di, dj) for r, di in rows for s, dj in cols]


def group_of(di, dj):
    return (2 if di else 0) + (1 if dj else 0)


class Geometry:
    def __init__(self, big, small, down, neck, n_dp):
        self.nb, self.hb = big[0], big[1] // 2
        self.ns, self.hs = small[0], small[1] // 2
        self.cb = big[3]
        self.ch = down[0]
        self.wc = down[3]
        self.nc = neck[3]
        self.n = n_dp
        self.big_rows = self.nb * self.hb * self.hb
        self.small_rows = self.ns * self.hs * self.hs
        self.rows = self.big_rows + self.small_rows
        self.total_rows = self.rows * n_dp
        self.tiles = [
            (i * self.hb * self.hb, self.hb * self.hb, 1, self.hb) for i in range(self.nb)
        ] + [(self.big_rows, self.small_rows, self.ns, self.hs)]


def shift_tile(value, tile, di, dj):
    _, rows, images, side = tile
    cols = value.shape[-1]
    if di:
        v = value.reshape(images, side, side, cols)
        blank = jnp.zeros((images, 1, side, cols), value.dtype)
        if di < 0:
            v = jnp.concatenate([blank, v[:, :-1]], axis=1)
        else:
            v = jnp.concatenate([v[:, 1:], blank], axis=1)
        value = v.reshape(rows, cols)
    if dj:
        v = pltpu.roll(value, 1 if dj < 0 else rows - 1, 0).reshape(rows // side, side, cols)
        at = lax.broadcasted_iota(jnp.int32, (1, side, cols), 1)
        keep = at >= 1 if dj < 0 else at < side - 1
        value = jnp.where(keep, v, 0.0).reshape(rows, cols)
    return value


def bits_of(n):
    return n.bit_length() - 1


def halving_plan(order):
    left = sorted(order)
    plan = []
    for bit in order:
        at = left.index(bit)
        plan.append((bit, 1 << (len(left) - 1 - at), 1 << at))
        left.remove(bit)
    return plan


CONV_SPLIT = (3, 3, 3)


def pair_bit(n):
    return bits_of(n) - 2


def reductions(g):
    rows = g.ch // g.n
    bits = tuple(range(bits_of(g.n)))
    paired = tuple(bit for bit in bits if bit != pair_bit(g.n))
    return {
        "down": (18, rows, g.wc // 2, paired),
        **{f"c{k}": (1, rows, t * g.nc, paired) for k, t in enumerate(CONV_SPLIT)},
        "a": (1, 2 * rows, g.nc, bits),
        "b": (1, 2 * rows, g.nc, bits),
        "in": (1, rows, g.nc, bits),
    }


def scratch_plan(g):
    n = g.n
    R = g.rows
    s = {}
    s["raw_big"] = ((g.nb * g.hb * 2, 2 * g.hb, g.cb), BF16)
    s["raw_small"] = ((g.ns * g.hs * 2, 2 * g.hs, g.cb), BF16)
    s["xg"] = ((4, 4, R, g.cb), BF16)
    s["wv"] = ((9, g.ch, g.wc), BF16)
    s["wn"] = ((g.ch, 9 * g.nc), BF16)
    s["ab"] = ((2 * g.ch, 2 * g.nc), BF16)
    s["nin"] = ((4, g.ch, g.nc), BF16)
    s["sar"] = ((4, g.wc, g.nc), BF16)
    s["sbr"] = ((4, g.wc, g.nc), BF16)
    s["cmat"] = ((4, g.wc, g.nc), BF16)
    s["pw"] = ((2, 4 * g.wc), F32)
    s["pn"] = ((2, 2, 4 * g.nc), F32)
    s["acc"] = ((4, R, g.wc), F32)
    s["n1"] = ((R, g.wc), F32)
    s["s1"] = ((R, g.wc), F32)
    s["wg"] = ((4, R, g.wc), BF16)
    for k in ("f", "b"):
        s["rs_send" + k] = ((2, R, g.nc), BF16)
        s["rs_recv" + k] = ((2, R, g.nc), BF16)
        s["rs_ys" + k] = ((R, g.nc), BF16)
        s["rs_yr" + k] = ((R, g.nc), BF16)
    s["rs_keep"] = ((2, R, g.nc), F32)
    s["n2"] = ((R, g.nc), F32)
    s["s2"] = ((R, g.nc), F32)
    s["fg"] = ((4, R, g.nc), BF16)
    s["yb"] = ((R, 9 * g.nc), F32)
    s["n3"] = ((R, g.nc), F32)
    s["s3"] = ((R, g.nc), F32)
    s["cg"] = ((R, 9 * g.nc), BF16)
    s["ga"] = ((4, R, g.nc), BF16)
    s["gb"] = ((4, R, g.nc), BF16)
    s["pb"] = ((R, g.nc), BF16)
    s["ng"] = ((4, R, g.nc), BF16)
    s["u"] = ((R, g.wc), F32)
    s["gsh"] = ((4, R, g.wc), BF16)
    s["cs"] = ((4, 2, R, g.cb), BF16)
    s["cr"] = ((4, 2, R, g.cb), BF16)
    s["cys"] = ((4, R, g.cb), BF16)
    s["cyr"] = ((4, R, g.cb), BF16)
    s["st"] = ((6, n, 2, g.wc), F32)
    s["nm"] = ((4 * n, 1, 128), F32)
    for name, (count, rows, cols, order) in reductions(g).items():
        for stage, (_, high, low) in enumerate(halving_plan(order)):
            s[f"h_{name}_s{stage}"] = ((count, high, 2, low, rows, cols), BF16)
            s[f"h_{name}_r{stage}"] = ((count, high, low, rows, cols), BF16)
    s["xz"] = ((2, 4, R, g.cb), BF16)
    s["fz"] = ((2, R, g.nc), BF16)
    s["cz"] = ((R, g.nc), BF16)
    s["cgz"] = ((R, 9 * g.nc), BF16)
    s["gz"] = ((2, R, g.wc // 2), BF16)
    s["qs"] = ((R, g.wc), BF16)
    s["nb"] = ((R, g.wc), BF16)
    s["nz"] = ((R, g.wc), BF16)
    s["gzs"] = ((4, R, g.wc), BF16)
    s["g_down"] = ((9, g.ch // n, g.wc), F32)
    s["g_conv"] = ((g.ch // n, 9 * g.nc), F32)
    s["p_a"] = ((2 * g.ch // n, g.nc), BF16)
    s["p_b"] = ((2 * g.ch // n, g.nc), BF16)
    s["p_in"] = ((g.ch // n, g.nc), BF16)
    s["g_a"] = ((2 * g.ch // n, g.nc), BF16)
    s["g_b"] = ((2 * g.ch // n, g.nc), BF16)
    s["g_in"] = ((g.ch // n, g.nc), BF16)
    s["m_down"] = ((9, g.ch // n, g.wc), F32)
    s["m_a"] = ((2 * g.ch // n, g.nc), F32)
    s["m_b"] = ((2 * g.ch // n, g.nc), F32)
    s["m_in"] = ((g.ch // n, g.nc), F32)
    s["m_conv"] = ((9, g.ch // n, g.nc), F32)
    s["k_down"] = ((9, g.ch // n, g.wc), BF16)
    s["k_a"] = ((2 * g.ch // n, g.nc), BF16)
    s["k_b"] = ((2 * g.ch // n, g.nc), BF16)
    s["k_in"] = ((g.ch // n, g.nc), BF16)
    s["k_conv"] = ((9, g.ch // n, g.nc), BF16)
    return s


def count_sems(g):
    used = BASE_SEMS
    for count, _, _, order in reductions(g).values():
        used += len(order) * (1 + count) if count > 1 else 1 + len(order)
    return used


BASE_SEMS = 106


def mega(g, names, *refs):
    (
        big, small, w_down, w_a, w_b, w_in, w_conv, p_wide, p_neck, c_big, c_small,
        m_down, m_a, m_b, m_in, m_conv,
    ) = refs[:16]
    (
        o_big, o_small, o_gbig, o_gsmall, o_ndown, o_na, o_nb, o_nin, o_nconv,
        o_mdown, o_ma, o_mb, o_min, o_mconv, o_wn, o_nn, o_ln,
    ) = refs[16:33]
    S = dict(zip(names, refs[33:-1], strict=True))
    sems = refs[-1]
    n, R, nc, wc, cb = g.n, g.rows, g.nc, g.wc, g.cb
    dp = lax.axis_index("dp")
    ch = lax.axis_index("chan")
    core = lax.rem(ch, 2)
    half = lax.div(ch, 2)
    sib = half * 2 + (1 - core)
    yp = (1 - half) * 2 + core
    diag = (1 - half) * 2 + (1 - core)
    other = 1 - half

    pair = pair_bit(n)
    pbit = lax.rem(lax.div(dp, 1 << pair), 2)
    mate = (dp + (1 - 2 * pbit) * (1 << pair), ch)
    gives = core != pbit
    takes = core == pbit

    used = [0]
    pending = []
    drain = []

    def sem():
        used[0] += 1
        return sems.at[used[0] - 1]

    load_sems = []

    def local(src, dst, own=None):
        if own is None:
            own = sem()
            load_sems.append(own)
        copy = pltpu.make_async_copy(src, dst, own)
        copy.start()
        return copy

    def remote(src, dst, device, ssem=None, rsem=None):
        copy = pltpu.make_async_remote_copy(
            src_ref=src, dst_ref=dst,
            send_sem=sem() if ssem is None else ssem,
            recv_sem=sem() if rsem is None else rsem,
            device_id=device, device_id_type=MESH,
        )
        if ssem is None:
            pending.append(copy)
        return copy

    def total(view, one):
        return pltpu.make_async_copy(view, view, one)

    def shared(view):
        one = sem()
        drain.append(total(view, one))
        return one
    ld_big = local(big, S["raw_big"])
    ld_small = local(small, S["raw_small"])
    ld_wv = local(w_down, S["wv"])
    ab_sem, wn_sem, ga_sem, gb_sem = sem(), sem(), sem(), sem()
    local(w_a, S["ab"].at[:, pl.ds(0, nc)], ab_sem)
    local(w_b, S["ab"].at[:, pl.ds(nc, nc)], ab_sem)
    ld_ab = total(S["ab"], ab_sem)
    ld_in = local(w_in, S["nin"].at[ch])
    ld_p = [local(p_wide, S["pw"]), local(p_neck, S["pn"])]
    for t in range(9):
        local(w_conv.at[t], S["wn"].at[:, pl.ds(t * nc, nc)], wn_sem)
    ld_wn = total(S["wn"], wn_sem)
    br, sr = g.big_rows, g.small_rows
    ld_c = []
    for k, name, one in ((0, "ga", ga_sem), (1, "gb", gb_sem)):
        local(c_big.at[k], S[name].at[ch, pl.ds(0, br)], one)
        local(c_small.at[k], S[name].at[ch, pl.ds(br, sr)], one)
        ld_c.append(total(S[name].at[ch], one))
    bar = pltpu.get_barrier_semaphore()

    def everyone(act):
        def one(k):
            act((lax.rem(dp + lax.div(k, 4), n), lax.rem(ch + lax.rem(k, 4), 4)))

        if n <= 8:
            for k in range(1, 4 * n):
                one(k)
        else:
            lax.fori_loop(1, 4 * n, lambda k, c: (one(k), c)[1], 0)

    bits = [lax.rem(lax.div(dp, 1 << i), 2) for i in range(bits_of(n))]
    dp_peers = [
        sum(((1 - b) if k >> i & 1 else b) * (1 << i) for i, b in enumerate(bits))
        for k in range(n - 1, 0, -1)
    ]
    peers = [(dp, yp), (dp, sib), (dp, diag)] + [(peer, ch) for peer in dp_peers]
    for peer in peers:
        pl.semaphore_signal(bar, inc=1, device_id=peer, device_id_type=MESH)
    xg = S["xg"]
    ld_big.wait()
    o_gbig[...] = S["raw_big"][...].astype(F32).reshape(o_gbig.shape)
    ld_small.wait()
    o_gsmall[...] = S["raw_small"][...].astype(F32).reshape(o_gsmall.shape)

    def split_plane(p):
        pr, pc = p // 2, p % 2
        xg[ch, p, 0:br] = (
            o_gbig[:, pr, pl.ds(pc, g.hb, stride=2), :].reshape(br, cb).astype(BF16)
        )
        xg[ch, p, br:R] = (
            o_gsmall[:, pr, pl.ds(pc, g.hs, stride=2), :].reshape(sr, cb).astype(BF16)
        )

    class Gather:
        def __init__(self, ref, plane=None, ssems=None):
            def block(c):
                return ref.at[c] if plane is None else ref.at[c, plane]

            if ssems is None:
                ssems = [shared(ref.at[pl.ds(0, 3)])] * 3
            self.to_sib = remote(block(ch), block(ch), (dp, sib), ssems[0])
            self.to_far = remote(block(ch), block(ch), (dp, yp), ssems[1])
            self.onward = remote(block(yp), block(yp), (dp, sib), ssems[2])

        def start(self):
            self.to_sib.start()
            self.to_far.start()

        def forward(self):
            self.to_far.wait_recv()
            self.onward.start()

        def near(self):
            self.to_sib.wait_recv()

        def far(self):
            self.onward.wait_recv()

    crop_sems = [shared(xg.at[0]) for _ in range(3)]
    crops = {p: Gather(xg, p, crop_sems) for p in PLANES}
    split_plane(PLANES[0])
    pl.semaphore_wait(bar, len(peers))
    class Cross:
        def __init__(self, buf, source):
            self.buf, self.source = S[buf], source
            self.ssem, self.rsem = shared(self.buf), sem()
            self.arrived = total(self.buf, self.rsem)
            self.onward = remote(self.buf, self.buf, (dp, sib), self.ssem, self.rsem)

        def send(self, block, h, *plane):
            @pl.when(gives)
            def _():
                remote(
                    self.source.at[(block, *plane)], self.buf.at[(h, *plane)], mate,
                    self.ssem, self.rsem,
                ).start()

        def hand_on(self):
            @pl.when(takes)
            def _():
                self.arrived.wait()
                self.onward.start()

        def finish(self):
            @pl.when(gives)
            def _():
                self.arrived.wait()

    cross_x = Cross("xz", xg)
    crops[PLANES[0]].start()
    cross_x.send(ch, half, PLANES[0])
    for p in PLANES[1:]:
        split_plane(p)
        crops[p].start()
        cross_x.send(ch, half, p)
    ld_in.wait()
    neck_in = Gather(S["nin"])
    ld_ab.wait()

    class Rows:
        def __init__(self, buf, lane):
            ref = S[buf]
            ssem, rsem = shared(ref.at[pl.ds(0, 3)]), sem()
            self.copies = [
                remote(
                    S["ab"].at[pl.ds(dev * wc, wc), pl.ds(lane, nc)], ref.at[ch], (dp, dev),
                    ssem, rsem,
                )
                for dev in (yp, diag, sib)
            ]
            self.arrived = total(ref.at[pl.ds(0, 3)], rsem)
            ref[ch] = S["ab"][pl.ds(ch * wc, wc), lane : lane + nc]

        def start(self):
            for c in self.copies:
                c.start()

        def wait(self):
            self.arrived.wait()

    b_rows = Rows("sbr", nc)
    a_rows = Rows("sar", 0)
    b_rows.start()
    neck_in.start()
    ld_wv.wait()
    wv, acc = S["wv"], S["acc"]

    def conv_part(side, p, first):
        x = jnp.concatenate([xg[2 * side, p], xg[2 * side + 1, p]], axis=1)
        for tap, di, dj in plane_taps(p):
            res = dot_nn(x, wv[tap, pl.ds(side * 2 * cb, 2 * cb), :])
            k = group_of(di, dj)
            if first:
                acc[k] = res
            else:
                acc[k] += res
    for p in PLANES:
        crops[p].near()
        conv_part(half, p, p == PLANES[0])
    for p in PLANES[:-1]:
        crops[p].forward()
        cross_x.send(yp, other, p)
        crops[p].far()
        conv_part(other, p, False)
    for tile in g.tiles:
        at = pl.ds(tile[0], tile[1])
        inner = acc[1, at] + shift_tile(acc[3, at], tile, -1, 0)
        acc[2, at] = shift_tile(acc[2, at], tile, -1, 0) + shift_tile(inner, tile, 0, -1)
    p = PLANES[-1]
    crops[p].forward()
    cross_x.send(yp, other, p)
    crops[p].far()
    conv_part(other, p, False)
    acc[0] = acc[0] + acc[2]

    st = S["st"]
    st_send, st_recv = sem(), [sem(), sem()]

    def exchange(phase, first, second, cols):
        st[phase, dp, 0:1, 0:cols] = first
        st[phase, dp, 1:2, 0:cols] = second
        ssem, rsem = st_send, st_recv[phase % 2]
        mine = st.at[phase, dp, :, pl.ds(0, cols)]
        for peer in dp_peers:
            pltpu.make_async_remote_copy(
                src_ref=mine, dst_ref=mine, send_sem=ssem, recv_sem=rsem,
                device_id=(peer, ch), device_id_type=MESH,
            ).start()
        some = st.at[phase, pl.ds(0, n - 1), :, pl.ds(0, cols)]

        def finish():
            total(some, rsem).wait()
            total(some, ssem).wait()
            return st[phase, :, :, 0:cols]

        return finish

    def norm_start(phase, ref):
        cols = ref.shape[-1]
        mean = jnp.sum(ref[...], axis=0, keepdims=True) * (1.0 / R)
        dev = ref[...] - mean
        return exchange(phase, mean, jnp.sum(dev * dev, axis=0, keepdims=True), cols)

    def norm_finish(finish):
        v = finish()
        tot = jnp.sum(v, axis=0)
        mean = tot[0:1] * (1.0 / n)
        off = v - mean[None]
        spread = jnp.sum(off * off, axis=0)[0:1]
        var = (tot[1:2] + R * spread) * (1.0 / g.total_rows)
        return mean, lax.rsqrt(var + EPSILON)

    def sums_finish(finish):
        tot = jnp.sum(finish(), axis=0)
        return tot[0:1], tot[1:2]
    fin = norm_start(0, acc.at[0])
    for c in ld_p:
        c.wait()
    gain1 = S["pw"][0:1, pl.ds(ch * wc, wc)]
    bias1 = S["pw"][1:2, pl.ds(ch * wc, wc)]
    neck_in.forward()
    neck_in.near()
    neck_in.far()
    b_rows.wait()
    rows_b = jnp.concatenate([S["sbr"][k] for k in range(4)], axis=1)
    for k in range(4):
        S["cmat"][k] = dot_nn(rows_b, S["nin"][k]).astype(BF16)
    mean1, inv1 = norm_finish(fin)
    wg = S["wg"]
    for t0 in range(0, R, 256):
        at = pl.ds(t0, 256)
        normed = (acc[0, at] - mean1) * inv1
        S["n1"][at] = normed
        S["nb"][at] = normed.astype(BF16)
        act, slope = mish_parts(normed * gain1 + bias1)
        wg[ch, at] = act.astype(BF16)
        S["s1"][at] = slope

    def reduce_chan(k, pair):
        send, recv = S["rs_send" + k], S["rs_recv" + k]
        ys, yr, keep = S["rs_ys" + k], S["rs_yr" + k], S["rs_keep"]
        parts = [pl.ds(0, R // 2), pl.ds(R // 2, R // 2)]
        s0, sy, r1 = shared(send), shared(ys), sem()
        c0 = [remote(send.at[0, at], recv.at[0, at], (dp, sib), s0) for at in parts]
        c1 = [remote(send.at[1, at], recv.at[1, at], (dp, sib), s0, r1) for at in parts]
        cy = [remote(ys.at[at], yr.at[at], (dp, yp), sy) for at in parts]
        for at, far, near in zip(parts, c0, c1, strict=True):
            part = pair(at, diag, sib).astype(BF16)
            send[0, at] = part[:, :nc]
            far.start()
            send[1, at] = part[:, nc:]
            near.start()
        for at, near, far in zip(parts, c0, cy, strict=True):
            part = pair(at, yp, ch)
            keep[1, at] = part[:, nc:]
            near.wait_recv()
            ys[at] = (part[:, :nc] + recv[0, at].astype(F32)).astype(BF16)
            far.start()
        total(recv.at[1], r1).wait()
        keep[1] += recv[1].astype(F32)

        def finish():
            for at, far in zip(parts, cy, strict=True):
                far.wait_recv()
                keep[1, at] += yr[at].astype(F32)

        return finish

    def neck_pair(at, d0, d1):
        return dot_nn(
            wg[ch, at], jnp.concatenate([S["cmat"][d0], S["cmat"][d1]], axis=1)
        )
    upper, lower = pl.ds(0, R // 2), pl.ds(R // 2, R // 2)
    n_mate = [remote(S["nb"].at[at], S["nz"].at[at], mate) for at in (upper, lower)]
    n_mate[0].start()
    rs_fin = reduce_chan("f", neck_pair)
    for c in ld_c:
        c.wait()
    gb_g = Gather(S["gb"])
    ga_g = Gather(S["ga"])
    wide_g = Gather(wg)
    cross_x.hand_on()
    rs_fin()
    a_rows.start()
    z2 = S["rs_keep"].at[1]
    fin = norm_start(1, z2)
    n_mate[1].start()
    gain2 = S["pn"][0, 0:1, pl.ds(ch * nc, nc)]
    bias2 = S["pn"][0, 1:2, pl.ds(ch * nc, nc)]
    gain3 = S["pn"][1, 0:1, pl.ds(ch * nc, nc)]
    bias3 = S["pn"][1, 1:2, pl.ds(ch * nc, nc)]
    mean2, inv2 = norm_finish(fin)
    fg = S["fg"]
    for t0 in range(0, R, 256):
        at = pl.ds(t0, 256)
        normed = (z2[at] - mean2) * inv2
        S["n2"][at] = normed
        act, slope = mish_parts(normed * gain2 + bias2)
        fg[ch, at] = act.astype(BF16)
        S["s2"][at] = slope
    first_g = Gather(fg)
    first_g.start()
    ld_wn.wait()
    wn, yb = S["wn"], S["yb"]

    def neck_part(side, first):
        x = jnp.concatenate([fg[2 * side], fg[2 * side + 1]], axis=1)
        w = wn[pl.ds(side * 2 * nc, 2 * nc), :]
        if first:
            yb[...] = dot_nn(x, w)
        else:
            yb[...] += dot_nn(x, w)

    first_g.near()
    neck_part(half, True)
    first_g.forward()
    first_g.far()
    gb_g.start()
    ga_g.start()
    neck_part(other, False)
    z3 = S["n3"]
    for tile in g.tiles:
        at = pl.ds(tile[0], tile[1])
        cols = []
        for s in range(3):
            cols.append(
                yb[at, (3 + s) * nc : (4 + s) * nc]
                + shift_tile(yb[at, s * nc : (s + 1) * nc], tile, -1, 0)
                + shift_tile(yb[at, (6 + s) * nc : (7 + s) * nc], tile, 1, 0)
            )
        z3[at] = (
            cols[1] + shift_tile(cols[0], tile, 0, -1) + shift_tile(cols[2], tile, 0, 1)
        )
    fin = norm_start(2, z3)
    cross_f = Cross("fz", fg)
    cross_f.send(ch, half)
    cross_f.send(yp, other)
    mean3, inv3 = norm_finish(fin)
    q_tot = jnp.zeros((1, nc), F32)
    qn_tot = jnp.zeros((1, nc), F32)
    for t0 in range(0, R, 256):
        at = pl.ds(t0, 256)
        normed = (z3[at] - mean3) * inv3
        act, slope = mish_parts(normed * gain3 + bias3)
        q = S["gb"][ch, at].astype(F32) * slope
        z3[at] = normed
        S["s3"][at] = q
        S["yb"][at, 0:nc] = act
        q_tot += jnp.sum(q, axis=0, keepdims=True)
        qn_tot += jnp.sum(q * normed, axis=0, keepdims=True)
    fin = exchange(3, qn_tot, q_tot, nc)

    def grad_in(q, normed, gain, inv, qn_sum, q_sum):
        return gain * inv * (
            q - q_sum * (1.0 / g.total_rows) - normed * (qn_sum * (1.0 / g.total_rows))
        )

    stage_sems = {}
    plans = reductions(g)

    class Halving:
        def __init__(self, name, item, result):
            self.name, self.item, self.result = name, item, result
            self.plan = halving_plan(plans[name][3])
            self.copies = []
            self.alone = S[f"h_{name}_s0"].shape[0] == 1
            if name not in stage_sems:
                stages = range(len(self.plan))
                stage_sems[name] = (
                    [sem()] * len(self.plan)
                    if self.alone
                    else [shared(S[f"h_{name}_s{i}"].at[:, :, 0]) for i in stages]
                )
            for i, (bit, high, low) in enumerate(self.plan):
                own = lax.rem(lax.div(dp, 1 << bit), 2)
                peer = dp + (1 - 2 * own) * (1 << bit)
                send = S[f"h_{name}_s{i}"]
                recv = S[f"h_{name}_r{i}"]
                self.copies.append(
                    remote(
                        send.at[item, :, 1 - own], recv.at[item], (peer, ch), stage_sems[name][i]
                    )
                )

        def start(self, stage=0):
            self.copies[stage].start()

        def step(self, stage):
            bit, high, low = self.plan[stage]
            own = lax.rem(lax.div(dp, 1 << bit), 2)
            send = S[f"h_{self.name}_s{stage}"]
            recv = S[f"h_{self.name}_r{stage}"]
            self.copies[stage].wait_recv()
            if self.alone:
                self.copies[stage].wait_send()
            both = send[self.item, :, own].astype(F32) + recv[self.item].astype(F32)
            if stage + 1 < len(self.plan):
                after = S[f"h_{self.name}_s{stage + 1}"]
                after[self.item] = both.astype(BF16).reshape(after.shape[1:])
                self.start(stage + 1)
            else:
                self.result[...] = both[0, 0].astype(self.result.dtype)

    def put_rows(name, value):
        ref = S[f"h_{name}_s0"]
        _, high, _, low, rows, cols = ref.shape
        value = value.astype(BF16)
        for e in range(n):
            r, c = e % (n // 4), e // (n // 4)
            ref[0, e // (2 * low), e // low % 2, e % low] = value[
                r * rows : (r + 1) * rows, c * cols : (c + 1) * cols
            ]

    quarter = n // 4
    at_home = lax.div(dp, quarter) == ch

    class Deliver:
        def __init__(self, name):
            self.src, self.dst = S[f"p_{name}"], S[f"g_{name}"]
            target = (ch * quarter + lax.rem(dp, quarter), lax.div(dp, quarter))
            self.copy = pltpu.make_async_remote_copy(
                src_ref=self.src, dst_ref=self.dst, send_sem=sem(), recv_sem=sem(),
                device_id=target, device_id_type=MESH,
            )

        def start(self):
            @pl.when(at_home)
            def _():
                self.dst[...] = self.src[...]

            @pl.when(jnp.logical_not(at_home))
            def _():
                self.copy.start()

        def finish(self):
            @pl.when(jnp.logical_not(at_home))
            def _():
                self.copy.wait_recv()
                self.copy.wait_send()

    def put(name, item, first_block, value):
        ref = S[f"h_{name}_s0"]
        _, high, _, low, rows, cols = ref.shape
        at = first_block // (2 * low)
        count = value.shape[0] // (rows * 2 * low)
        ref[item, at : at + count] = value.astype(BF16).reshape(count, 2, low, rows, cols)
    gb_g.forward()
    gb_g.near()
    gb_g.far()
    u = S["u"]
    u[...] = dot_nt(
        jnp.concatenate([S["gb"][k] for k in range(4)], axis=1),
        jnp.concatenate([S["sbr"][k] for k in range(4)], axis=1),
    )
    qn3, q3 = sums_finish(fin)
    cg = S["cg"]

    def tap_shifts(dst, tile, v):
        at = pl.ds(tile[0], tile[1])
        for r in range(3):
            vi = shift_tile(v, tile, 1 - r, 0)
            for s in range(3):
                t = r * 3 + s
                dst[at, t * nc : (t + 1) * nc] = shift_tile(vi, tile, 0, 1 - s).astype(BF16)

    for tile in g.tiles:
        at = pl.ds(tile[0], tile[1])
        v = grad_in(S["s3"][at], z3[at], gain3, inv3, qn3, q3)
        tap_shifts(cg, tile, v.astype(BF16).astype(F32))
    to_mate = remote(cg.at[:, pl.ds(4 * nc, nc)], S["cz"], mate)
    to_mate.start()

    rows = g.ch // n
    reuse = [*load_sems, ab_sem, wn_sem, ga_sem, gb_sem]
    ld_m = [
        local(src, S[name], one)
        for (src, name), one in zip(
            (
                (m_down, "m_down"), (m_a, "m_a"), (m_b, "m_b"), (m_in, "m_in"),
                (m_conv, "m_conv"),
                (w_down.at[:, pl.ds(dp * rows, rows)], "k_down"),
                (w_a.at[pl.ds(dp * 2 * rows, 2 * rows)], "k_a"),
                (w_b.at[pl.ds(dp * 2 * rows, 2 * rows)], "k_b"),
                (w_in.at[pl.ds(dp * rows, rows)], "k_in"),
                (w_conv.at[:, pl.ds(dp * rows, rows)], "k_conv"),
            ),
            reuse,
            strict=True,
        )
    ]

    def back_pair(at, d0, d1):
        w = jnp.concatenate([wn[pl.ds(d0 * nc, nc), :], wn[pl.ds(d1 * nc, nc), :]], axis=0)
        return dot_nt(cg[at], w)
    rs_fin = reduce_chan("b", back_pair)
    ga_g.forward()
    ga_g.near()
    ga_g.far()
    a_rows.wait()
    u[...] += dot_nt(
        jnp.concatenate([S["ga"][k] for k in range(4)], axis=1),
        jnp.concatenate([S["sar"][k] for k in range(4)], axis=1),
    )
    h_a = Halving("a", 0, S["p_a"])
    put_rows("a", dot_tn(wg[ch], jnp.concatenate([S["ga"][k] for k in range(4)], axis=1)))
    deliveries = []
    done = {}

    def on(what):
        h = h_down[what] if isinstance(what, int) else what
        stage = done.setdefault((h.name, h.item), 0)
        if stage >= len(h.plan):
            return
        h.step(stage)
        done[h.name, h.item] += 1
        if h.name in ("a", "b", "in") and stage == len(h.plan) - 1:
            deliveries.append(Deliver(h.name))
            deliveries[-1].start()

    starts = [sum(CONV_SPLIT[:k]) * nc for k in range(len(CONV_SPLIT) + 1)]
    h_conv = [
        Halving(f"c{k}", 0, S["g_conv"].at[:, pl.ds(starts[k], starts[k + 1] - starts[k])])
        for k in range(len(CONV_SPLIT))
    ]
    rs_fin()
    q_tot = jnp.zeros((1, nc), F32)
    qn_tot = jnp.zeros((1, nc), F32)
    q2r = S["rs_keep"].at[1]
    for t0 in range(0, R, 256):
        at = pl.ds(t0, 256)
        q = q2r[at] * S["s2"][at]
        q2r[at] = q
        q_tot += jnp.sum(q, axis=0, keepdims=True)
        qn_tot += jnp.sum(q * S["n2"][at], axis=0, keepdims=True)
    fin = exchange(4, qn_tot, q_tot, nc)
    h_a.start()
    cross_f.hand_on()
    to_mate.wait_recv()
    for tile in g.tiles:
        tap_shifts(S["cgz"], tile, S["cz"][pl.ds(tile[0], tile[1])].astype(F32))
    cross_f.finish()
    mine = jnp.concatenate([fg[pbit], fg[pbit + 2]], axis=1)
    theirs = jnp.concatenate([S["fz"][0], S["fz"][1]], axis=1)
    for k, h in enumerate(h_conv):
        cols = slice(starts[k], starts[k + 1])
        put(h.name, 0, 0, dot_tn(mine, cg[:, cols]) + dot_tn(theirs, S["cgz"][:, cols]))
        h.start()
    qn2, q2 = sums_finish(fin)
    ng = S["ng"]
    for t0 in range(0, R, 256):
        at = pl.ds(t0, 256)
        ng[ch, at] = grad_in(q2r[at], S["n2"][at], gain2, inv2, qn2, q2).astype(BF16)
    neck_g = Gather(ng)
    neck_g.start()
    def wide_part(side):
        return dot_nt(
            jnp.concatenate([ng[2 * side], ng[2 * side + 1]], axis=1),
            jnp.concatenate([S["cmat"][2 * side], S["cmat"][2 * side + 1]], axis=1),
        )
    neck_g.near()
    u[...] += wide_part(half)
    on(h_a)
    on(h_conv[0])
    neck_g.forward()
    neck_g.far()
    wide_g.start()
    u[...] += wide_part(other)
    q_tot = jnp.zeros((1, wc), F32)
    qn_tot = jnp.zeros((1, wc), F32)
    for t0 in range(0, R, 256):
        at = pl.ds(t0, 256)
        q = u[at] * S["s1"][at]
        u[at] = q
        q_tot += jnp.sum(q, axis=0, keepdims=True)
        qn_tot += jnp.sum(q * S["n1"][at], axis=0, keepdims=True)
    fin = exchange(5, qn_tot, q_tot, wc)
    for t0 in range(0, R, 256):
        at = pl.ds(t0, 256)
        S["qs"][at] = (u[at] - q_tot * (1.0 / R) - S["n1"][at] * (qn_tot * (1.0 / R))).astype(BF16)
    hw = wc // 2
    halves = [pl.ds(h * hw, hw) for h in range(2)]
    g_mate = [remote(S["qs"].at[:, halves[h]], S["gz"].at[h], mate) for h in range(2)]
    for c in g_mate:
        c.start()

    ng_whole = jnp.concatenate([ng[k] for k in range(4)], axis=1)
    h_b = Halving("b", 0, S["p_b"])
    cols = []
    for k in range(4):
        back = dot_nt(
            ng_whole,
            jnp.concatenate([S["nin"][c, k * nc : (k + 1) * nc] for c in range(4)], axis=1),
        )
        cols.append((S["gb"][k].astype(F32) + back).astype(BF16))
    put_rows("b", dot_tn(wg[ch], jnp.concatenate(cols, axis=1)))
    on(h_conv[1])
    on(h_conv[2])
    h_b.start()
    h_in = Halving("in", 0, S["p_in"])
    qn1, q1 = sums_finish(fin)
    gsh, gzs = S["gsh"], S["gzs"]

    def row_shifts(dst, tile, cols, v):
        at = pl.ds(tile[0], tile[1])
        dst[1, at, cols] = shift_tile(v, tile, 0, 1).astype(BF16)
        v = shift_tile(v, tile, 1, 0)
        dst[2, at, cols] = v.astype(BF16)
        dst[3, at, cols] = shift_tile(v, tile, 0, 1).astype(BF16)

    for tile in g.tiles:
        at = pl.ds(tile[0], tile[1])
        v = grad_in(u[at], S["n1"][at], gain1, inv1, qn1, q1)
        gsh[0, at] = v.astype(BF16)
    for tile in g.tiles:
        at = pl.ds(tile[0], tile[1])
        row_shifts(gsh, tile, slice(0, wc), gsh[0, at].astype(F32))

    where = {tap: (tap, p, k) for tap, p, k in
             ((t, p, group_of(di, dj)) for p in PLANES for t, di, dj in plane_taps(p))}

    def split_job():
        pb = S["pb"]
        split = dot_nn(
            jnp.concatenate([wg[k] for k in range(4)], axis=1), S["ab"][...]
        )
        o_big[0] = split[:br, :nc].astype(BF16)
        o_small[0] = split[br:, :nc].astype(BF16)
        part = split[:, nc:].astype(BF16)
        pb[...] = part
        block = (part.astype(F32) + yb[:, 0:nc]).astype(BF16)
        o_big[1] = block[:br]
        o_small[1] = block[br:]

    def in_job():
        put_rows("in", dot_tn(S["pb"][...], jnp.concatenate([ng[k] for k in range(4)], axis=1)))
        h_in.start()

    taps = [(tap, p, group_of(di, dj)) for p in PLANES for tap, di, dj in plane_taps(p)]
    parts = [(tap, p, k, h) for h in range(2) for tap, p, k in taps]
    h_down = [
        Halving("down", i, S["g_down"].at[tap, :, halves[h]])
        for i, (tap, _, _, h) in enumerate(parts)
    ]

    def down_part(i):
        _, p, k, h = parts[i]
        mine = jnp.concatenate([xg[pbit, p], xg[pbit + 2, p]], axis=1)
        theirs = jnp.concatenate([S["xz"][0, p], S["xz"][1, p]], axis=1)
        cols = slice(h * hw, (h + 1) * hw)
        put("down", i, 0, dot_tn(mine, gsh[k, :, cols]) + dot_tn(theirs, gzs[k, :, cols]))
        h_down[i].start()

    cs, cr, cys, cyr = S["cs"], S["cr"], S["cys"], S["cyr"]
    cs_sem, cys_sem = shared(cs), shared(cys)
    c_sib = {
        p: [remote(cs.at[p, k], cr.at[p, k], (dp, sib), cs_sem) for k in range(2)] for p in PLANES
    }
    c_far = {p: remote(cys.at[p], cyr.at[p], (dp, yp), cys_sem) for p in PLANES}

    def crop_pair(p, d0, d1):
        part = None
        for tap, di, dj in plane_taps(p):
            w = jnp.concatenate(
                [wv[tap, pl.ds(d0 * cb, cb), :], wv[tap, pl.ds(d1 * cb, cb), :]], axis=0
            )
            res = dot_nt(gsh[group_of(di, dj)], w)
            part = res if part is None else part + res
        return part

    def crop_near(p):
        part = crop_pair(p, diag, sib).astype(BF16)
        cs[p, 0] = part[:, :cb]
        c_sib[p][0].start()
        cs[p, 1] = part[:, cb:]
        c_sib[p][1].start()

    def crop_own(p):
        acc[p] = crop_pair(p, yp, ch)

    def crop_send(p):
        c_sib[p][0].wait_recv()
        cys[p] = (acc[p, :, :cb] + cr[p, 0].astype(F32)).astype(BF16)
        c_far[p].start()
        c_sib[p][1].wait_recv()
        acc[p, :, cb:] += cr[p, 1].astype(F32)

    def crop_end(p):
        pr, pc = p // 2, p % 2
        c_far[p].wait_recv()
        v = acc[p, :, cb:] + cyr[p].astype(F32)
        o_gbig[:, pr, pl.ds(pc, g.hb, stride=2), :] = v[:br].reshape(-1, g.hb, cb)
        o_gsmall[:, pr, pl.ds(pc, g.hs, stride=2), :] = v[br:].reshape(-1, g.hs, cb)


    def job(kind, key=None):
        if kind == "d":
            down_part(key)
        elif kind == "near":
            crop_near(key)
        elif kind == "own":
            crop_own(key)
        elif kind == "send":
            crop_send(key)
        elif kind == "end":
            crop_end(key)
        elif kind == "wide":
            wide_g.forward()
            wide_g.near()
        else:
            wide_g.far()
            split_job()
            in_job()

    def receive(h):
        g_mate[h].wait_recv()
        cols = slice(h * hw, (h + 1) * hw)
        theirs = st[5, mate[0], :, cols] * (1.0 / R)
        scale = gain1[:, cols] * inv1[:, cols]
        shift = theirs[1:2] - q1[:, cols] * (1.0 / g.total_rows)
        slope = theirs[0:1] - qn1[:, cols] * (1.0 / g.total_rows)
        for tile in g.tiles:
            at = pl.ds(tile[0], tile[1])
            v = S["gz"][h, at].astype(F32) + shift + S["nz"][at, cols].astype(F32) * slope
            v = (scale * v).astype(BF16)
            gzs[0, at, cols] = v
            row_shifts(gzs, tile, cols, v.astype(F32))

    def both(*pairs):
        for i, *ready in pairs:
            job("d", i)
            for k in ready:
                on(k)

    job("near", 0)
    job("own", 0)
    job("near", 1)
    job("own", 1)
    n_mate[0].wait_recv()
    n_mate[1].wait_recv()
    job("send", 0)
    receive(0)
    cross_x.finish()
    both((0,), (1,), (2,))
    job("send", 1)
    both((3,), (4,))
    on(h_a)
    on(h_b)
    both((5,), (6, 0))
    job("wide")
    both((7, 1), (8, 2))
    job("near", 2)
    job("split")
    on(3)
    on(4)
    receive(1)
    both((9, 5), (10, 6), (11, 7))
    job("own", 2)
    job("send", 2)
    both((12, 8),)
    on(h_b)
    both((13,),)
    job("near", 3)
    on(h_in)
    on(9)
    both((14, 10), (15, 11))
    job("own", 3)
    on(h_a)
    both((16, 12), (17, 13))
    job("send", 3)
    on(h_in)
    on(14)
    on(15)
    on(h_b)
    on(16)
    on(17)
    on(h_in)
    for h in h_conv:
        on(h)
    job("end", 0)
    job("end", 1)
    for i in range(0, 9):
        on(i)
    job("end", 2)
    for i in range(9, 18):
        on(i)
    job("end", 3)
    for _ in range(bits_of(n)):
        for h in (*h_conv, h_a, h_b, h_in, *h_down):
            on(h)
    for d in deliveries:
        d.finish()
    for c in ld_m:
        c.wait()

    def sq(value):
        v = value * value
        while v.ndim > 2:
            v = jnp.sum(v, axis=0)
        v = jnp.sum(v, axis=0, keepdims=True)
        out = v[:, 0:128]
        for k in range(128, v.shape[1], 128):
            out = out + v[:, k : k + 128]
        return out

    grads = {
        "down": S["g_down"][...],
        "a": S["g_a"][...].astype(F32),
        "b": S["g_b"][...].astype(F32),
        "in": S["g_in"][...].astype(F32),
    }
    g_conv = S["g_conv"]
    layers = ("down", "a", "b", "in", "conv")
    nm = S["nm"]
    lane = lax.broadcasted_iota(jnp.int32, (1, 128), 1)
    mine = jnp.zeros((1, 128), F32)
    for i, name in enumerate(layers):
        weight = S["k_" + name][...].astype(F32)
        grad = g_conv[...] if name == "conv" else grads[name]
        mine = jnp.where(lane == i, jnp.sum(sq(weight), axis=1, keepdims=True), mine)
        mine = jnp.where(lane == 5 + i, jnp.sum(sq(grad), axis=1, keepdims=True), mine)
    place = nm.at[dp * 4 + ch]
    place[...] = mine
    ssem, rsem = sem(), sem()
    everyone(
        lambda peer: pltpu.make_async_remote_copy(
            src_ref=place, dst_ref=place, send_sem=ssem, recv_sem=rsem,
            device_id=peer, device_id_type=MESH,
        ).start()
    )
    some = nm.at[pl.ds(0, 4 * n - 1)]
    total(some, rsem).wait()
    total(some, ssem).wait()
    roots = jnp.sqrt(jnp.sum(nm[...], axis=0))
    norms = [jnp.sum(jnp.where(lane == k, roots, 0.0), axis=1, keepdims=True) for k in range(10)]
    row = lax.broadcasted_iota(jnp.int32, (2, 5), 0)
    col = lax.broadcasted_iota(jnp.int32, (2, 5), 1)
    table = jnp.zeros((2, 5), F32)
    for k in range(10):
        table = jnp.where((row == k // 5) & (col == k % 5), norms[k], table)
    o_ln[...] = table
    o_wn[0:1] = qn1
    o_wn[1:2] = q1
    o_nn[0, 0:1] = qn2
    o_nn[0, 1:2] = q2
    o_nn[1, 0:1] = qn3
    o_nn[1, 1:2] = q3

    def update(rate, weight, grad, moment):
        after = MOMENTUM * moment + rate * (grad + DECAY * weight)
        return weight - after, after

    for i, name in enumerate(layers):
        wnorm = norms[i]
        rate = TRUST * wnorm / (norms[5 + i] + DECAY * wnorm)
        o_new, o_next = {
            "down": (o_ndown, o_mdown), "a": (o_na, o_ma), "b": (o_nb, o_mb),
            "in": (o_nin, o_min), "conv": (o_nconv, o_mconv),
        }[name]
        if name == "down":
            for t in range(9):
                new, after = update(
                    rate, S["k_down"][t].astype(F32), S["g_down"][t], S["m_down"][t]
                )
                o_new[t] = new
                o_next[t] = after
        elif name == "conv":
            for t in range(9):
                new, after = update(
                    rate,
                    S["k_conv"][t].astype(F32),
                    g_conv[:, t * nc : (t + 1) * nc],
                    S["m_conv"][t],
                )
                o_new[t] = new
                o_next[t] = after
        else:
            new, after = update(rate, S["k_" + name][...].astype(F32), grads[name], S["m_" + name][...])
            o_new[...] = new
            o_next[...] = after
    for c in pending:
        c.wait_send()
    for c in drain:
        c.wait()
    assert used[0] == sems.shape[0], used[0]


def hand_over(*refs):
    count = len(refs) // 2
    copies = [
        pltpu.make_async_copy(refs[k], refs[count + k], refs[-1].at[k]) for k in range(count)
    ]
    for c in copies:
        c.start()
    for c in copies:
        c.wait()


def per_device(
    big_crops, small_crops, conv_down, split_a, split_b, neck_in, neck_conv, norm_wide, norm_neck,
    cot_big, cot_small, mom_down, mom_a, mom_b, mom_in, mom_conv,
):
    n = lax.axis_size("dp")
    g = Geometry(big_crops.shape, small_crops.shape, conv_down.shape, neck_conv.shape, n)

    def taps_first(w):
        return jnp.transpose(w, (1, 2, 0, 3)).reshape(9, w.shape[0], w.shape[3])

    def taps_back(w):
        return jnp.transpose(w.reshape(3, 3, w.shape[1], w.shape[2]), (2, 0, 1, 3))

    args = (
        big_crops.reshape(g.nb * g.hb * 2, 2 * g.hb, g.cb),
        small_crops.reshape(g.ns * g.hs * 2, 2 * g.hs, g.cb),
        taps_first(conv_down), split_a, split_b, neck_in, taps_first(neck_conv),
        norm_wide, norm_neck,
        cot_big.reshape(2, g.big_rows, g.nc), cot_small.reshape(2, g.small_rows, g.nc),
        taps_first(mom_down), mom_a, mom_b, mom_in, taps_first(mom_conv),
    )
    sds = jax.ShapeDtypeStruct
    up = [
        sds((9, g.ch // n, g.wc), F32), sds(mom_a.shape, F32), sds(mom_b.shape, F32),
        sds(mom_in.shape, F32), sds((9, g.ch // n, g.nc), F32),
    ]
    out_shape = [
        sds((2, g.big_rows, g.nc), BF16), sds((2, g.small_rows, g.nc), BF16),
        sds((g.nb * g.hb, 2, 2 * g.hb, g.cb), F32), sds((g.ns * g.hs, 2, 2 * g.hs, g.cb), F32),
        *up, *up,
        sds((2, g.wc), F32), sds((2, 2, g.nc), F32), sds((2, 5), F32),
    ]
    anywhere = pl.BlockSpec(memory_space=pl.ANY)
    vmem = pl.BlockSpec(memory_space=pltpu.VMEM)
    plan = scratch_plan(g)
    res = pl.pallas_call(
        functools.partial(mega, g, tuple(plan)),
        out_shape=[pltpu.VMEM(o.shape, o.dtype) for o in out_shape],
        in_specs=[anywhere] * 16,
        out_specs=[vmem] * 17,
        scratch_shapes=[pltpu.VMEM(shape, dtype) for shape, dtype in plan.values()]
        + [pltpu.SemaphoreType.DMA((count_sems(g),))],
        compiler_params=pltpu.CompilerParams(
            collective_id=0, has_side_effects=True, vmem_limit_bytes=58 * 2**20
        ),
    )(*args)
    res = pl.pallas_call(
        hand_over,
        out_shape=out_shape,
        in_specs=[anywhere] * 17,
        out_specs=[anywhere] * 17,
        scratch_shapes=[pltpu.SemaphoreType.DMA((17,))],
        compiler_params=pltpu.CompilerParams(vmem_limit_bytes=2**20),
    )(*res)
    res = list(res)
    res[0] = res[0].reshape(cot_big.shape)
    res[1] = res[1].reshape(cot_small.shape)
    res[2] = res[2].reshape(big_crops.shape)
    res[3] = res[3].reshape(small_crops.shape)
    for k in (4, 8, 9, 13):
        res[k] = taps_back(res[k])
    return tuple(res)


def solution(mesh):
    in_specs = (
        P("dp", None, None, "chan"),
        P("dp", None, None, "chan"),
        P(None, None, None, "chan"),
        P(None, "chan"),
        P(None, "chan"),
        P(None, "chan"),
        P(None, None, None, "chan"),
        P(),
        P(),
        P(None, "dp", None, None, "chan"),
        P(None, "dp", None, None, "chan"),
        P("dp", None, None, "chan"),
        P("dp", "chan"),
        P("dp", "chan"),
        P("dp", "chan"),
        P("dp", None, None, "chan"),
    )
    out_specs = (
        P(None, "dp", None, None, "chan"),
        P(None, "dp", None, None, "chan"),
        P("dp", None, None, "chan"),
        P("dp", None, None, "chan"),
        P("dp", None, None, "chan"),
        P("dp", "chan"),
        P("dp", "chan"),
        P("dp", "chan"),
        P("dp", None, None, "chan"),
        P("dp", None, None, "chan"),
        P("dp", "chan"),
        P("dp", "chan"),
        P("dp", "chan"),
        P("dp", None, None, "chan"),
        P(None, "chan"),
        P(None, None, "chan"),
        P(),
    )
    return jax.shard_map(
        per_device, mesh=mesh, in_specs=in_specs, out_specs=out_specs, check_vma=False
    )
```

```python
import functools

import jax
import jax.numpy as jnp
from jax import lax
from jax.experimental import pallas as pl
from jax.experimental.pallas import tpu as pltpu
from jax.sharding import PartitionSpec as P

EPSILON = 1e-05
MOMENTUM = 0.9
DECAY = 0.0005
TRUST = 0.1
F32 = jnp.float32
BF16 = jnp.bfloat16
MESH = pl.DeviceIdType.MESH
PLANES = (3, 1, 2, 0)


def dot_nn(left, right):
    return lax.dot_general(left, right, (((1,), (0,)), ((), ())), preferred_element_type=F32)


def dot_nt(left, right):
    return lax.dot_general(left, right, (((1,), (1,)), ((), ())), preferred_element_type=F32)


def dot_tn(left, right):
    return lax.dot_general(left, right, (((0,), (0,)), ((), ())), preferred_element_type=F32)


def mish_parts(v):
    u = jnp.exp(-jnp.abs(v))
    pos = v >= 0
    num = jnp.where(pos, 1.0 + 2.0 * u, u * (u + 2.0))
    rest = jnp.where(pos, 2.0 * u * u, 2.0)
    den = num + rest
    inv = 1.0 / den
    tangent = num * inv
    slope = tangent + v * (rest * (den + num) * inv * inv) * (jnp.where(pos, 1.0, u) / (1.0 + u))
    return v * tangent, slope


def plane_taps(p):
    rows = ((0, -1), (2, 0)) if p // 2 else ((1, 0),)
    cols = ((0, -1), (2, 0)) if p % 2 else ((1, 0),)
    return [(r * 3 + s, di, dj) for r, di in rows for s, dj in cols]


def group_of(di, dj):
    return (2 if di else 0) + (1 if dj else 0)


class Geometry:
    def __init__(self, big, small, down, neck, n_dp):
        self.nb, self.hb = big[0], big[1] // 2
        self.ns, self.hs = small[0], small[1] // 2
        self.cb = big[3]
        self.ch = down[0]
        self.wc = down[3]
        self.nc = neck[3]
        self.n = n_dp
        self.big_rows = self.nb * self.hb * self.hb
        self.small_rows = self.ns * self.hs * self.hs
        self.rows = self.big_rows + self.small_rows
        self.total_rows = self.rows * n_dp
        self.tiles = [
            (i * self.hb * self.hb, self.hb * self.hb, 1, self.hb) for i in range(self.nb)
        ] + [(self.big_rows, self.small_rows, self.ns, self.hs)]


def shift_tile(value, tile, di, dj):
    _, rows, images, side = tile
    cols = value.shape[-1]
    if di:
        v = value.reshape(images, side, side, cols)
        blank = jnp.zeros((images, 1, side, cols), value.dtype)
        if di < 0:
            v = jnp.concatenate([blank, v[:, :-1]], axis=1)
        else:
            v = jnp.concatenate([v[:, 1:], blank], axis=1)
        value = v.reshape(rows, cols)
    if dj:
        v = pltpu.roll(value, 1 if dj < 0 else rows - 1, 0).reshape(rows // side, side, cols)
        at = lax.broadcasted_iota(jnp.int32, (1, side, cols), 1)
        keep = at >= 1 if dj < 0 else at < side - 1
        value = jnp.where(keep, v, 0.0).reshape(rows, cols)
    return value


def bits_of(n):
    return n.bit_length() - 1


def halving_plan(order):
    left = sorted(order)
    plan = []
    for bit in order:
        at = left.index(bit)
        plan.append((bit, 1 << (len(left) - 1 - at), 1 << at))
        left.remove(bit)
    return plan


CONV_SPLIT = (3, 3, 3)


def pair_bit(n):
    return bits_of(n) - 2


def reductions(g):
    rows = g.ch // g.n
    bits = tuple(range(bits_of(g.n)))
    paired = tuple(bit for bit in bits if bit != pair_bit(g.n))
    return {
        "d2": (8, rows, g.wc, paired),
        "d1": (2, rows, g.wc // 2, paired),
        **{f"c{k}": (1, rows, t * g.nc, paired) for k, t in enumerate(CONV_SPLIT)},
        "a": (1, 2 * rows, g.nc, bits),
        "b": (1, 2 * rows, g.nc, bits),
        "in": (1, rows, g.nc, bits),
    }


def scratch_plan(g):
    n = g.n
    R = g.rows
    s = {}
    s["raw_big"] = ((g.nb * g.hb * 2, 2 * g.hb, g.cb), BF16)
    s["raw_small"] = ((g.ns * g.hs * 2, 2 * g.hs, g.cb), BF16)
    s["xg"] = ((4, 4, R, g.cb), BF16)
    s["wv"] = ((9, g.ch, g.wc), BF16)
    s["wn"] = ((g.ch, 9 * g.nc), BF16)
    s["ab"] = ((2 * g.ch, 2 * g.nc), BF16)
    s["nin"] = ((4, g.ch, g.nc), BF16)
    s["sar"] = ((4, g.wc, g.nc), BF16)
    s["sbr"] = ((4, g.wc, g.nc), BF16)
    s["cmat"] = ((4, g.wc, g.nc), BF16)
    s["pw"] = ((2, 4 * g.wc), F32)
    s["pn"] = ((2, 2, 4 * g.nc), F32)
    s["acc"] = ((4, R, g.wc), F32)
    s["n1"] = ((R, g.wc), F32)
    s["s1"] = ((R, g.wc), F32)
    s["wg"] = ((4, R, g.wc), BF16)
    for k in ("f", "b"):
        s["rs_send" + k] = ((2, R, g.nc), BF16)
        s["rs_recv" + k] = ((2, R, g.nc), BF16)
        s["rs_ys" + k] = ((R, g.nc), BF16)
        s["rs_yr" + k] = ((R, g.nc), BF16)
    s["rs_keep"] = ((2, R, g.nc), F32)
    s["n2"] = ((R, g.nc), F32)
    s["s2"] = ((R, g.nc), F32)
    s["fg"] = ((4, R, g.nc), BF16)
    s["yb"] = ((R, 9 * g.nc), F32)
    s["n3"] = ((R, g.nc), F32)
    s["s3"] = ((R, g.nc), F32)
    s["cg"] = ((R, 9 * g.nc), BF16)
    s["ga"] = ((4, R, g.nc), BF16)
    s["gb"] = ((4, R, g.nc), BF16)
    s["pb"] = ((R, g.nc), BF16)
    s["ng"] = ((4, R, g.nc), BF16)
    s["u"] = ((R, g.wc), F32)
    s["gsh"] = ((4, R, g.wc), BF16)
    s["cs"] = ((4, 2, R, g.cb), BF16)
    s["cr"] = ((4, 2, R, g.cb), BF16)
    s["cys"] = ((4, R, g.cb), BF16)
    s["cyr"] = ((4, R, g.cb), BF16)
    s["st"] = ((6, n, 2, g.wc), F32)
    s["nm"] = ((4 * n, 1, 128), F32)
    s["squares"] = ((1, 128), F32)
    for name, (count, rows, cols, order) in reductions(g).items():
        for stage, (_, high, low) in enumerate(halving_plan(order)):
            s[f"h_{name}_s{stage}"] = ((count, high, 2, low, rows, cols), BF16)
            s[f"h_{name}_r{stage}"] = ((count, high, low, rows, cols), BF16)
    s["xz"] = ((2, 4, R, g.cb), BF16)
    s["fz"] = ((2, R, g.nc), BF16)
    s["cz"] = ((R, g.nc), BF16)
    s["cgz"] = ((R, 9 * g.nc), BF16)
    s["gz"] = ((2, R, g.wc // 2), BF16)
    s["qs"] = ((R, g.wc), BF16)
    s["nb"] = ((R, g.wc), BF16)
    s["nz"] = ((R, g.wc), BF16)
    s["gzs"] = ((4, R, g.wc), BF16)
    s["g_down"] = ((9, g.ch // n, g.wc), F32)
    s["g_conv"] = ((g.ch // n, 9 * g.nc), F32)
    s["p_a"] = ((2 * g.ch // n, g.nc), BF16)
    s["p_b"] = ((2 * g.ch // n, g.nc), BF16)
    s["p_in"] = ((g.ch // n, g.nc), BF16)
    s["g_a"] = ((2 * g.ch // n, g.nc), BF16)
    s["g_b"] = ((2 * g.ch // n, g.nc), BF16)
    s["g_in"] = ((g.ch // n, g.nc), BF16)
    s["m_down"] = ((9, g.ch // n, g.wc), F32)
    s["m_a"] = ((2 * g.ch // n, g.nc), F32)
    s["m_b"] = ((2 * g.ch // n, g.nc), F32)
    s["m_in"] = ((g.ch // n, g.nc), F32)
    s["m_conv"] = ((9, g.ch // n, g.nc), F32)
    s["k_down"] = ((9, g.ch // n, g.wc), BF16)
    s["k_a"] = ((2 * g.ch // n, g.nc), BF16)
    s["k_b"] = ((2 * g.ch // n, g.nc), BF16)
    s["k_in"] = ((g.ch // n, g.nc), BF16)
    s["k_conv"] = ((9, g.ch // n, g.nc), BF16)
    return s


def count_sems(g):
    early = [1 + len(order) for name, (_, _, _, order) in reductions(g).items() if name[0] != "d"]
    return BASE_SEMS + sum(early) + 40 * (bits_of(g.n) - 3)


BASE_SEMS = 96


def mega(g, names, *refs):
    (
        big, small, w_down, w_a, w_b, w_in, w_conv, p_wide, p_neck, c_big, c_small,
        m_down, m_a, m_b, m_in, m_conv,
    ) = refs[:16]
    (
        o_big, o_small, o_gbig, o_gsmall, o_ndown, o_na, o_nb, o_nin, o_nconv,
        o_mdown, o_ma, o_mb, o_min, o_mconv, o_wn, o_nn, o_ln,
    ) = refs[16:33]
    S = dict(zip(names, refs[33:-1], strict=True))
    sems = refs[-1]
    n, R, nc, wc, cb = g.n, g.rows, g.nc, g.wc, g.cb
    dp = lax.axis_index("dp")
    ch = lax.axis_index("chan")
    core = lax.rem(ch, 2)
    half = lax.div(ch, 2)
    sib = half * 2 + (1 - core)
    yp = (1 - half) * 2 + core
    diag = (1 - half) * 2 + (1 - core)
    other = 1 - half

    pair = pair_bit(n)
    pbit = lax.rem(lax.div(dp, 1 << pair), 2)
    mate = (dp + (1 - 2 * pbit) * (1 << pair), ch)
    gives = core != pbit
    takes = core == pbit

    used = [0]
    pending = []
    drain = []

    free = []

    def sem():
        if free:
            return free.pop()
        used[0] += 1
        return sems.at[used[0] - 1]

    load_sems = []

    def local(src, dst, own=None):
        if own is None:
            own = sem()
            load_sems.append(own)
        copy = pltpu.make_async_copy(src, dst, own)
        copy.start()
        return copy

    def remote(src, dst, device, ssem=None, rsem=None):
        copy = pltpu.make_async_remote_copy(
            src_ref=src, dst_ref=dst,
            send_sem=sem() if ssem is None else ssem,
            recv_sem=sem() if rsem is None else rsem,
            device_id=device, device_id_type=MESH,
        )
        if ssem is None:
            pending.append(copy)
        return copy

    def total(view, one):
        return pltpu.make_async_copy(view, view, one)

    def shared(view):
        one = sem()
        drain.append(total(view, one))
        return one
    ld_big = local(big, S["raw_big"])
    ld_small = local(small, S["raw_small"])
    ld_wv = local(w_down, S["wv"])
    ab_sem, wn_sem, ga_sem, gb_sem = sem(), sem(), sem(), sem()
    local(w_a, S["ab"].at[:, pl.ds(0, nc)], ab_sem)
    local(w_b, S["ab"].at[:, pl.ds(nc, nc)], ab_sem)
    ld_ab = total(S["ab"], ab_sem)
    ld_in = local(w_in, S["nin"].at[ch])
    ld_p = [local(p_wide, S["pw"]), local(p_neck, S["pn"])]
    for t in range(9):
        local(w_conv.at[t], S["wn"].at[:, pl.ds(t * nc, nc)], wn_sem)
    ld_wn = total(S["wn"], wn_sem)
    br, sr = g.big_rows, g.small_rows
    ld_c = []
    for k, name, one in ((0, "ga", ga_sem), (1, "gb", gb_sem)):
        local(c_big.at[k], S[name].at[ch, pl.ds(0, br)], one)
        local(c_small.at[k], S[name].at[ch, pl.ds(br, sr)], one)
        ld_c.append(total(S[name].at[ch], one))
    bar = pltpu.get_barrier_semaphore()

    def everyone(act):
        def one(k):
            act((lax.rem(dp + lax.div(k, 4), n), lax.rem(ch + lax.rem(k, 4), 4)))

        if n <= 8:
            for k in range(1, 4 * n):
                one(k)
        else:
            lax.fori_loop(1, 4 * n, lambda k, c: (one(k), c)[1], 0)

    bits = [lax.rem(lax.div(dp, 1 << i), 2) for i in range(bits_of(n))]
    dp_peers = [
        sum(((1 - b) if k >> i & 1 else b) * (1 << i) for i, b in enumerate(bits))
        for k in range(n - 1, 0, -1)
    ]
    peers = [(dp, yp), (dp, sib), (dp, diag)] + [(peer, ch) for peer in dp_peers]
    for peer in peers:
        pl.semaphore_signal(bar, inc=1, device_id=peer, device_id_type=MESH)
    xg = S["xg"]
    ld_big.wait()
    o_gbig[...] = S["raw_big"][...].astype(F32).reshape(o_gbig.shape)
    ld_small.wait()
    o_gsmall[...] = S["raw_small"][...].astype(F32).reshape(o_gsmall.shape)

    def split_plane(p):
        pr, pc = p // 2, p % 2
        xg[ch, p, 0:br] = (
            o_gbig[:, pr, pl.ds(pc, g.hb, stride=2), :].reshape(br, cb).astype(BF16)
        )
        xg[ch, p, br:R] = (
            o_gsmall[:, pr, pl.ds(pc, g.hs, stride=2), :].reshape(sr, cb).astype(BF16)
        )

    class Gather:
        def __init__(self, ref, plane=None, ssems=None, rows=None):
            def block(c):
                if rows is not None:
                    return ref.at[c, rows]
                return ref.at[c] if plane is None else ref.at[c, plane]

            if ssems is None:
                three = ref.at[pl.ds(0, 3)] if rows is None else ref.at[pl.ds(0, 3), rows]
                ssems = [shared(three)] * 3
            self.to_sib = remote(block(ch), block(ch), (dp, sib), ssems[0])
            self.to_far = remote(block(ch), block(ch), (dp, yp), ssems[1])
            self.onward = remote(block(yp), block(yp), (dp, sib), ssems[2])

        def start(self):
            self.to_sib.start()
            self.to_far.start()

        def forward(self):
            self.to_far.wait_recv()
            self.onward.start()

        def near(self):
            self.to_sib.wait_recv()

        def far(self):
            self.onward.wait_recv()

    crop_sems = [shared(xg.at[0]) for _ in range(3)]
    crops = {p: Gather(xg, p, crop_sems) for p in PLANES}
    split_plane(PLANES[0])
    pl.semaphore_wait(bar, len(peers))
    upper, lower = pl.ds(0, R // 2), pl.ds(R // 2, R // 2)

    class Cross:
        def __init__(self, buf, source):
            self.buf, self.source = S[buf], source
            self.ssem, self.rsem = shared(self.buf), sem()
            self.arrived = total(self.buf, self.rsem)
            self.onward = remote(self.buf, self.buf, (dp, sib), self.ssem, self.rsem)

        def send(self, block, h, *plane):
            @pl.when(gives)
            def _():
                remote(
                    self.source.at[(block, *plane)], self.buf.at[(h, *plane)], mate,
                    self.ssem, self.rsem,
                ).start()

        def hand_on(self):
            @pl.when(takes)
            def _():
                self.arrived.wait()
                self.onward.start()

        def finish(self):
            @pl.when(gives)
            def _():
                self.arrived.wait()

    cross_x = Cross("xz", xg)
    crops[PLANES[0]].start()
    cross_x.send(ch, half, PLANES[0])
    for p in PLANES[1:]:
        split_plane(p)
        crops[p].start()
        cross_x.send(ch, half, p)
    ld_in.wait()
    neck_in = Gather(S["nin"])
    ld_ab.wait()

    class Rows:
        def __init__(self, buf, lane):
            ref = S[buf]
            ssem, rsem = shared(ref.at[pl.ds(0, 3)]), sem()
            self.copies = [
                remote(
                    S["ab"].at[pl.ds(dev * wc, wc), pl.ds(lane, nc)], ref.at[ch], (dp, dev),
                    ssem, rsem,
                )
                for dev in (yp, diag, sib)
            ]
            self.arrived = total(ref.at[pl.ds(0, 3)], rsem)
            ref[ch] = S["ab"][pl.ds(ch * wc, wc), lane : lane + nc]

        def start(self):
            for c in self.copies:
                c.start()

        def wait(self):
            self.arrived.wait()

    b_rows = Rows("sbr", nc)
    a_rows = Rows("sar", 0)
    b_rows.start()
    neck_in.start()
    ld_wv.wait()
    wv, acc = S["wv"], S["acc"]

    def conv_part(side, p, first):
        x = jnp.concatenate([xg[2 * side, p], xg[2 * side + 1, p]], axis=1)
        for tap, di, dj in plane_taps(p):
            res = dot_nn(x, wv[tap, pl.ds(side * 2 * cb, 2 * cb), :])
            k = group_of(di, dj)
            if first:
                acc[k] = res
            else:
                acc[k] += res
    for p in PLANES:
        crops[p].near()
        conv_part(half, p, p == PLANES[0])
    for p in PLANES[:-1]:
        crops[p].forward()
        cross_x.send(yp, other, p)
        crops[p].far()
        conv_part(other, p, False)
    for tile in g.tiles:
        at = pl.ds(tile[0], tile[1])
        inner = acc[1, at] + shift_tile(acc[3, at], tile, -1, 0)
        acc[2, at] = shift_tile(acc[2, at], tile, -1, 0) + shift_tile(inner, tile, 0, -1)
    p = PLANES[-1]
    crops[p].forward()
    cross_x.send(yp, other, p)
    crops[p].far()
    conv_part(other, p, False)
    acc[0] = acc[0] + acc[2]

    st = S["st"]
    st_send, st_recv = sem(), [sem(), sem()]

    def exchange(phase, first, second, cols):
        st[phase, dp, 0:1, 0:cols] = first
        st[phase, dp, 1:2, 0:cols] = second
        ssem, rsem = st_send, st_recv[phase % 2]
        mine = st.at[phase, dp, :, pl.ds(0, cols)]
        for peer in dp_peers:
            pltpu.make_async_remote_copy(
                src_ref=mine, dst_ref=mine, send_sem=ssem, recv_sem=rsem,
                device_id=(peer, ch), device_id_type=MESH,
            ).start()
        some = st.at[phase, pl.ds(0, n - 1), :, pl.ds(0, cols)]

        def finish():
            total(some, rsem).wait()
            total(some, ssem).wait()
            return st[phase, :, :, 0:cols]

        return finish

    def norm_start(phase, ref):
        cols = ref.shape[-1]
        mean = jnp.sum(ref[...], axis=0, keepdims=True) * (1.0 / R)
        dev = ref[...] - mean
        return exchange(phase, mean, jnp.sum(dev * dev, axis=0, keepdims=True), cols)

    def norm_finish(finish):
        v = finish()
        tot = jnp.sum(v, axis=0)
        mean = tot[0:1] * (1.0 / n)
        off = v - mean[None]
        spread = jnp.sum(off * off, axis=0)[0:1]
        var = (tot[1:2] + R * spread) * (1.0 / g.total_rows)
        return mean, lax.rsqrt(var + EPSILON)

    def sums_finish(finish):
        tot = jnp.sum(finish(), axis=0)
        return tot[0:1], tot[1:2]
    fin = norm_start(0, acc.at[0])
    for c in ld_p:
        c.wait()
    gain1 = S["pw"][0:1, pl.ds(ch * wc, wc)]
    bias1 = S["pw"][1:2, pl.ds(ch * wc, wc)]
    neck_in.forward()
    neck_in.near()
    neck_in.far()
    b_rows.wait()
    rows_b = jnp.concatenate([S["sbr"][k] for k in range(4)], axis=1)
    for k in range(4):
        S["cmat"][k] = dot_nn(rows_b, S["nin"][k]).astype(BF16)
    mean1, inv1 = norm_finish(fin)
    wg = S["wg"]
    for t0 in range(0, R, 256):
        at = pl.ds(t0, 256)
        normed = (acc[0, at] - mean1) * inv1
        S["n1"][at] = normed
        S["nb"][at] = normed.astype(BF16)
        wg[ch, at] = mish_parts(normed * gain1 + bias1)[0].astype(BF16)

    summed = []

    def reduce_chan(k, pair):
        send, recv = S["rs_send" + k], S["rs_recv" + k]
        ys, yr, keep = S["rs_ys" + k], S["rs_yr" + k], S["rs_keep"]
        parts = [pl.ds(0, R // 2), pl.ds(R // 2, R // 2)]
        s0, sy, r1 = shared(send), shared(ys), sem()
        summed.append(r1)
        c0 = [remote(send.at[0, at], recv.at[0, at], (dp, sib), s0) for at in parts]
        c1 = [remote(send.at[1, at], recv.at[1, at], (dp, sib), s0, r1) for at in parts]
        cy = [remote(ys.at[at], yr.at[at], (dp, yp), sy) for at in parts]
        summed.extend(c.dst_sem for c in (*c0, *cy))
        for at, far, near in zip(parts, c0, c1, strict=True):
            part = pair(at, diag, sib).astype(BF16)
            send[0, at] = part[:, :nc]
            far.start()
            send[1, at] = part[:, nc:]
            near.start()
        for at, near, far in zip(parts, c0, cy, strict=True):
            part = pair(at, yp, ch)
            keep[1, at] = part[:, nc:]
            near.wait_recv()
            ys[at] = (part[:, :nc] + recv[0, at].astype(F32)).astype(BF16)
            far.start()
        total(recv.at[1], r1).wait()
        keep[1] += recv[1].astype(F32)

        def finish():
            for at, far in zip(parts, cy, strict=True):
                far.wait_recv()
                keep[1, at] += yr[at].astype(F32)

        return finish

    def neck_pair(at, d0, d1):
        return dot_nn(
            wg[ch, at], jnp.concatenate([S["cmat"][d0], S["cmat"][d1]], axis=1)
        )
    n_mate = [remote(S["nb"].at[at], S["nz"].at[at], mate) for at in (upper, lower)]
    n_mate[0].start()
    rs_fin = reduce_chan("f", neck_pair)
    for c in ld_c:
        c.wait()
    gb_g = Gather(S["gb"])
    ga_g = Gather(S["ga"])
    wide_g = Gather(wg)
    cross_x.hand_on()
    for t0 in range(0, R, 256):
        at = pl.ds(t0, 256)
        S["s1"][at] = mish_parts(S["n1"][at] * gain1 + bias1)[1]
    rs_fin()
    a_rows.start()
    z2 = S["rs_keep"].at[1]
    fin = norm_start(1, z2)
    n_mate[1].start()
    gain2 = S["pn"][0, 0:1, pl.ds(ch * nc, nc)]
    bias2 = S["pn"][0, 1:2, pl.ds(ch * nc, nc)]
    gain3 = S["pn"][1, 0:1, pl.ds(ch * nc, nc)]
    bias3 = S["pn"][1, 1:2, pl.ds(ch * nc, nc)]
    mean2, inv2 = norm_finish(fin)
    fg = S["fg"]
    for t0 in range(0, R, 256):
        at = pl.ds(t0, 256)
        normed = (z2[at] - mean2) * inv2
        S["n2"][at] = normed
        fg[ch, at] = mish_parts(normed * gain2 + bias2)[0].astype(BF16)
    first_g = Gather(fg)
    first_g.start()
    ld_wn.wait()
    wn, yb = S["wn"], S["yb"]

    def neck_part(side, first):
        x = jnp.concatenate([fg[2 * side], fg[2 * side + 1]], axis=1)
        w = wn[pl.ds(side * 2 * nc, 2 * nc), :]
        if first:
            yb[...] = dot_nn(x, w)
        else:
            yb[...] += dot_nn(x, w)

    first_g.near()
    neck_part(half, True)
    for t0 in range(0, R, 256):
        at = pl.ds(t0, 256)
        S["s2"][at] = mish_parts(S["n2"][at] * gain2 + bias2)[1]
    first_g.forward()
    first_g.far()
    gb_g.start()
    ga_g.start()
    neck_part(other, False)
    z3 = S["n3"]
    for tile in g.tiles:
        at = pl.ds(tile[0], tile[1])
        cols = []
        for s in range(3):
            cols.append(
                yb[at, (3 + s) * nc : (4 + s) * nc]
                + shift_tile(yb[at, s * nc : (s + 1) * nc], tile, -1, 0)
                + shift_tile(yb[at, (6 + s) * nc : (7 + s) * nc], tile, 1, 0)
            )
        z3[at] = (
            cols[1] + shift_tile(cols[0], tile, 0, -1) + shift_tile(cols[2], tile, 0, 1)
        )
    fin = norm_start(2, z3)
    cross_f = Cross("fz", fg)
    cross_f.send(ch, half)
    cross_f.send(yp, other)
    mean3, inv3 = norm_finish(fin)
    q_tot = jnp.zeros((1, nc), F32)
    qn_tot = jnp.zeros((1, nc), F32)
    for t0 in range(0, R, 256):
        at = pl.ds(t0, 256)
        normed = (z3[at] - mean3) * inv3
        slope = mish_parts(normed * gain3 + bias3)[1]
        q = S["gb"][ch, at].astype(F32) * slope
        z3[at] = normed
        S["s3"][at] = q
        q_tot += jnp.sum(q, axis=0, keepdims=True)
        qn_tot += jnp.sum(q * normed, axis=0, keepdims=True)
    fin = exchange(3, qn_tot, q_tot, nc)

    def grad_in(q, normed, gain, inv, qn_sum, q_sum):
        return gain * inv * (
            q - q_sum * (1.0 / g.total_rows) - normed * (qn_sum * (1.0 / g.total_rows))
        )

    stage_sems = {}
    plans = reductions(g)

    class Halving:
        def __init__(self, name, item, *results):
            self.name, self.item, self.results = name, item, results
            self.plan = halving_plan(plans[name][3])
            self.copies = []
            self.alone = S[f"h_{name}_s0"].shape[0] == 1
            if name not in stage_sems:
                stages = range(len(self.plan))
                stage_sems[name] = (
                    [sem()] * len(self.plan)
                    if self.alone
                    else [shared(S[f"h_{name}_s{i}"].at[:, :, 0]) for i in stages]
                )
            for i, (bit, high, low) in enumerate(self.plan):
                own = lax.rem(lax.div(dp, 1 << bit), 2)
                peer = dp + (1 - 2 * own) * (1 << bit)
                send = S[f"h_{name}_s{i}"]
                recv = S[f"h_{name}_r{i}"]
                self.copies.append(
                    remote(
                        send.at[item, :, 1 - own], recv.at[item], (peer, ch), stage_sems[name][i]
                    )
                )

        def start(self, stage=0):
            self.copies[stage].start()

        def step(self, stage):
            bit, high, low = self.plan[stage]
            own = lax.rem(lax.div(dp, 1 << bit), 2)
            send = S[f"h_{self.name}_s{stage}"]
            recv = S[f"h_{self.name}_r{stage}"]
            self.copies[stage].wait_recv()
            if self.alone:
                self.copies[stage].wait_send()
            both = send[self.item, :, own].astype(F32) + recv[self.item].astype(F32)
            if stage + 1 < len(self.plan):
                after = S[f"h_{self.name}_s{stage + 1}"]
                after[self.item] = both.astype(BF16).reshape(after.shape[1:])
                self.start(stage + 1)
            else:
                width = self.results[0].shape[-1]
                for k, ref in enumerate(self.results):
                    ref[...] = both[0, 0, :, k * width : (k + 1) * width].astype(ref.dtype)

    def put_rows(name, value):
        ref = S[f"h_{name}_s0"]
        _, high, _, low, rows, cols = ref.shape
        value = value.astype(BF16)
        for e in range(n):
            r, c = e % (n // 4), e // (n // 4)
            ref[0, e // (2 * low), e // low % 2, e % low] = value[
                r * rows : (r + 1) * rows, c * cols : (c + 1) * cols
            ]

    quarter = n // 4
    at_home = lax.div(dp, quarter) == ch

    class Deliver:
        def __init__(self, name):
            self.src, self.dst = S[f"p_{name}"], S[f"g_{name}"]
            target = (ch * quarter + lax.rem(dp, quarter), lax.div(dp, quarter))
            self.copy = pltpu.make_async_remote_copy(
                src_ref=self.src, dst_ref=self.dst, send_sem=sem(), recv_sem=sem(),
                device_id=target, device_id_type=MESH,
            )

        def start(self):
            @pl.when(at_home)
            def _():
                self.dst[...] = self.src[...]

            @pl.when(jnp.logical_not(at_home))
            def _():
                self.copy.start()

        def finish(self):
            @pl.when(jnp.logical_not(at_home))
            def _():
                self.copy.wait_recv()
                self.copy.wait_send()

    def put(name, item, first_block, value):
        ref = S[f"h_{name}_s0"]
        _, high, _, low, rows, cols = ref.shape
        at = first_block // (2 * low)
        count = value.shape[0] // (rows * 2 * low)
        ref[item, at : at + count] = value.astype(BF16).reshape(count, 2, low, rows, cols)

    for t0 in range(0, R, 256):
        at = pl.ds(t0, 256)
        yb[at, 0:nc] = mish_parts(z3[at] * gain3 + bias3)[0]
    gb_g.forward()
    gb_g.near()
    gb_g.far()
    u = S["u"]
    u[...] = dot_nt(
        jnp.concatenate([S["gb"][k] for k in range(4)], axis=1),
        jnp.concatenate([S["sbr"][k] for k in range(4)], axis=1),
    )
    qn3, q3 = sums_finish(fin)
    cg = S["cg"]

    def tap_shifts(dst, tile, v):
        at = pl.ds(tile[0], tile[1])
        for r in range(3):
            vi = shift_tile(v, tile, 1 - r, 0)
            for s in range(3):
                t = r * 3 + s
                dst[at, t * nc : (t + 1) * nc] = shift_tile(vi, tile, 0, 1 - s).astype(BF16)

    for tile in g.tiles:
        at = pl.ds(tile[0], tile[1])
        v = grad_in(S["s3"][at], z3[at], gain3, inv3, qn3, q3)
        tap_shifts(cg, tile, v.astype(BF16).astype(F32))
    to_mate = remote(cg.at[:, pl.ds(4 * nc, nc)], S["cz"], mate)
    to_mate.start()

    rows = g.ch // n
    reuse = [*load_sems, ab_sem, wn_sem, ga_sem, gb_sem]
    ld_m = [
        local(src, S[name], one)
        for (src, name), one in zip(
            (
                (m_down, "m_down"), (m_a, "m_a"), (m_b, "m_b"), (m_in, "m_in"),
                (m_conv, "m_conv"),
                (w_down.at[:, pl.ds(dp * rows, rows)], "k_down"),
                (w_a.at[pl.ds(dp * 2 * rows, 2 * rows)], "k_a"),
                (w_b.at[pl.ds(dp * 2 * rows, 2 * rows)], "k_b"),
                (w_in.at[pl.ds(dp * rows, rows)], "k_in"),
                (w_conv.at[:, pl.ds(dp * rows, rows)], "k_conv"),
            ),
            reuse,
            strict=True,
        )
    ]

    def back_pair(at, d0, d1):
        w = jnp.concatenate([wn[pl.ds(d0 * nc, nc), :], wn[pl.ds(d1 * nc, nc), :]], axis=0)
        return dot_nt(cg[at], w)
    rs_fin = reduce_chan("b", back_pair)
    ga_g.forward()
    ga_g.near()
    ga_g.far()
    a_rows.wait()
    u[...] += dot_nt(
        jnp.concatenate([S["ga"][k] for k in range(4)], axis=1),
        jnp.concatenate([S["sar"][k] for k in range(4)], axis=1),
    )
    h_a = Halving("a", 0, S["p_a"])
    put_rows("a", dot_tn(wg[ch], jnp.concatenate([S["ga"][k] for k in range(4)], axis=1)))
    deliveries = []
    done = {}

    def on(what):
        h = h_down[what] if isinstance(what, int) else what
        stage = done.setdefault((h.name, h.item), 0)
        if stage >= len(h.plan):
            return
        h.step(stage)
        done[h.name, h.item] += 1
        if h.name in ("a", "b", "in") and stage == len(h.plan) - 1:
            deliveries.append(Deliver(h.name))
            deliveries[-1].start()

    starts = [sum(CONV_SPLIT[:k]) * nc for k in range(len(CONV_SPLIT) + 1)]
    h_conv = [
        Halving(f"c{k}", 0, S["g_conv"].at[:, pl.ds(starts[k], starts[k + 1] - starts[k])])
        for k in range(len(CONV_SPLIT))
    ]
    def sq(value):
        v = value * value
        while v.ndim > 2:
            v = jnp.sum(v, axis=0)
        v = jnp.sum(v, axis=0, keepdims=True)
        out = v[:, 0:128]
        for k in range(128, v.shape[1], 128):
            out = out + v[:, k : k + 128]
        return out

    layers = ("down", "a", "b", "in", "conv")
    lane = lax.broadcasted_iota(jnp.int32, (1, 128), 1)

    def add_square(i, value):
        total_sq = jnp.sum(sq(value), axis=1, keepdims=True)
        S["squares"][...] = jnp.where(lane == i, total_sq, S["squares"][...])

    S["squares"][...] = jnp.zeros((1, 128), F32)
    for c in ld_m:
        c.wait()
    for i, name in enumerate(layers):
        add_square(i, S["k_" + name][...].astype(F32))
    rs_fin()
    q_tot = jnp.zeros((1, nc), F32)
    qn_tot = jnp.zeros((1, nc), F32)
    q2r = S["rs_keep"].at[1]
    for t0 in range(0, R, 256):
        at = pl.ds(t0, 256)
        q = q2r[at] * S["s2"][at]
        q2r[at] = q
        q_tot += jnp.sum(q, axis=0, keepdims=True)
        qn_tot += jnp.sum(q * S["n2"][at], axis=0, keepdims=True)
    fin = exchange(4, qn_tot, q_tot, nc)
    h_a.start()
    cross_f.hand_on()
    to_mate.wait_recv()
    for tile in g.tiles:
        tap_shifts(S["cgz"], tile, S["cz"][pl.ds(tile[0], tile[1])].astype(F32))
    cross_f.finish()
    mine = jnp.concatenate([fg[pbit], fg[pbit + 2]], axis=1)
    theirs = jnp.concatenate([S["fz"][0], S["fz"][1]], axis=1)
    for k, h in enumerate(h_conv):
        cols = slice(starts[k], starts[k + 1])
        put(h.name, 0, 0, dot_tn(mine, cg[:, cols]) + dot_tn(theirs, S["cgz"][:, cols]))
        h.start()
    qn2, q2 = sums_finish(fin)
    ng = S["ng"]
    for t0 in range(0, R, 256):
        at = pl.ds(t0, 256)
        ng[ch, at] = grad_in(q2r[at], S["n2"][at], gain2, inv2, qn2, q2).astype(BF16)
    neck_g = Gather(ng)
    neck_g.start()
    def wide_part(side):
        return dot_nt(
            jnp.concatenate([ng[2 * side], ng[2 * side + 1]], axis=1),
            jnp.concatenate([S["cmat"][2 * side], S["cmat"][2 * side + 1]], axis=1),
        )
    neck_g.near()
    u[...] += wide_part(half)
    on(h_a)
    on(h_conv[0])
    neck_g.forward()
    neck_g.far()
    wide_g.start()
    u[...] += wide_part(other)
    q_tot = jnp.zeros((1, wc), F32)
    qn_tot = jnp.zeros((1, wc), F32)
    for t0 in range(0, R, 256):
        at = pl.ds(t0, 256)
        q = u[at] * S["s1"][at]
        u[at] = q
        q_tot += jnp.sum(q, axis=0, keepdims=True)
        qn_tot += jnp.sum(q * S["n1"][at], axis=0, keepdims=True)
    fin = exchange(5, qn_tot, q_tot, wc)
    for t0 in range(0, R, 256):
        at = pl.ds(t0, 256)
        S["qs"][at] = (u[at] - q_tot * (1.0 / R) - S["n1"][at] * (qn_tot * (1.0 / R))).astype(BF16)
    hw = wc // 2
    halves = [pl.ds(h * hw, hw) for h in range(2)]
    g_mate = [remote(S["qs"].at[:, halves[h]], S["gz"].at[h], mate) for h in range(2)]
    for c in g_mate:
        c.start()

    ng_whole = jnp.concatenate([ng[k] for k in range(4)], axis=1)
    h_b = Halving("b", 0, S["p_b"])
    cols = []
    for k in range(4):
        back = dot_nt(
            ng_whole,
            jnp.concatenate([S["nin"][c, k * nc : (k + 1) * nc] for c in range(4)], axis=1),
        )
        cols.append((S["gb"][k].astype(F32) + back).astype(BF16))
    put_rows("b", dot_tn(wg[ch], jnp.concatenate(cols, axis=1)))
    on(h_conv[1])
    on(h_conv[2])
    h_b.start()
    h_in = Halving("in", 0, S["p_in"])
    qn1, q1 = sums_finish(fin)
    gsh, gzs = S["gsh"], S["gzs"]

    for one in (*crops.values(), neck_in, first_g, gb_g, ga_g):
        free.extend((one.to_sib.dst_sem, one.to_far.dst_sem, one.onward.dst_sem))
    free.extend(summed)

    def row_shifts(dst, tile, cols, v):
        at = pl.ds(tile[0], tile[1])
        dst[1, at, cols] = shift_tile(v, tile, 0, 1).astype(BF16)
        v = shift_tile(v, tile, 1, 0)
        dst[2, at, cols] = v.astype(BF16)
        dst[3, at, cols] = shift_tile(v, tile, 0, 1).astype(BF16)

    for tile in g.tiles:
        at = pl.ds(tile[0], tile[1])
        v = grad_in(u[at], S["n1"][at], gain1, inv1, qn1, q1)
        gsh[0, at] = v.astype(BF16)
    for tile in g.tiles:
        at = pl.ds(tile[0], tile[1])
        row_shifts(gsh, tile, slice(0, wc), gsh[0, at].astype(F32))

    where = {tap: (tap, p, k) for tap, p, k in
             ((t, p, group_of(di, dj)) for p in PLANES for t, di, dj in plane_taps(p))}

    def split_job():
        pb = S["pb"]
        split = dot_nn(
            jnp.concatenate([wg[k] for k in range(4)], axis=1), S["ab"][...]
        )
        o_big[0] = split[:br, :nc].astype(BF16)
        o_small[0] = split[br:, :nc].astype(BF16)
        part = split[:, nc:].astype(BF16)
        pb[...] = part
        block = (part.astype(F32) + yb[:, 0:nc]).astype(BF16)
        o_big[1] = block[:br]
        o_small[1] = block[br:]

    def in_job():
        put_rows("in", dot_tn(S["pb"][...], jnp.concatenate([ng[k] for k in range(4)], axis=1)))
        h_in.start()

    taps = [(tap, p, group_of(di, dj)) for p in PLANES for tap, di, dj in plane_taps(p)]
    parts = []
    for h in range(2):
        for p in PLANES:
            of_plane = [(tap, k) for tap, q, k in taps if q == p]
            parts += [(h, p, of_plane[i : i + 2]) for i in range(0, len(of_plane), 2)]
    h_down = []
    counts = {1: 0, 2: 0}
    for h, p, two in parts:
        results = [S["g_down"].at[tap, :, halves[h]] for tap, _ in two]
        h_down.append(Halving(f"d{len(two)}", counts[len(two)], *results))
        counts[len(two)] += 1

    def down_part(i):
        h, p, two = parts[i]
        mine = jnp.concatenate([xg[pbit, p], xg[pbit + 2, p]], axis=1)
        theirs = jnp.concatenate([S["xz"][0, p], S["xz"][1, p]], axis=1)
        cols = slice(h * hw, (h + 1) * hw)
        own = jnp.concatenate([gsh[k, :, cols] for _, k in two], axis=1)
        far = jnp.concatenate([gzs[k, :, cols] for _, k in two], axis=1)
        put(h_down[i].name, h_down[i].item, 0, dot_tn(mine, own) + dot_tn(theirs, far))
        h_down[i].start()

    cs, cr, cys, cyr = S["cs"], S["cr"], S["cys"], S["cyr"]
    cs_sem, cys_sem = shared(cs), shared(cys)
    c_sib = {
        p: [remote(cs.at[p, k], cr.at[p, k], (dp, sib), cs_sem) for k in range(2)] for p in PLANES
    }
    c_far = {p: remote(cys.at[p], cyr.at[p], (dp, yp), cys_sem) for p in PLANES}

    def crop_pair(p, d0, d1):
        left, right = [], []
        for tap, di, dj in plane_taps(p):
            left.append(gsh[group_of(di, dj)])
            right.append(
                jnp.concatenate(
                    [wv[tap, pl.ds(d0 * cb, cb), :], wv[tap, pl.ds(d1 * cb, cb), :]], axis=0
                )
            )
        return dot_nt(jnp.concatenate(left, axis=1), jnp.concatenate(right, axis=1))

    def crop_near(p):
        part = crop_pair(p, diag, sib).astype(BF16)
        cs[p, 0] = part[:, :cb]
        c_sib[p][0].start()
        cs[p, 1] = part[:, cb:]
        c_sib[p][1].start()

    def crop_own(p):
        acc[p] = crop_pair(p, yp, ch)

    def crop_send(p):
        c_sib[p][0].wait_recv()
        cys[p] = (acc[p, :, :cb] + cr[p, 0].astype(F32)).astype(BF16)
        c_far[p].start()
        c_sib[p][1].wait_recv()
        acc[p, :, cb:] += cr[p, 1].astype(F32)

    def crop_end(p):
        pr, pc = p // 2, p % 2
        c_far[p].wait_recv()
        v = acc[p, :, cb:] + cyr[p].astype(F32)
        o_gbig[:, pr, pl.ds(pc, g.hb, stride=2), :] = v[:br].reshape(-1, g.hb, cb)
        o_gsmall[:, pr, pl.ds(pc, g.hs, stride=2), :] = v[br:].reshape(-1, g.hs, cb)


    def job(kind, key=None):
        if kind == "d":
            down_part(key)
        elif kind == "near":
            crop_near(key)
        elif kind == "own":
            crop_own(key)
        elif kind == "send":
            crop_send(key)
        elif kind == "end":
            crop_end(key)
        elif kind == "wide":
            wide_g.forward()
            wide_g.near()
        else:
            wide_g.far()
            split_job()
            in_job()

    def receive(h):
        g_mate[h].wait_recv()
        cols = slice(h * hw, (h + 1) * hw)
        theirs = st[5, mate[0], :, cols] * (1.0 / R)
        scale = gain1[:, cols] * inv1[:, cols]
        shift = theirs[1:2] - q1[:, cols] * (1.0 / g.total_rows)
        slope = theirs[0:1] - qn1[:, cols] * (1.0 / g.total_rows)
        for tile in g.tiles:
            at = pl.ds(tile[0], tile[1])
            v = S["gz"][h, at].astype(F32) + shift + S["nz"][at, cols].astype(F32) * slope
            v = (scale * v).astype(BF16)
            gzs[0, at, cols] = v
            row_shifts(gzs, tile, cols, v.astype(F32))

    def both(*pairs):
        for i, *ready in pairs:
            job("d", i)
            for k in ready:
                on(k)

    job("near", 0)
    job("own", 0)
    job("near", 1)
    job("own", 1)
    n_mate[0].wait_recv()
    n_mate[1].wait_recv()
    job("send", 0)
    receive(0)
    cross_x.finish()
    both((0,), (1,))
    job("send", 1)
    on(h_a)
    on(h_b)
    both((2,), (3, 0))
    job("wide")
    both((4, 1),)
    job("near", 2)
    job("split")
    on(2)
    on(3)
    receive(1)
    both((5, 4), (6,))
    job("own", 2)
    job("send", 2)
    on(h_b)
    job("near", 3)
    both((7, 5),)
    on(h_in)
    both((8, 6), (9,))
    job("own", 3)
    on(h_a)
    on(7)
    job("send", 3)
    on(h_in)
    on(8)
    on(h_b)
    on(9)
    on(h_in)
    for h in h_conv:
        on(h)
    add_square(9, S["g_conv"][...])
    job("end", 0)
    job("end", 1)
    for i in range(0, 5):
        on(i)
    job("end", 2)
    for i in range(5, 10):
        on(i)
    job("end", 3)
    for _ in range(bits_of(n)):
        for h in (*h_conv, h_a, h_b, h_in, *h_down):
            on(h)
    for d in deliveries:
        d.finish()
    for i, name in enumerate(layers):
        if name in ("a", "b", "in"):
            add_square(5 + i, S["g_" + name][...].astype(F32))

    grads = {
        "down": S["g_down"][...],
        "a": S["g_a"][...].astype(F32),
        "b": S["g_b"][...].astype(F32),
        "in": S["g_in"][...].astype(F32),
    }
    g_conv = S["g_conv"]
    nm = S["nm"]
    add_square(5, S["g_down"][...])
    place = nm.at[dp * 4 + ch]
    place[...] = S["squares"][...]
    ssem, rsem = sem(), sem()
    everyone(
        lambda peer: pltpu.make_async_remote_copy(
            src_ref=place, dst_ref=place, send_sem=ssem, recv_sem=rsem,
            device_id=peer, device_id_type=MESH,
        ).start()
    )
    some = nm.at[pl.ds(0, 4 * n - 1)]
    total(some, rsem).wait()
    total(some, ssem).wait()
    roots = jnp.sqrt(jnp.sum(nm[...], axis=0))
    norms = [jnp.sum(jnp.where(lane == k, roots, 0.0), axis=1, keepdims=True) for k in range(10)]
    row = lax.broadcasted_iota(jnp.int32, (2, 5), 0)
    col = lax.broadcasted_iota(jnp.int32, (2, 5), 1)
    table = jnp.zeros((2, 5), F32)
    for k in range(10):
        table = jnp.where((row == k // 5) & (col == k % 5), norms[k], table)
    o_ln[...] = table
    o_wn[0:1] = qn1
    o_wn[1:2] = q1
    o_nn[0, 0:1] = qn2
    o_nn[0, 1:2] = q2
    o_nn[1, 0:1] = qn3
    o_nn[1, 1:2] = q3

    def update(rate, weight, grad, moment):
        after = MOMENTUM * moment + rate * (grad + DECAY * weight)
        return weight - after, after

    for i, name in enumerate(layers):
        wnorm = norms[i]
        rate = TRUST * wnorm / (norms[5 + i] + DECAY * wnorm)
        o_new, o_next = {
            "down": (o_ndown, o_mdown), "a": (o_na, o_ma), "b": (o_nb, o_mb),
            "in": (o_nin, o_min), "conv": (o_nconv, o_mconv),
        }[name]
        if name == "down":
            for t in range(9):
                new, after = update(
                    rate, S["k_down"][t].astype(F32), S["g_down"][t], S["m_down"][t]
                )
                o_new[t] = new
                o_next[t] = after
        elif name == "conv":
            for t in range(9):
                new, after = update(
                    rate,
                    S["k_conv"][t].astype(F32),
                    g_conv[:, t * nc : (t + 1) * nc],
                    S["m_conv"][t],
                )
                o_new[t] = new
                o_next[t] = after
        else:
            new, after = update(rate, S["k_" + name][...].astype(F32), grads[name], S["m_" + name][...])
            o_new[...] = new
            o_next[...] = after
    for c in pending:
        c.wait_send()
    for c in drain:
        c.wait()
    assert used[0] <= sems.shape[0], used[0]


def hand_over(*refs):
    count = len(refs) // 2
    copies = [
        pltpu.make_async_copy(refs[k], refs[count + k], refs[-1].at[k]) for k in range(count)
    ]
    for c in copies:
        c.start()
    for c in copies:
        c.wait()


def per_device(
    big_crops, small_crops, conv_down, split_a, split_b, neck_in, neck_conv, norm_wide, norm_neck,
    cot_big, cot_small, mom_down, mom_a, mom_b, mom_in, mom_conv,
):
    n = lax.axis_size("dp")
    g = Geometry(big_crops.shape, small_crops.shape, conv_down.shape, neck_conv.shape, n)

    def taps_first(w):
        return jnp.transpose(w, (1, 2, 0, 3)).reshape(9, w.shape[0], w.shape[3])

    def taps_back(w):
        return jnp.transpose(w.reshape(3, 3, w.shape[1], w.shape[2]), (2, 0, 1, 3))

    args = (
        big_crops.reshape(g.nb * g.hb * 2, 2 * g.hb, g.cb),
        small_crops.reshape(g.ns * g.hs * 2, 2 * g.hs, g.cb),
        taps_first(conv_down), split_a, split_b, neck_in, taps_first(neck_conv),
        norm_wide, norm_neck,
        cot_big.reshape(2, g.big_rows, g.nc), cot_small.reshape(2, g.small_rows, g.nc),
        taps_first(mom_down), mom_a, mom_b, mom_in, taps_first(mom_conv),
    )
    sds = jax.ShapeDtypeStruct
    up = [
        sds((9, g.ch // n, g.wc), F32), sds(mom_a.shape, F32), sds(mom_b.shape, F32),
        sds(mom_in.shape, F32), sds((9, g.ch // n, g.nc), F32),
    ]
    out_shape = [
        sds((2, g.big_rows, g.nc), BF16), sds((2, g.small_rows, g.nc), BF16),
        sds((g.nb * g.hb, 2, 2 * g.hb, g.cb), F32), sds((g.ns * g.hs, 2, 2 * g.hs, g.cb), F32),
        *up, *up,
        sds((2, g.wc), F32), sds((2, 2, g.nc), F32), sds((2, 5), F32),
    ]
    anywhere = pl.BlockSpec(memory_space=pl.ANY)
    vmem = pl.BlockSpec(memory_space=pltpu.VMEM)
    plan = scratch_plan(g)
    res = pl.pallas_call(
        functools.partial(mega, g, tuple(plan)),
        out_shape=[pltpu.VMEM(o.shape, o.dtype) for o in out_shape],
        in_specs=[anywhere] * 16,
        out_specs=[vmem] * 17,
        scratch_shapes=[pltpu.VMEM(shape, dtype) for shape, dtype in plan.values()]
        + [pltpu.SemaphoreType.DMA((count_sems(g),))],
        compiler_params=pltpu.CompilerParams(
            collective_id=0, has_side_effects=True, vmem_limit_bytes=58 * 2**20
        ),
    )(*args)
    res = pl.pallas_call(
        hand_over,
        out_shape=out_shape,
        in_specs=[anywhere] * 17,
        out_specs=[anywhere] * 17,
        scratch_shapes=[pltpu.SemaphoreType.DMA((17,))],
        compiler_params=pltpu.CompilerParams(vmem_limit_bytes=2**20),
    )(*res)
    res = list(res)
    res[0] = res[0].reshape(cot_big.shape)
    res[1] = res[1].reshape(cot_small.shape)
    res[2] = res[2].reshape(big_crops.shape)
    res[3] = res[3].reshape(small_crops.shape)
    for k in (4, 8, 9, 13):
        res[k] = taps_back(res[k])
    return tuple(res)


def solution(mesh):
    in_specs = (
        P("dp", None, None, "chan"),
        P("dp", None, None, "chan"),
        P(None, None, None, "chan"),
        P(None, "chan"),
        P(None, "chan"),
        P(None, "chan"),
        P(None, None, None, "chan"),
        P(),
        P(),
        P(None, "dp", None, None, "chan"),
        P(None, "dp", None, None, "chan"),
        P("dp", None, None, "chan"),
        P("dp", "chan"),
        P("dp", "chan"),
        P("dp", "chan"),
        P("dp", None, None, "chan"),
    )
    out_specs = (
        P(None, "dp", None, None, "chan"),
        P(None, "dp", None, None, "chan"),
        P("dp", None, None, "chan"),
        P("dp", None, None, "chan"),
        P("dp", None, None, "chan"),
        P("dp", "chan"),
        P("dp", "chan"),
        P("dp", "chan"),
        P("dp", None, None, "chan"),
        P("dp", None, None, "chan"),
        P("dp", "chan"),
        P("dp", "chan"),
        P("dp", "chan"),
        P("dp", None, None, "chan"),
        P(None, "chan"),
        P(None, None, "chan"),
        P(),
    )
    return jax.shard_map(
        per_device, mesh=mesh, in_specs=in_specs, out_specs=out_specs, check_vma=False
    )
```

```python
import functools

import jax
import jax.numpy as jnp
from jax import lax
from jax.experimental import pallas as pl
from jax.experimental.pallas import tpu as pltpu
from jax.sharding import PartitionSpec as P

EPSILON = 1e-05
MOMENTUM = 0.9
DECAY = 0.0005
TRUST = 0.1
F32 = jnp.float32
BF16 = jnp.bfloat16
MESH = pl.DeviceIdType.MESH
PLANES = (3, 1, 2, 0)


def dot_nn(left, right):
    return lax.dot_general(left, right, (((1,), (0,)), ((), ())), preferred_element_type=F32)


def dot_nt(left, right):
    return lax.dot_general(left, right, (((1,), (1,)), ((), ())), preferred_element_type=F32)


def dot_tn(left, right):
    return lax.dot_general(left, right, (((0,), (0,)), ((), ())), preferred_element_type=F32)


def mish_parts(v):
    u = jnp.exp(-jnp.abs(v))
    pos = v >= 0
    num = jnp.where(pos, 1.0 + 2.0 * u, u * (u + 2.0))
    rest = jnp.where(pos, 2.0 * u * u, 2.0)
    den = num + rest
    inv = 1.0 / den
    tangent = num * inv
    slope = tangent + v * (rest * (den + num) * inv * inv) * (jnp.where(pos, 1.0, u) / (1.0 + u))
    return v * tangent, slope


def plane_taps(p):
    rows = ((0, -1), (2, 0)) if p // 2 else ((1, 0),)
    cols = ((0, -1), (2, 0)) if p % 2 else ((1, 0),)
    return [(r * 3 + s, di, dj) for r, di in rows for s, dj in cols]


def group_of(di, dj):
    return (2 if di else 0) + (1 if dj else 0)


class Geometry:
    def __init__(self, big, small, down, neck, n_dp):
        self.nb, self.hb = big[0], big[1] // 2
        self.ns, self.hs = small[0], small[1] // 2
        self.cb = big[3]
        self.ch = down[0]
        self.wc = down[3]
        self.nc = neck[3]
        self.n = n_dp
        self.big_rows = self.nb * self.hb * self.hb
        self.small_rows = self.ns * self.hs * self.hs
        self.rows = self.big_rows + self.small_rows
        self.total_rows = self.rows * n_dp
        self.tiles = [
            (i * self.hb * self.hb, self.hb * self.hb, 1, self.hb) for i in range(self.nb)
        ] + [(self.big_rows, self.small_rows, self.ns, self.hs)]


def shift_tile(value, tile, di, dj):
    _, rows, images, side = tile
    cols = value.shape[-1]
    if di:
        v = value.reshape(images, side, side, cols)
        blank = jnp.zeros((images, 1, side, cols), value.dtype)
        if di < 0:
            v = jnp.concatenate([blank, v[:, :-1]], axis=1)
        else:
            v = jnp.concatenate([v[:, 1:], blank], axis=1)
        value = v.reshape(rows, cols)
    if dj:
        v = pltpu.roll(value, 1 if dj < 0 else rows - 1, 0).reshape(rows // side, side, cols)
        at = lax.broadcasted_iota(jnp.int32, (1, side, cols), 1)
        keep = at >= 1 if dj < 0 else at < side - 1
        value = jnp.where(keep, v, 0.0).reshape(rows, cols)
    return value


def bits_of(n):
    return n.bit_length() - 1


def halving_plan(order):
    left = sorted(order)
    plan = []
    for bit in order:
        at = left.index(bit)
        plan.append((bit, 1 << (len(left) - 1 - at), 1 << at))
        left.remove(bit)
    return plan


CONV_SPLIT = (3, 3, 3)


def pair_bit(n):
    return bits_of(n) - 2


def reductions(g):
    rows = g.ch // g.n
    bits = tuple(range(bits_of(g.n)))
    paired = tuple(bit for bit in bits if bit != pair_bit(g.n))
    return {
        "d2": (8, rows, g.wc, paired),
        "d1": (2, rows, g.wc // 2, paired),
        **{f"c{k}": (1, rows, t * g.nc, paired) for k, t in enumerate(CONV_SPLIT)},
        "a": (1, 2 * rows, g.nc, bits),
        "b": (1, 2 * rows, g.nc, bits),
        "in": (1, rows, g.nc, bits),
    }


def scratch_plan(g):
    n = g.n
    R = g.rows
    s = {}
    s["raw_big"] = ((g.nb * g.hb * 2, 2 * g.hb, g.cb), BF16)
    s["raw_small"] = ((g.ns * g.hs * 2, 2 * g.hs, g.cb), BF16)
    s["xg"] = ((4, 4, R, g.cb), BF16)
    s["wv"] = ((9, g.ch, g.wc), BF16)
    s["wn"] = ((g.ch, 9 * g.nc), BF16)
    s["ab"] = ((2 * g.ch, 2 * g.nc), BF16)
    s["nin"] = ((4, g.ch, g.nc), BF16)
    s["sar"] = ((4, g.wc, g.nc), BF16)
    s["sbr"] = ((4, g.wc, g.nc), BF16)
    s["cmat"] = ((4, g.wc, g.nc), BF16)
    s["pw"] = ((2, 4 * g.wc), F32)
    s["pn"] = ((2, 2, 4 * g.nc), F32)
    s["acc"] = ((4, R, g.wc), F32)
    s["n1"] = ((R, g.wc), F32)
    s["s1"] = ((R, g.wc), F32)
    s["wg"] = ((4, R, g.wc), BF16)
    for k in ("f", "b"):
        s["rs_send" + k] = ((2, R, g.nc), BF16)
        s["rs_recv" + k] = ((2, R, g.nc), BF16)
        s["rs_ys" + k] = ((R, g.nc), BF16)
        s["rs_yr" + k] = ((R, g.nc), BF16)
    s["rs_keep"] = ((2, R, g.nc), F32)
    s["n2"] = ((R, g.nc), F32)
    s["s2"] = ((R, g.nc), F32)
    s["fg"] = ((4, R, g.nc), BF16)
    s["yb"] = ((R, 9 * g.nc), F32)
    s["n3"] = ((R, g.nc), F32)
    s["s3"] = ((R, g.nc), F32)
    s["cg"] = ((R, 9 * g.nc), BF16)
    s["ga"] = ((4, R, g.nc), BF16)
    s["gb"] = ((4, R, g.nc), BF16)
    s["pb"] = ((R, g.nc), BF16)
    s["ng"] = ((4, R, g.nc), BF16)
    s["u"] = ((R, g.wc), F32)
    s["gsh"] = ((4, R, g.wc), BF16)
    s["cs"] = ((4, 2, R, g.cb), BF16)
    s["cr"] = ((4, 2, R, g.cb), BF16)
    s["cys"] = ((4, R, g.cb), BF16)
    s["cyr"] = ((4, R, g.cb), BF16)
    s["st"] = ((6, n, 2, g.wc), F32)
    s["nm"] = ((4 * n, 1, 128), F32)
    s["squares"] = ((1, 128), F32)
    for name, (count, rows, cols, order) in reductions(g).items():
        for stage, (_, high, low) in enumerate(halving_plan(order)):
            s[f"h_{name}_s{stage}"] = ((count, high, 2, low, rows, cols), BF16)
            s[f"h_{name}_r{stage}"] = ((count, high, low, rows, cols), BF16)
    s["xz"] = ((2, 4, R, g.cb), BF16)
    s["fz"] = ((2, R, g.nc), BF16)
    s["cz"] = ((R, g.nc), BF16)
    s["cgz"] = ((R, 9 * g.nc), BF16)
    s["gz"] = ((2, R, g.wc // 2), BF16)
    s["qs"] = ((R, g.wc), BF16)
    s["nb"] = ((R, g.wc), BF16)
    s["nz"] = ((R, g.wc), BF16)
    s["gzs"] = ((4, R, g.wc), BF16)
    s["g_down"] = ((9, g.ch // n, g.wc), F32)
    s["g_conv"] = ((g.ch // n, 9 * g.nc), F32)
    s["p_a"] = ((2 * g.ch // n, g.nc), BF16)
    s["p_b"] = ((2 * g.ch // n, g.nc), BF16)
    s["p_in"] = ((g.ch // n, g.nc), BF16)
    s["g_a"] = ((2 * g.ch // n, g.nc), BF16)
    s["g_b"] = ((2 * g.ch // n, g.nc), BF16)
    s["g_in"] = ((g.ch // n, g.nc), BF16)
    s["m_down"] = ((9, g.ch // n, g.wc), F32)
    s["m_a"] = ((2 * g.ch // n, g.nc), F32)
    s["m_b"] = ((2 * g.ch // n, g.nc), F32)
    s["m_in"] = ((g.ch // n, g.nc), F32)
    s["m_conv"] = ((9, g.ch // n, g.nc), F32)
    s["k_down"] = ((9, g.ch // n, g.wc), BF16)
    s["k_a"] = ((2 * g.ch // n, g.nc), BF16)
    s["k_b"] = ((2 * g.ch // n, g.nc), BF16)
    s["k_in"] = ((g.ch // n, g.nc), BF16)
    s["k_conv"] = ((9, g.ch // n, g.nc), BF16)
    return s


def count_sems(g):
    early = [1 + len(order) for name, (_, _, _, order) in reductions(g).items() if name[0] != "d"]
    return BASE_SEMS + sum(early) + 40 * (bits_of(g.n) - 3)


BASE_SEMS = 96


def mega(g, names, *refs):
    (
        big, small, w_down, w_a, w_b, w_in, w_conv, p_wide, p_neck, c_big, c_small,
        m_down, m_a, m_b, m_in, m_conv,
    ) = refs[:16]
    (
        o_big, o_small, o_gbig, o_gsmall, o_ndown, o_na, o_nb, o_nin, o_nconv,
        o_mdown, o_ma, o_mb, o_min, o_mconv, o_wn, o_nn, o_ln,
    ) = refs[16:33]
    S = dict(zip(names, refs[33:-1], strict=True))
    sems = refs[-1]
    n, R, nc, wc, cb = g.n, g.rows, g.nc, g.wc, g.cb
    dp = lax.axis_index("dp")
    ch = lax.axis_index("chan")
    core = lax.rem(ch, 2)
    half = lax.div(ch, 2)
    sib = half * 2 + (1 - core)
    yp = (1 - half) * 2 + core
    diag = (1 - half) * 2 + (1 - core)
    other = 1 - half

    pair = pair_bit(n)
    pbit = lax.rem(lax.div(dp, 1 << pair), 2)
    mate = (dp + (1 - 2 * pbit) * (1 << pair), ch)
    gives = core != pbit
    takes = core == pbit

    used = [0]
    pending = []
    drain = []

    free = []

    def sem():
        if free:
            return free.pop()
        used[0] += 1
        return sems.at[used[0] - 1]

    load_sems = []

    def local(src, dst, own=None):
        if own is None:
            own = sem()
            load_sems.append(own)
        copy = pltpu.make_async_copy(src, dst, own)
        copy.start()
        return copy

    def remote(src, dst, device, ssem=None, rsem=None):
        copy = pltpu.make_async_remote_copy(
            src_ref=src, dst_ref=dst,
            send_sem=sem() if ssem is None else ssem,
            recv_sem=sem() if rsem is None else rsem,
            device_id=device, device_id_type=MESH,
        )
        if ssem is None:
            pending.append(copy)
        return copy

    def total(view, one):
        return pltpu.make_async_copy(view, view, one)

    def shared(view):
        one = sem()
        drain.append(total(view, one))
        return one
    ld_big = local(big, S["raw_big"])
    ld_small = local(small, S["raw_small"])
    ld_wv = local(w_down, S["wv"])
    ab_sem, wn_sem, ga_sem, gb_sem = sem(), sem(), sem(), sem()
    local(w_a, S["ab"].at[:, pl.ds(0, nc)], ab_sem)
    local(w_b, S["ab"].at[:, pl.ds(nc, nc)], ab_sem)
    ld_ab = total(S["ab"], ab_sem)
    ld_in = local(w_in, S["nin"].at[ch])
    ld_p = [local(p_wide, S["pw"]), local(p_neck, S["pn"])]
    for t in range(9):
        local(w_conv.at[t], S["wn"].at[:, pl.ds(t * nc, nc)], wn_sem)
    ld_wn = total(S["wn"], wn_sem)
    br, sr = g.big_rows, g.small_rows
    ld_c = []
    for k, name, one in ((0, "ga", ga_sem), (1, "gb", gb_sem)):
        local(c_big.at[k], S[name].at[ch, pl.ds(0, br)], one)
        local(c_small.at[k], S[name].at[ch, pl.ds(br, sr)], one)
        ld_c.append(total(S[name].at[ch], one))
    bar = pltpu.get_barrier_semaphore()

    def everyone(act):
        def one(k):
            act((lax.rem(dp + lax.div(k, 4), n), lax.rem(ch + lax.rem(k, 4), 4)))

        if n <= 8:
            for k in range(1, 4 * n):
                one(k)
        else:
            lax.fori_loop(1, 4 * n, lambda k, c: (one(k), c)[1], 0)

    bits = [lax.rem(lax.div(dp, 1 << i), 2) for i in range(bits_of(n))]
    dp_peers = [
        sum(((1 - b) if k >> i & 1 else b) * (1 << i) for i, b in enumerate(bits))
        for k in range(n - 1, 0, -1)
    ]
    peers = [(dp, yp), (dp, sib), (dp, diag)] + [(peer, ch) for peer in dp_peers]
    for peer in peers:
        pl.semaphore_signal(bar, inc=1, device_id=peer, device_id_type=MESH)
    xg = S["xg"]
    ld_big.wait()
    o_gbig[...] = S["raw_big"][...].astype(F32).reshape(o_gbig.shape)
    ld_small.wait()
    o_gsmall[...] = S["raw_small"][...].astype(F32).reshape(o_gsmall.shape)

    def split_plane(p):
        pr, pc = p // 2, p % 2
        xg[ch, p, 0:br] = (
            o_gbig[:, pr, pl.ds(pc, g.hb, stride=2), :].reshape(br, cb).astype(BF16)
        )
        xg[ch, p, br:R] = (
            o_gsmall[:, pr, pl.ds(pc, g.hs, stride=2), :].reshape(sr, cb).astype(BF16)
        )

    class Gather:
        def __init__(self, ref, plane=None, ssems=None, rows=None):
            def block(c):
                if rows is not None:
                    return ref.at[c, rows]
                return ref.at[c] if plane is None else ref.at[c, plane]

            if ssems is None:
                three = ref.at[pl.ds(0, 3)] if rows is None else ref.at[pl.ds(0, 3), rows]
                ssems = [shared(three)] * 3
            self.to_sib = remote(block(ch), block(ch), (dp, sib), ssems[0])
            self.to_far = remote(block(ch), block(ch), (dp, yp), ssems[1])
            self.onward = remote(block(yp), block(yp), (dp, sib), ssems[2])

        def start(self):
            self.to_sib.start()
            self.to_far.start()

        def forward(self):
            self.to_far.wait_recv()
            self.onward.start()

        def near(self):
            self.to_sib.wait_recv()

        def far(self):
            self.onward.wait_recv()

    crop_sems = [shared(xg.at[0]) for _ in range(3)]
    crops = {p: Gather(xg, p, crop_sems) for p in PLANES}
    split_plane(PLANES[0])
    pl.semaphore_wait(bar, len(peers))
    upper, lower = pl.ds(0, R // 2), pl.ds(R // 2, R // 2)

    class Cross:
        def __init__(self, buf, source):
            self.buf, self.source = S[buf], source
            self.ssem, self.rsem = shared(self.buf), sem()
            self.arrived = total(self.buf, self.rsem)
            self.onward = remote(self.buf, self.buf, (dp, sib), self.ssem, self.rsem)

        def send(self, block, h, *plane):
            @pl.when(gives)
            def _():
                remote(
                    self.source.at[(block, *plane)], self.buf.at[(h, *plane)], mate,
                    self.ssem, self.rsem,
                ).start()

        def hand_on(self):
            @pl.when(takes)
            def _():
                self.arrived.wait()
                self.onward.start()

        def finish(self):
            @pl.when(gives)
            def _():
                self.arrived.wait()

    cross_x = Cross("xz", xg)
    crops[PLANES[0]].start()
    cross_x.send(ch, half, PLANES[0])
    for p in PLANES[1:]:
        split_plane(p)
        crops[p].start()
        cross_x.send(ch, half, p)
    ld_in.wait()
    neck_in = Gather(S["nin"])
    ld_ab.wait()

    class Rows:
        def __init__(self, buf, lane):
            ref = S[buf]
            ssem, rsem = shared(ref.at[pl.ds(0, 3)]), sem()
            self.copies = [
                remote(
                    S["ab"].at[pl.ds(dev * wc, wc), pl.ds(lane, nc)], ref.at[ch], (dp, dev),
                    ssem, rsem,
                )
                for dev in (yp, diag, sib)
            ]
            self.arrived = total(ref.at[pl.ds(0, 3)], rsem)
            ref[ch] = S["ab"][pl.ds(ch * wc, wc), lane : lane + nc]

        def start(self):
            for c in self.copies:
                c.start()

        def wait(self):
            self.arrived.wait()

    b_rows = Rows("sbr", nc)
    a_rows = Rows("sar", 0)
    neck_in.start()
    b_rows.start()
    ld_wv.wait()
    wv, acc = S["wv"], S["acc"]

    def conv_part(side, p, first):
        x = jnp.concatenate([xg[2 * side, p], xg[2 * side + 1, p]], axis=1)
        for tap, di, dj in plane_taps(p):
            res = dot_nn(x, wv[tap, pl.ds(side * 2 * cb, 2 * cb), :])
            k = group_of(di, dj)
            if first:
                acc[k] = res
            else:
                acc[k] += res
    for p in PLANES:
        crops[p].near()
        conv_part(half, p, p == PLANES[0])
    for p in PLANES[:-1]:
        crops[p].forward()
        cross_x.send(yp, other, p)
        crops[p].far()
        conv_part(other, p, False)
    for tile in g.tiles:
        at = pl.ds(tile[0], tile[1])
        inner = acc[1, at] + shift_tile(acc[3, at], tile, -1, 0)
        acc[2, at] = shift_tile(acc[2, at], tile, -1, 0) + shift_tile(inner, tile, 0, -1)
    p = PLANES[-1]
    crops[p].forward()
    cross_x.send(yp, other, p)
    crops[p].far()
    conv_part(other, p, False)
    acc[0] = acc[0] + acc[2]

    st = S["st"]
    st_send, st_recv = sem(), [sem(), sem()]

    def exchange(phase, first, second, cols):
        st[phase, dp, 0:1, 0:cols] = first
        st[phase, dp, 1:2, 0:cols] = second
        ssem, rsem = st_send, st_recv[phase % 2]
        mine = st.at[phase, dp, :, pl.ds(0, cols)]
        for peer in dp_peers:
            pltpu.make_async_remote_copy(
                src_ref=mine, dst_ref=mine, send_sem=ssem, recv_sem=rsem,
                device_id=(peer, ch), device_id_type=MESH,
            ).start()
        some = st.at[phase, pl.ds(0, n - 1), :, pl.ds(0, cols)]

        def finish():
            total(some, rsem).wait()
            total(some, ssem).wait()
            return st[phase, :, :, 0:cols]

        return finish

    def norm_start(phase, ref):
        cols = ref.shape[-1]
        mean = jnp.sum(ref[...], axis=0, keepdims=True) * (1.0 / R)
        dev = ref[...] - mean
        return exchange(phase, mean, jnp.sum(dev * dev, axis=0, keepdims=True), cols)

    def norm_finish(finish):
        v = finish()
        tot = jnp.sum(v, axis=0)
        mean = tot[0:1] * (1.0 / n)
        off = v - mean[None]
        spread = jnp.sum(off * off, axis=0)[0:1]
        var = (tot[1:2] + R * spread) * (1.0 / g.total_rows)
        return mean, lax.rsqrt(var + EPSILON)

    def sums_finish(finish):
        tot = jnp.sum(finish(), axis=0)
        return tot[0:1], tot[1:2]
    fin = norm_start(0, acc.at[0])
    for c in ld_p:
        c.wait()
    gain1 = S["pw"][0:1, pl.ds(ch * wc, wc)]
    bias1 = S["pw"][1:2, pl.ds(ch * wc, wc)]
    neck_in.forward()
    neck_in.near()
    neck_in.far()
    b_rows.wait()
    rows_b = jnp.concatenate([S["sbr"][k] for k in range(4)], axis=1)
    for k in range(4):
        S["cmat"][k] = dot_nn(rows_b, S["nin"][k]).astype(BF16)
    mean1, inv1 = norm_finish(fin)
    wg = S["wg"]
    for t0 in range(0, R, 256):
        at = pl.ds(t0, 256)
        normed = (acc[0, at] - mean1) * inv1
        S["n1"][at] = normed
        S["nb"][at] = normed.astype(BF16)
        wg[ch, at] = mish_parts(normed * gain1 + bias1)[0].astype(BF16)

    summed = []

    def reduce_chan(k, pair):
        send, recv = S["rs_send" + k], S["rs_recv" + k]
        ys, yr, keep = S["rs_ys" + k], S["rs_yr" + k], S["rs_keep"]
        parts = [pl.ds(0, R // 2), pl.ds(R // 2, R // 2)]
        s0, sy, r1 = shared(send), shared(ys), sem()
        summed.append(r1)
        c0 = [remote(send.at[0, at], recv.at[0, at], (dp, sib), s0) for at in parts]
        c1 = [remote(send.at[1, at], recv.at[1, at], (dp, sib), s0, r1) for at in parts]
        cy = [remote(ys.at[at], yr.at[at], (dp, yp), sy) for at in parts]
        summed.extend(c.dst_sem for c in (*c0, *cy))
        for at, far, near in zip(parts, c0, c1, strict=True):
            part = pair(at, diag, sib).astype(BF16)
            send[0, at] = part[:, :nc]
            far.start()
            send[1, at] = part[:, nc:]
            near.start()
        for at, near, far in zip(parts, c0, cy, strict=True):
            part = pair(at, yp, ch)
            keep[1, at] = part[:, nc:]
            near.wait_recv()
            ys[at] = (part[:, :nc] + recv[0, at].astype(F32)).astype(BF16)
            far.start()
        total(recv.at[1], r1).wait()
        keep[1] += recv[1].astype(F32)

        def finish():
            for at, far in zip(parts, cy, strict=True):
                far.wait_recv()
                keep[1, at] += yr[at].astype(F32)

        return finish

    def neck_pair(at, d0, d1):
        return dot_nn(
            wg[ch, at], jnp.concatenate([S["cmat"][d0], S["cmat"][d1]], axis=1)
        )
    n_mate = [remote(S["nb"].at[at], S["nz"].at[at], mate) for at in (upper, lower)]
    n_mate[0].start()
    rs_fin = reduce_chan("f", neck_pair)
    for c in ld_c:
        c.wait()
    gb_g = Gather(S["gb"])
    ga_g = Gather(S["ga"])
    wide_g = Gather(wg)
    cross_x.hand_on()
    for t0 in range(0, R, 256):
        at = pl.ds(t0, 256)
        S["s1"][at] = mish_parts(S["n1"][at] * gain1 + bias1)[1]
    rs_fin()
    a_rows.start()
    z2 = S["rs_keep"].at[1]
    fin = norm_start(1, z2)
    n_mate[1].start()
    gain2 = S["pn"][0, 0:1, pl.ds(ch * nc, nc)]
    bias2 = S["pn"][0, 1:2, pl.ds(ch * nc, nc)]
    gain3 = S["pn"][1, 0:1, pl.ds(ch * nc, nc)]
    bias3 = S["pn"][1, 1:2, pl.ds(ch * nc, nc)]
    mean2, inv2 = norm_finish(fin)
    fg = S["fg"]
    for t0 in range(0, R, 256):
        at = pl.ds(t0, 256)
        normed = (z2[at] - mean2) * inv2
        S["n2"][at] = normed
        fg[ch, at] = mish_parts(normed * gain2 + bias2)[0].astype(BF16)
    first_g = Gather(fg)
    first_g.start()
    ld_wn.wait()
    wn, yb = S["wn"], S["yb"]

    def neck_part(side, first):
        x = jnp.concatenate([fg[2 * side], fg[2 * side + 1]], axis=1)
        w = wn[pl.ds(side * 2 * nc, 2 * nc), :]
        if first:
            yb[...] = dot_nn(x, w)
        else:
            yb[...] += dot_nn(x, w)

    first_g.near()
    neck_part(half, True)
    for t0 in range(0, R, 256):
        at = pl.ds(t0, 256)
        S["s2"][at] = mish_parts(S["n2"][at] * gain2 + bias2)[1]
    first_g.forward()
    first_g.far()
    gb_g.start()
    ga_g.start()
    neck_part(other, False)
    z3 = S["n3"]
    for tile in g.tiles:
        at = pl.ds(tile[0], tile[1])
        cols = []
        for s in range(3):
            cols.append(
                yb[at, (3 + s) * nc : (4 + s) * nc]
                + shift_tile(yb[at, s * nc : (s + 1) * nc], tile, -1, 0)
                + shift_tile(yb[at, (6 + s) * nc : (7 + s) * nc], tile, 1, 0)
            )
        z3[at] = (
            cols[1] + shift_tile(cols[0], tile, 0, -1) + shift_tile(cols[2], tile, 0, 1)
        )
    fin = norm_start(2, z3)
    cross_f = Cross("fz", fg)
    cross_f.send(ch, half)
    cross_f.send(yp, other)
    mean3, inv3 = norm_finish(fin)
    q_tot = jnp.zeros((1, nc), F32)
    qn_tot = jnp.zeros((1, nc), F32)
    for t0 in range(0, R, 256):
        at = pl.ds(t0, 256)
        normed = (z3[at] - mean3) * inv3
        slope = mish_parts(normed * gain3 + bias3)[1]
        q = S["gb"][ch, at].astype(F32) * slope
        z3[at] = normed
        S["s3"][at] = q
        q_tot += jnp.sum(q, axis=0, keepdims=True)
        qn_tot += jnp.sum(q * normed, axis=0, keepdims=True)
    fin = exchange(3, qn_tot, q_tot, nc)

    def grad_in(q, normed, gain, inv, qn_sum, q_sum):
        return gain * inv * (
            q - q_sum * (1.0 / g.total_rows) - normed * (qn_sum * (1.0 / g.total_rows))
        )

    stage_sems = {}
    plans = reductions(g)

    class Halving:
        def __init__(self, name, item, *results):
            self.name, self.item, self.results = name, item, results
            self.plan = halving_plan(plans[name][3])
            self.copies = []
            self.alone = S[f"h_{name}_s0"].shape[0] == 1
            if name not in stage_sems:
                stages = range(len(self.plan))
                stage_sems[name] = (
                    [sem()] * len(self.plan)
                    if self.alone
                    else [shared(S[f"h_{name}_s{i}"].at[:, :, 0]) for i in stages]
                )
            for i, (bit, high, low) in enumerate(self.plan):
                own = lax.rem(lax.div(dp, 1 << bit), 2)
                peer = dp + (1 - 2 * own) * (1 << bit)
                send = S[f"h_{name}_s{i}"]
                recv = S[f"h_{name}_r{i}"]
                self.copies.append(
                    remote(
                        send.at[item, :, 1 - own], recv.at[item], (peer, ch), stage_sems[name][i]
                    )
                )

        def start(self, stage=0):
            self.copies[stage].start()

        def step(self, stage):
            bit, high, low = self.plan[stage]
            own = lax.rem(lax.div(dp, 1 << bit), 2)
            send = S[f"h_{self.name}_s{stage}"]
            recv = S[f"h_{self.name}_r{stage}"]
            self.copies[stage].wait_recv()
            if self.alone:
                self.copies[stage].wait_send()
            both = send[self.item, :, own].astype(F32) + recv[self.item].astype(F32)
            if stage + 1 < len(self.plan):
                after = S[f"h_{self.name}_s{stage + 1}"]
                after[self.item] = both.astype(BF16).reshape(after.shape[1:])
                self.start(stage + 1)
            else:
                width = self.results[0].shape[-1]
                for k, ref in enumerate(self.results):
                    ref[...] = both[0, 0, :, k * width : (k + 1) * width].astype(ref.dtype)

    def put_rows(name, value):
        ref = S[f"h_{name}_s0"]
        _, high, _, low, rows, cols = ref.shape
        value = value.astype(BF16)
        for e in range(n):
            r, c = e % (n // 4), e // (n // 4)
            ref[0, e // (2 * low), e // low % 2, e % low] = value[
                r * rows : (r + 1) * rows, c * cols : (c + 1) * cols
            ]

    quarter = n // 4
    at_home = lax.div(dp, quarter) == ch

    class Deliver:
        def __init__(self, name):
            self.src, self.dst = S[f"p_{name}"], S[f"g_{name}"]
            target = (ch * quarter + lax.rem(dp, quarter), lax.div(dp, quarter))
            self.copy = pltpu.make_async_remote_copy(
                src_ref=self.src, dst_ref=self.dst, send_sem=sem(), recv_sem=sem(),
                device_id=target, device_id_type=MESH,
            )

        def start(self):
            @pl.when(at_home)
            def _():
                self.dst[...] = self.src[...]

            @pl.when(jnp.logical_not(at_home))
            def _():
                self.copy.start()

        def finish(self):
            @pl.when(jnp.logical_not(at_home))
            def _():
                self.copy.wait_recv()
                self.copy.wait_send()

    def put(name, item, first_block, value):
        ref = S[f"h_{name}_s0"]
        _, high, _, low, rows, cols = ref.shape
        at = first_block // (2 * low)
        count = value.shape[0] // (rows * 2 * low)
        ref[item, at : at + count] = value.astype(BF16).reshape(count, 2, low, rows, cols)

    for t0 in range(0, R, 256):
        at = pl.ds(t0, 256)
        yb[at, 0:nc] = mish_parts(z3[at] * gain3 + bias3)[0]
    gb_g.forward()
    gb_g.near()
    gb_g.far()
    u = S["u"]
    u[...] = dot_nt(
        jnp.concatenate([S["gb"][k] for k in range(4)], axis=1),
        jnp.concatenate([S["sbr"][k] for k in range(4)], axis=1),
    )
    qn3, q3 = sums_finish(fin)
    cg = S["cg"]

    def tap_shifts(dst, tile, v):
        at = pl.ds(tile[0], tile[1])
        for r in range(3):
            vi = shift_tile(v, tile, 1 - r, 0)
            for s in range(3):
                t = r * 3 + s
                dst[at, t * nc : (t + 1) * nc] = shift_tile(vi, tile, 0, 1 - s).astype(BF16)

    for tile in g.tiles:
        at = pl.ds(tile[0], tile[1])
        v = grad_in(S["s3"][at], z3[at], gain3, inv3, qn3, q3)
        tap_shifts(cg, tile, v.astype(BF16).astype(F32))
    to_mate = remote(cg.at[:, pl.ds(4 * nc, nc)], S["cz"], mate)
    to_mate.start()

    rows = g.ch // n
    reuse = [*load_sems, ab_sem, wn_sem, ga_sem, gb_sem]
    ld_m = [
        local(src, S[name], one)
        for (src, name), one in zip(
            (
                (m_down, "m_down"), (m_a, "m_a"), (m_b, "m_b"), (m_in, "m_in"),
                (m_conv, "m_conv"),
                (w_down.at[:, pl.ds(dp * rows, rows)], "k_down"),
                (w_a.at[pl.ds(dp * 2 * rows, 2 * rows)], "k_a"),
                (w_b.at[pl.ds(dp * 2 * rows, 2 * rows)], "k_b"),
                (w_in.at[pl.ds(dp * rows, rows)], "k_in"),
                (w_conv.at[:, pl.ds(dp * rows, rows)], "k_conv"),
            ),
            reuse,
            strict=True,
        )
    ]

    def back_pair(at, d0, d1):
        w = jnp.concatenate([wn[pl.ds(d0 * nc, nc), :], wn[pl.ds(d1 * nc, nc), :]], axis=0)
        return dot_nt(cg[at], w)

    cross_f.hand_on()
    rs_fin = reduce_chan("b", back_pair)
    ga_g.forward()
    ga_g.near()
    ga_g.far()
    a_rows.wait()
    u[...] += dot_nt(
        jnp.concatenate([S["ga"][k] for k in range(4)], axis=1),
        jnp.concatenate([S["sar"][k] for k in range(4)], axis=1),
    )
    h_a = Halving("a", 0, S["p_a"])
    put_rows("a", dot_tn(wg[ch], jnp.concatenate([S["ga"][k] for k in range(4)], axis=1)))
    h_a.start()
    deliveries = []
    done = {}

    def on(what):
        h = h_down[what] if isinstance(what, int) else what
        stage = done.setdefault((h.name, h.item), 0)
        if stage >= len(h.plan):
            return
        h.step(stage)
        done[h.name, h.item] += 1
        if h.name in ("a", "b", "in") and stage == len(h.plan) - 1:
            deliveries.append(Deliver(h.name))
            deliveries[-1].start()

    starts = [sum(CONV_SPLIT[:k]) * nc for k in range(len(CONV_SPLIT) + 1)]
    h_conv = [
        Halving(f"c{k}", 0, S["g_conv"].at[:, pl.ds(starts[k], starts[k + 1] - starts[k])])
        for k in range(len(CONV_SPLIT))
    ]
    def sq(value):
        v = value * value
        while v.ndim > 2:
            v = jnp.sum(v, axis=0)
        v = jnp.sum(v, axis=0, keepdims=True)
        out = v[:, 0:128]
        for k in range(128, v.shape[1], 128):
            out = out + v[:, k : k + 128]
        return out

    layers = ("down", "a", "b", "in", "conv")
    lane = lax.broadcasted_iota(jnp.int32, (1, 128), 1)

    def add_square(i, value):
        total_sq = jnp.sum(sq(value), axis=1, keepdims=True)
        S["squares"][...] = jnp.where(lane == i, total_sq, S["squares"][...])

    S["squares"][...] = jnp.zeros((1, 128), F32)
    for c in ld_m:
        c.wait()
    for i, name in enumerate(layers):
        add_square(i, S["k_" + name][...].astype(F32))
    rs_fin()
    q_tot = jnp.zeros((1, nc), F32)
    qn_tot = jnp.zeros((1, nc), F32)
    q2r = S["rs_keep"].at[1]
    for t0 in range(0, R, 256):
        at = pl.ds(t0, 256)
        q = q2r[at] * S["s2"][at]
        q2r[at] = q
        q_tot += jnp.sum(q, axis=0, keepdims=True)
        qn_tot += jnp.sum(q * S["n2"][at], axis=0, keepdims=True)
    fin = exchange(4, qn_tot, q_tot, nc)
    to_mate.wait_recv()
    for tile in g.tiles:
        tap_shifts(S["cgz"], tile, S["cz"][pl.ds(tile[0], tile[1])].astype(F32))
    cross_f.finish()
    mine = jnp.concatenate([fg[pbit], fg[pbit + 2]], axis=1)
    theirs = jnp.concatenate([S["fz"][0], S["fz"][1]], axis=1)
    for k, h in enumerate(h_conv):
        cols = slice(starts[k], starts[k + 1])
        put(h.name, 0, 0, dot_tn(mine, cg[:, cols]) + dot_tn(theirs, S["cgz"][:, cols]))
        h.start()


    on(h_a)
    qn2, q2 = sums_finish(fin)
    ng = S["ng"]
    for t0 in range(0, R, 256):
        at = pl.ds(t0, 256)
        ng[ch, at] = grad_in(q2r[at], S["n2"][at], gain2, inv2, qn2, q2).astype(BF16)
    neck_g = Gather(ng)
    neck_g.start()
    def wide_part(side):
        return dot_nt(
            jnp.concatenate([ng[2 * side], ng[2 * side + 1]], axis=1),
            jnp.concatenate([S["cmat"][2 * side], S["cmat"][2 * side + 1]], axis=1),
        )
    neck_g.near()
    u[...] += wide_part(half)
    on(h_a)
    on(h_conv[0])
    neck_g.forward()
    on(h_conv[1])
    neck_g.far()
    wide_g.start()
    u[...] += wide_part(other)
    q_tot = jnp.zeros((1, wc), F32)
    qn_tot = jnp.zeros((1, wc), F32)
    for t0 in range(0, R, 256):
        at = pl.ds(t0, 256)
        q = u[at] * S["s1"][at]
        u[at] = q
        q_tot += jnp.sum(q, axis=0, keepdims=True)
        qn_tot += jnp.sum(q * S["n1"][at], axis=0, keepdims=True)
    fin = exchange(5, qn_tot, q_tot, wc)
    for t0 in range(0, R, 256):
        at = pl.ds(t0, 256)
        S["qs"][at] = (u[at] - q_tot * (1.0 / R) - S["n1"][at] * (qn_tot * (1.0 / R))).astype(BF16)
    hw = wc // 2
    halves = [pl.ds(h * hw, hw) for h in range(2)]
    g_mate = [remote(S["qs"].at[:, halves[h]], S["gz"].at[h], mate) for h in range(2)]
    for c in g_mate:
        c.start()

    ng_whole = jnp.concatenate([ng[k] for k in range(4)], axis=1)
    h_b = Halving("b", 0, S["p_b"])
    cols = []
    for k in range(4):
        back = dot_nt(
            ng_whole,
            jnp.concatenate([S["nin"][c, k * nc : (k + 1) * nc] for c in range(4)], axis=1),
        )
        cols.append((S["gb"][k].astype(F32) + back).astype(BF16))
    put_rows("b", dot_tn(wg[ch], jnp.concatenate(cols, axis=1)))
    on(h_conv[2])
    h_b.start()
    h_in = Halving("in", 0, S["p_in"])
    qn1, q1 = sums_finish(fin)
    gsh, gzs = S["gsh"], S["gzs"]

    for one in (*crops.values(), neck_in, first_g, gb_g, ga_g):
        free.extend((one.to_sib.dst_sem, one.to_far.dst_sem, one.onward.dst_sem))
    free.extend(summed)

    def row_shifts(dst, tile, cols, v):
        at = pl.ds(tile[0], tile[1])
        dst[1, at, cols] = shift_tile(v, tile, 0, 1).astype(BF16)
        v = shift_tile(v, tile, 1, 0)
        dst[2, at, cols] = v.astype(BF16)
        dst[3, at, cols] = shift_tile(v, tile, 0, 1).astype(BF16)

    for tile in g.tiles:
        at = pl.ds(tile[0], tile[1])
        v = grad_in(u[at], S["n1"][at], gain1, inv1, qn1, q1)
        gsh[0, at] = v.astype(BF16)
    for tile in g.tiles:
        at = pl.ds(tile[0], tile[1])
        row_shifts(gsh, tile, slice(0, wc), gsh[0, at].astype(F32))

    where = {tap: (tap, p, k) for tap, p, k in
             ((t, p, group_of(di, dj)) for p in PLANES for t, di, dj in plane_taps(p))}

    def split_job():
        pb = S["pb"]
        split = dot_nn(
            jnp.concatenate([wg[k] for k in range(4)], axis=1), S["ab"][...]
        )
        o_big[0] = split[:br, :nc].astype(BF16)
        o_small[0] = split[br:, :nc].astype(BF16)
        part = split[:, nc:].astype(BF16)
        pb[...] = part
        block = (part.astype(F32) + yb[:, 0:nc]).astype(BF16)
        o_big[1] = block[:br]
        o_small[1] = block[br:]

    def in_job():
        put_rows("in", dot_tn(S["pb"][...], jnp.concatenate([ng[k] for k in range(4)], axis=1)))
        h_in.start()

    taps = [(tap, p, group_of(di, dj)) for p in PLANES for tap, di, dj in plane_taps(p)]
    parts = []
    for h in range(2):
        for p in PLANES:
            of_plane = [(tap, k) for tap, q, k in taps if q == p]
            parts += [(h, p, of_plane[i : i + 2]) for i in range(0, len(of_plane), 2)]
    h_down = []
    counts = {1: 0, 2: 0}
    for h, p, two in parts:
        results = [S["g_down"].at[tap, :, halves[h]] for tap, _ in two]
        h_down.append(Halving(f"d{len(two)}", counts[len(two)], *results))
        counts[len(two)] += 1

    def down_part(i):
        h, p, two = parts[i]
        mine = jnp.concatenate([xg[pbit, p], xg[pbit + 2, p]], axis=1)
        theirs = jnp.concatenate([S["xz"][0, p], S["xz"][1, p]], axis=1)
        cols = slice(h * hw, (h + 1) * hw)
        own = jnp.concatenate([gsh[k, :, cols] for _, k in two], axis=1)
        far = jnp.concatenate([gzs[k, :, cols] for _, k in two], axis=1)
        put(h_down[i].name, h_down[i].item, 0, dot_tn(mine, own) + dot_tn(theirs, far))
        h_down[i].start()

    cs, cr, cys, cyr = S["cs"], S["cr"], S["cys"], S["cyr"]
    cs_sem, cys_sem = shared(cs), shared(cys)
    c_sib = {
        p: [remote(cs.at[p, k], cr.at[p, k], (dp, sib), cs_sem) for k in range(2)] for p in PLANES
    }
    c_far = {p: remote(cys.at[p], cyr.at[p], (dp, yp), cys_sem) for p in PLANES}

    def crop_pair(p, d0, d1):
        left, right = [], []
        for tap, di, dj in plane_taps(p):
            left.append(gsh[group_of(di, dj)])
            right.append(
                jnp.concatenate(
                    [wv[tap, pl.ds(d0 * cb, cb), :], wv[tap, pl.ds(d1 * cb, cb), :]], axis=0
                )
            )
        return dot_nt(jnp.concatenate(left, axis=1), jnp.concatenate(right, axis=1))

    def crop_near(p):
        part = crop_pair(p, diag, sib).astype(BF16)
        cs[p, 0] = part[:, :cb]
        c_sib[p][0].start()
        cs[p, 1] = part[:, cb:]
        c_sib[p][1].start()

    def crop_own(p):
        acc[p] = crop_pair(p, yp, ch)

    def crop_send(p):
        c_sib[p][0].wait_recv()
        cys[p] = (acc[p, :, :cb] + cr[p, 0].astype(F32)).astype(BF16)
        c_far[p].start()
        c_sib[p][1].wait_recv()
        acc[p, :, cb:] += cr[p, 1].astype(F32)

    def crop_end(p):
        pr, pc = p // 2, p % 2
        c_far[p].wait_recv()
        v = acc[p, :, cb:] + cyr[p].astype(F32)
        o_gbig[:, pr, pl.ds(pc, g.hb, stride=2), :] = v[:br].reshape(-1, g.hb, cb)
        o_gsmall[:, pr, pl.ds(pc, g.hs, stride=2), :] = v[br:].reshape(-1, g.hs, cb)


    def job(kind, key=None):
        if kind == "d":
            down_part(key)
        elif kind == "near":
            crop_near(key)
        elif kind == "own":
            crop_own(key)
        elif kind == "send":
            crop_send(key)
        elif kind == "end":
            crop_end(key)
        elif kind == "wide":
            wide_g.forward()
            wide_g.near()
        else:
            wide_g.far()
            split_job()
            in_job()

    def receive(h):
        g_mate[h].wait_recv()
        cols = slice(h * hw, (h + 1) * hw)
        theirs = st[5, mate[0], :, cols] * (1.0 / R)
        scale = gain1[:, cols] * inv1[:, cols]
        shift = theirs[1:2] - q1[:, cols] * (1.0 / g.total_rows)
        slope = theirs[0:1] - qn1[:, cols] * (1.0 / g.total_rows)
        for tile in g.tiles:
            at = pl.ds(tile[0], tile[1])
            v = S["gz"][h, at].astype(F32) + shift + S["nz"][at, cols].astype(F32) * slope
            v = (scale * v).astype(BF16)
            gzs[0, at, cols] = v
            row_shifts(gzs, tile, cols, v.astype(F32))

    def both(*pairs):
        for i, *ready in pairs:
            job("d", i)
            for k in ready:
                on(k)

    job("near", 0)
    job("own", 0)
    job("near", 1)
    job("own", 1)
    n_mate[0].wait_recv()
    n_mate[1].wait_recv()
    job("send", 0)
    receive(0)
    cross_x.finish()
    both((0,), (1,))
    job("send", 1)
    on(h_a)
    on(h_b)
    both((2,), (3, 0))
    job("wide")
    both((4, 1),)
    job("near", 2)
    job("split")
    on(2)
    on(3)
    receive(1)
    both((5, 4), (6,))
    job("own", 2)
    job("send", 2)
    on(h_b)
    job("near", 3)
    both((7, 5),)
    on(h_in)
    both((8, 6), (9,))
    job("own", 3)
    on(h_a)
    on(7)
    job("send", 3)
    on(h_in)
    on(8)
    on(h_b)
    on(9)
    on(h_in)
    for h in h_conv:
        on(h)
    add_square(9, S["g_conv"][...])
    job("end", 0)
    job("end", 1)
    for i in range(0, 5):
        on(i)
    job("end", 2)
    for i in range(5, 10):
        on(i)
    job("end", 3)
    for _ in range(bits_of(n)):
        for h in (*h_conv, h_a, h_b, h_in, *h_down):
            on(h)
    for d in deliveries:
        d.finish()
    for i, name in enumerate(layers):
        if name in ("a", "b", "in"):
            add_square(5 + i, S["g_" + name][...].astype(F32))

    grads = {
        "down": S["g_down"][...],
        "a": S["g_a"][...].astype(F32),
        "b": S["g_b"][...].astype(F32),
        "in": S["g_in"][...].astype(F32),
    }
    g_conv = S["g_conv"]
    nm = S["nm"]
    add_square(5, S["g_down"][...])
    place = nm.at[dp * 4 + ch]
    place[...] = S["squares"][...]
    ssem, rsem = sem(), sem()
    everyone(
        lambda peer: pltpu.make_async_remote_copy(
            src_ref=place, dst_ref=place, send_sem=ssem, recv_sem=rsem,
            device_id=peer, device_id_type=MESH,
        ).start()
    )
    some = nm.at[pl.ds(0, 4 * n - 1)]
    total(some, rsem).wait()
    total(some, ssem).wait()
    roots = jnp.sqrt(jnp.sum(nm[...], axis=0))
    norms = [jnp.sum(jnp.where(lane == k, roots, 0.0), axis=1, keepdims=True) for k in range(10)]
    row = lax.broadcasted_iota(jnp.int32, (2, 5), 0)
    col = lax.broadcasted_iota(jnp.int32, (2, 5), 1)
    table = jnp.zeros((2, 5), F32)
    for k in range(10):
        table = jnp.where((row == k // 5) & (col == k % 5), norms[k], table)
    o_ln[...] = table
    o_wn[0:1] = qn1
    o_wn[1:2] = q1
    o_nn[0, 0:1] = qn2
    o_nn[0, 1:2] = q2
    o_nn[1, 0:1] = qn3
    o_nn[1, 1:2] = q3

    def update(rate, weight, grad, moment):
        after = MOMENTUM * moment + rate * (grad + DECAY * weight)
        return weight - after, after

    for i, name in enumerate(layers):
        wnorm = norms[i]
        rate = TRUST * wnorm / (norms[5 + i] + DECAY * wnorm)
        o_new, o_next = {
            "down": (o_ndown, o_mdown), "a": (o_na, o_ma), "b": (o_nb, o_mb),
            "in": (o_nin, o_min), "conv": (o_nconv, o_mconv),
        }[name]
        if name == "down":
            for t in range(9):
                new, after = update(
                    rate, S["k_down"][t].astype(F32), S["g_down"][t], S["m_down"][t]
                )
                o_new[t] = new
                o_next[t] = after
        elif name == "conv":
            for t in range(9):
                new, after = update(
                    rate,
                    S["k_conv"][t].astype(F32),
                    g_conv[:, t * nc : (t + 1) * nc],
                    S["m_conv"][t],
                )
                o_new[t] = new
                o_next[t] = after
        else:
            new, after = update(rate, S["k_" + name][...].astype(F32), grads[name], S["m_" + name][...])
            o_new[...] = new
            o_next[...] = after
    for c in pending:
        c.wait_send()
    for c in drain:
        c.wait()
    assert used[0] <= sems.shape[0], used[0]


def hand_over(*refs):
    count = len(refs) // 2
    copies = [
        pltpu.make_async_copy(refs[k], refs[count + k], refs[-1].at[k]) for k in range(count)
    ]
    for c in copies:
        c.start()
    for c in copies:
        c.wait()


def per_device(
    big_crops, small_crops, conv_down, split_a, split_b, neck_in, neck_conv, norm_wide, norm_neck,
    cot_big, cot_small, mom_down, mom_a, mom_b, mom_in, mom_conv,
):
    n = lax.axis_size("dp")
    g = Geometry(big_crops.shape, small_crops.shape, conv_down.shape, neck_conv.shape, n)

    def taps_first(w):
        return jnp.transpose(w, (1, 2, 0, 3)).reshape(9, w.shape[0], w.shape[3])

    def taps_back(w):
        return jnp.transpose(w.reshape(3, 3, w.shape[1], w.shape[2]), (2, 0, 1, 3))

    args = (
        big_crops.reshape(g.nb * g.hb * 2, 2 * g.hb, g.cb),
        small_crops.reshape(g.ns * g.hs * 2, 2 * g.hs, g.cb),
        taps_first(conv_down), split_a, split_b, neck_in, taps_first(neck_conv),
        norm_wide, norm_neck,
        cot_big.reshape(2, g.big_rows, g.nc), cot_small.reshape(2, g.small_rows, g.nc),
        taps_first(mom_down), mom_a, mom_b, mom_in, taps_first(mom_conv),
    )
    sds = jax.ShapeDtypeStruct
    up = [
        sds((9, g.ch // n, g.wc), F32), sds(mom_a.shape, F32), sds(mom_b.shape, F32),
        sds(mom_in.shape, F32), sds((9, g.ch // n, g.nc), F32),
    ]
    out_shape = [
        sds((2, g.big_rows, g.nc), BF16), sds((2, g.small_rows, g.nc), BF16),
        sds((g.nb * g.hb, 2, 2 * g.hb, g.cb), F32), sds((g.ns * g.hs, 2, 2 * g.hs, g.cb), F32),
        *up, *up,
        sds((2, g.wc), F32), sds((2, 2, g.nc), F32), sds((2, 5), F32),
    ]
    anywhere = pl.BlockSpec(memory_space=pl.ANY)
    vmem = pl.BlockSpec(memory_space=pltpu.VMEM)
    plan = scratch_plan(g)
    res = pl.pallas_call(
        functools.partial(mega, g, tuple(plan)),
        out_shape=[pltpu.VMEM(o.shape, o.dtype) for o in out_shape],
        in_specs=[anywhere] * 16,
        out_specs=[vmem] * 17,
        scratch_shapes=[pltpu.VMEM(shape, dtype) for shape, dtype in plan.values()]
        + [pltpu.SemaphoreType.DMA((count_sems(g),))],
        compiler_params=pltpu.CompilerParams(
            collective_id=0, has_side_effects=True, vmem_limit_bytes=58 * 2**20
        ),
    )(*args)
    res = pl.pallas_call(
        hand_over,
        out_shape=out_shape,
        in_specs=[anywhere] * 17,
        out_specs=[anywhere] * 17,
        scratch_shapes=[pltpu.SemaphoreType.DMA((17,))],
        compiler_params=pltpu.CompilerParams(vmem_limit_bytes=2**20),
    )(*res)
    res = list(res)
    res[0] = res[0].reshape(cot_big.shape)
    res[1] = res[1].reshape(cot_small.shape)
    res[2] = res[2].reshape(big_crops.shape)
    res[3] = res[3].reshape(small_crops.shape)
    for k in (4, 8, 9, 13):
        res[k] = taps_back(res[k])
    return tuple(res)


def solution(mesh):
    in_specs = (
        P("dp", None, None, "chan"),
        P("dp", None, None, "chan"),
        P(None, None, None, "chan"),
        P(None, "chan"),
        P(None, "chan"),
        P(None, "chan"),
        P(None, None, None, "chan"),
        P(),
        P(),
        P(None, "dp", None, None, "chan"),
        P(None, "dp", None, None, "chan"),
        P("dp", None, None, "chan"),
        P("dp", "chan"),
        P("dp", "chan"),
        P("dp", "chan"),
        P("dp", None, None, "chan"),
    )
    out_specs = (
        P(None, "dp", None, None, "chan"),
        P(None, "dp", None, None, "chan"),
        P("dp", None, None, "chan"),
        P("dp", None, None, "chan"),
        P("dp", None, None, "chan"),
        P("dp", "chan"),
        P("dp", "chan"),
        P("dp", "chan"),
        P("dp", None, None, "chan"),
        P("dp", None, None, "chan"),
        P("dp", "chan"),
        P("dp", "chan"),
        P("dp", "chan"),
        P("dp", None, None, "chan"),
        P(None, "chan"),
        P(None, None, "chan"),
        P(),
    )
    return jax.shard_map(
        per_device, mesh=mesh, in_specs=in_specs, out_specs=out_specs, check_vma=False
    )
```

```python
import functools

import jax
import jax.numpy as jnp
from jax import lax
from jax.experimental import pallas as pl
from jax.experimental.pallas import tpu as pltpu
from jax.sharding import PartitionSpec as P

EPSILON = 1e-05
MOMENTUM = 0.9
DECAY = 0.0005
TRUST = 0.1
F32 = jnp.float32
BF16 = jnp.bfloat16
MESH = pl.DeviceIdType.MESH
PLANES = (3, 1, 2, 0)


def dot_nn(left, right):
    return lax.dot_general(left, right, (((1,), (0,)), ((), ())), preferred_element_type=F32)


def dot_nt(left, right):
    return lax.dot_general(left, right, (((1,), (1,)), ((), ())), preferred_element_type=F32)


def dot_tn(left, right):
    return lax.dot_general(left, right, (((0,), (0,)), ((), ())), preferred_element_type=F32)


def mish_parts(v):
    u = jnp.exp(-jnp.abs(v))
    pos = v >= 0
    num = jnp.where(pos, 1.0 + 2.0 * u, u * (u + 2.0))
    rest = jnp.where(pos, 2.0 * u * u, 2.0)
    den = num + rest
    inv = 1.0 / den
    tangent = num * inv
    slope = tangent + v * (rest * (den + num) * inv * inv) * (jnp.where(pos, 1.0, u) / (1.0 + u))
    return v * tangent, slope


def plane_taps(p):
    rows = ((0, -1), (2, 0)) if p // 2 else ((1, 0),)
    cols = ((0, -1), (2, 0)) if p % 2 else ((1, 0),)
    return [(r * 3 + s, di, dj) for r, di in rows for s, dj in cols]


def group_of(di, dj):
    return (2 if di else 0) + (1 if dj else 0)


class Geometry:
    def __init__(self, big, small, down, neck, n_dp):
        self.nb, self.hb = big[0], big[1] // 2
        self.ns, self.hs = small[0], small[1] // 2
        self.cb = big[3]
        self.ch = down[0]
        self.wc = down[3]
        self.nc = neck[3]
        self.n = n_dp
        self.big_rows = self.nb * self.hb * self.hb
        self.small_rows = self.ns * self.hs * self.hs
        self.rows = self.big_rows + self.small_rows
        self.total_rows = self.rows * n_dp
        self.tiles = [
            (i * self.hb * self.hb, self.hb * self.hb, 1, self.hb) for i in range(self.nb)
        ] + [(self.big_rows, self.small_rows, self.ns, self.hs)]


def shift_tile(value, tile, di, dj):
    _, rows, images, side = tile
    cols = value.shape[-1]
    if di:
        v = value.reshape(images, side, side, cols)
        blank = jnp.zeros((images, 1, side, cols), value.dtype)
        if di < 0:
            v = jnp.concatenate([blank, v[:, :-1]], axis=1)
        else:
            v = jnp.concatenate([v[:, 1:], blank], axis=1)
        value = v.reshape(rows, cols)
    if dj:
        v = pltpu.roll(value, 1 if dj < 0 else rows - 1, 0).reshape(rows // side, side, cols)
        at = lax.broadcasted_iota(jnp.int32, (1, side, cols), 1)
        keep = at >= 1 if dj < 0 else at < side - 1
        value = jnp.where(keep, v, 0.0).reshape(rows, cols)
    return value


def bits_of(n):
    return n.bit_length() - 1


def halving_plan(order):
    left = sorted(order)
    plan = []
    for bit in order:
        at = left.index(bit)
        plan.append((bit, 1 << (len(left) - 1 - at), 1 << at))
        left.remove(bit)
    return plan


CONV_SPLIT = (3, 3, 3)


def pair_bit(n):
    return bits_of(n) - 2


def reductions(g):
    rows = g.ch // g.n
    bits = tuple(range(bits_of(g.n)))
    paired = tuple(bit for bit in bits if bit != pair_bit(g.n))
    return {
        "d2": (8, rows, g.wc, paired),
        "d1": (2, rows, g.wc // 2, paired),
        **{f"c{k}": (1, rows, t * g.nc, paired) for k, t in enumerate(CONV_SPLIT)},
        "a": (1, 2 * rows, g.nc, bits),
        "b": (1, 2 * rows, g.nc, bits),
        "in": (1, rows, g.nc, bits),
    }


def scratch_plan(g):
    n = g.n
    R = g.rows
    s = {}
    s["raw_big"] = ((g.nb * g.hb * 2, 2 * g.hb, g.cb), BF16)
    s["raw_small"] = ((g.ns * g.hs * 2, 2 * g.hs, g.cb), BF16)
    s["xg"] = ((4, 4, R, g.cb), BF16)
    s["wv"] = ((9, g.ch, g.wc), BF16)
    s["wn"] = ((g.ch, 9 * g.nc), BF16)
    s["ab"] = ((2 * g.ch, 2 * g.nc), BF16)
    s["nin"] = ((4, g.ch, g.nc), BF16)
    s["sar"] = ((4, g.wc, g.nc), BF16)
    s["sbr"] = ((4, g.wc, g.nc), BF16)
    s["cmat"] = ((4, g.wc, g.nc), BF16)
    s["pw"] = ((2, 4 * g.wc), F32)
    s["pn"] = ((2, 2, 4 * g.nc), F32)
    s["acc"] = ((4, R, g.wc), F32)
    s["n1"] = ((R, g.wc), F32)
    s["s1"] = ((R, g.wc), F32)
    s["wg"] = ((4, R, g.wc), BF16)
    for k in ("f", "b"):
        s["rs_send" + k] = ((2, R, g.nc), BF16)
        s["rs_recv" + k] = ((2, R, g.nc), BF16)
        s["rs_ys" + k] = ((R, g.nc), BF16)
        s["rs_yr" + k] = ((R, g.nc), BF16)
    s["rs_keep"] = ((2, R, g.nc), F32)
    s["n2"] = ((R, g.nc), F32)
    s["s2"] = ((R, g.nc), F32)
    s["fg"] = ((4, R, g.nc), BF16)
    s["yb"] = ((R, 9 * g.nc), F32)
    s["n3"] = ((R, g.nc), F32)
    s["s3"] = ((R, g.nc), F32)
    s["cg"] = ((R, 9 * g.nc), BF16)
    s["ga"] = ((4, R, g.nc), BF16)
    s["gb"] = ((4, R, g.nc), BF16)
    s["pb"] = ((R, g.nc), BF16)
    s["ng"] = ((4, R, g.nc), BF16)
    s["u"] = ((R, g.wc), F32)
    s["gsh"] = ((4, R, g.wc), BF16)
    s["cs"] = ((4, 2, R, g.cb), BF16)
    s["cr"] = ((4, 2, R, g.cb), BF16)
    s["cys"] = ((4, R, g.cb), BF16)
    s["cyr"] = ((4, R, g.cb), BF16)
    s["st"] = ((6, n, 2, g.wc), F32)
    s["nm"] = ((4 * n, 1, 128), F32)
    s["squares"] = ((1, 128), F32)
    for name, (count, rows, cols, order) in reductions(g).items():
        for stage, (_, high, low) in enumerate(halving_plan(order)):
            s[f"h_{name}_s{stage}"] = ((count, high, 2, low, rows, cols), BF16)
            s[f"h_{name}_r{stage}"] = ((count, high, low, rows, cols), BF16)
    s["xz"] = ((2, 4, R, g.cb), BF16)
    s["fz"] = ((2, R, g.nc), BF16)
    s["cz"] = ((R, g.nc), BF16)
    s["cgz"] = ((R, 9 * g.nc), BF16)
    s["gz"] = ((2, R, g.wc // 2), BF16)
    s["qs"] = ((R, g.wc), BF16)
    s["nb"] = ((R, g.wc), BF16)
    s["nz"] = ((R, g.wc), BF16)
    s["gzs"] = ((4, R, g.wc), BF16)
    s["g_down"] = ((9, g.ch // n, g.wc), F32)
    s["g_conv"] = ((g.ch // n, 9 * g.nc), F32)
    s["p_a"] = ((2 * g.ch // n, g.nc), BF16)
    s["p_b"] = ((2 * g.ch // n, g.nc), BF16)
    s["p_in"] = ((g.ch // n, g.nc), BF16)
    s["g_a"] = ((2 * g.ch // n, g.nc), BF16)
    s["g_b"] = ((2 * g.ch // n, g.nc), BF16)
    s["g_in"] = ((g.ch // n, g.nc), BF16)
    s["m_down"] = ((9, g.ch // n, g.wc), F32)
    s["m_a"] = ((2 * g.ch // n, g.nc), F32)
    s["m_b"] = ((2 * g.ch // n, g.nc), F32)
    s["m_in"] = ((g.ch // n, g.nc), F32)
    s["m_conv"] = ((9, g.ch // n, g.nc), F32)
    s["k_down"] = ((9, g.ch // n, g.wc), BF16)
    s["k_a"] = ((2 * g.ch // n, g.nc), BF16)
    s["k_b"] = ((2 * g.ch // n, g.nc), BF16)
    s["k_in"] = ((g.ch // n, g.nc), BF16)
    s["k_conv"] = ((9, g.ch // n, g.nc), BF16)
    return s


def count_sems(g):
    early = [1 + len(order) for name, (_, _, _, order) in reductions(g).items() if name[0] != "d"]
    return BASE_SEMS + sum(early) + 40 * (bits_of(g.n) - 3)


BASE_SEMS = 96


def mega(g, names, *refs):
    (
        big, small, w_down, w_a, w_b, w_in, w_conv, p_wide, p_neck, c_big, c_small,
        m_down, m_a, m_b, m_in, m_conv,
    ) = refs[:16]
    (
        o_big, o_small, o_gbig, o_gsmall, o_ndown, o_na, o_nb, o_nin, o_nconv,
        o_mdown, o_ma, o_mb, o_min, o_mconv, o_wn, o_nn, o_ln,
    ) = refs[16:33]
    S = dict(zip(names, refs[33:-1], strict=True))
    sems = refs[-1]
    n, R, nc, wc, cb = g.n, g.rows, g.nc, g.wc, g.cb
    dp = lax.axis_index("dp")
    ch = lax.axis_index("chan")
    core = lax.rem(ch, 2)
    half = lax.div(ch, 2)
    sib = half * 2 + (1 - core)
    yp = (1 - half) * 2 + core
    diag = (1 - half) * 2 + (1 - core)
    other = 1 - half

    pair = pair_bit(n)
    pbit = lax.rem(lax.div(dp, 1 << pair), 2)
    mate = (dp + (1 - 2 * pbit) * (1 << pair), ch)
    gives = core != pbit
    takes = core == pbit

    used = [0]
    pending = []
    drain = []

    free = []

    def sem():
        if free:
            return free.pop()
        used[0] += 1
        return sems.at[used[0] - 1]

    load_sems = []

    def local(src, dst, own=None):
        if own is None:
            own = sem()
            load_sems.append(own)
        copy = pltpu.make_async_copy(src, dst, own)
        copy.start()
        return copy

    def remote(src, dst, device, ssem=None, rsem=None):
        copy = pltpu.make_async_remote_copy(
            src_ref=src, dst_ref=dst,
            send_sem=sem() if ssem is None else ssem,
            recv_sem=sem() if rsem is None else rsem,
            device_id=device, device_id_type=MESH,
        )
        if ssem is None:
            pending.append(copy)
        return copy

    def total(view, one):
        return pltpu.make_async_copy(view, view, one)

    def shared(view):
        one = sem()
        drain.append(total(view, one))
        return one
    ld_big = local(big, S["raw_big"])
    ld_small = local(small, S["raw_small"])
    ld_wv = local(w_down, S["wv"])
    ab_sem, wn_sem, ga_sem, gb_sem = sem(), sem(), sem(), sem()
    local(w_a, S["ab"].at[:, pl.ds(0, nc)], ab_sem)
    local(w_b, S["ab"].at[:, pl.ds(nc, nc)], ab_sem)
    ld_ab = total(S["ab"], ab_sem)
    ld_in = local(w_in, S["nin"].at[ch])
    ld_p = [local(p_wide, S["pw"]), local(p_neck, S["pn"])]
    for t in range(9):
        local(w_conv.at[t], S["wn"].at[:, pl.ds(t * nc, nc)], wn_sem)
    ld_wn = total(S["wn"], wn_sem)
    br, sr = g.big_rows, g.small_rows
    ld_c = []
    for k, name, one in ((0, "ga", ga_sem), (1, "gb", gb_sem)):
        local(c_big.at[k], S[name].at[ch, pl.ds(0, br)], one)
        local(c_small.at[k], S[name].at[ch, pl.ds(br, sr)], one)
        ld_c.append(total(S[name].at[ch], one))
    bar = pltpu.get_barrier_semaphore()

    def everyone(act):
        def one(k):
            act((lax.rem(dp + lax.div(k, 4), n), lax.rem(ch + lax.rem(k, 4), 4)))

        if n <= 8:
            for k in range(1, 4 * n):
                one(k)
        else:
            lax.fori_loop(1, 4 * n, lambda k, c: (one(k), c)[1], 0)

    bits = [lax.rem(lax.div(dp, 1 << i), 2) for i in range(bits_of(n))]
    dp_peers = [
        sum(((1 - b) if k >> i & 1 else b) * (1 << i) for i, b in enumerate(bits))
        for k in range(n - 1, 0, -1)
    ]
    peers = [(dp, yp), (dp, sib), (dp, diag)] + [(peer, ch) for peer in dp_peers]
    for peer in peers:
        pl.semaphore_signal(bar, inc=1, device_id=peer, device_id_type=MESH)
    xg = S["xg"]
    ld_big.wait()
    o_gbig[...] = S["raw_big"][...].astype(F32).reshape(o_gbig.shape)
    ld_small.wait()
    o_gsmall[...] = S["raw_small"][...].astype(F32).reshape(o_gsmall.shape)

    def split_plane(p):
        pr, pc = p // 2, p % 2
        xg[ch, p, 0:br] = (
            o_gbig[:, pr, pl.ds(pc, g.hb, stride=2), :].reshape(br, cb).astype(BF16)
        )
        xg[ch, p, br:R] = (
            o_gsmall[:, pr, pl.ds(pc, g.hs, stride=2), :].reshape(sr, cb).astype(BF16)
        )

    class Gather:
        def __init__(self, ref, plane=None, ssems=None, rows=None):
            def block(c):
                if rows is not None:
                    return ref.at[c, rows]
                return ref.at[c] if plane is None else ref.at[c, plane]

            if ssems is None:
                three = ref.at[pl.ds(0, 3)] if rows is None else ref.at[pl.ds(0, 3), rows]
                ssems = [shared(three)] * 3
            self.to_sib = remote(block(ch), block(ch), (dp, sib), ssems[0])
            self.to_far = remote(block(ch), block(ch), (dp, yp), ssems[1])
            self.onward = remote(block(yp), block(yp), (dp, sib), ssems[2])

        def start(self):
            self.to_sib.start()
            self.to_far.start()

        def forward(self):
            self.to_far.wait_recv()
            self.onward.start()

        def near(self):
            self.to_sib.wait_recv()

        def far(self):
            self.onward.wait_recv()

    crop_sems = [shared(xg.at[0]) for _ in range(3)]
    crops = {p: Gather(xg, p, crop_sems) for p in PLANES}
    split_plane(PLANES[0])
    pl.semaphore_wait(bar, len(peers))
    upper, lower = pl.ds(0, R // 2), pl.ds(R // 2, R // 2)

    class Cross:
        def __init__(self, buf, source):
            self.buf, self.source = S[buf], source
            self.ssem, self.rsem = shared(self.buf), sem()
            self.arrived = total(self.buf, self.rsem)
            self.onward = remote(self.buf, self.buf, (dp, sib), self.ssem, self.rsem)

        def send(self, block, h, *plane):
            @pl.when(gives)
            def _():
                remote(
                    self.source.at[(block, *plane)], self.buf.at[(h, *plane)], mate,
                    self.ssem, self.rsem,
                ).start()

        def hand_on(self):
            @pl.when(takes)
            def _():
                self.arrived.wait()
                self.onward.start()

        def finish(self):
            @pl.when(gives)
            def _():
                self.arrived.wait()

    cross_x = Cross("xz", xg)
    crops[PLANES[0]].start()
    cross_x.send(ch, half, PLANES[0])
    for p in PLANES[1:]:
        split_plane(p)
        crops[p].start()
        cross_x.send(ch, half, p)
    ld_in.wait()
    neck_in = Gather(S["nin"])
    ld_ab.wait()

    class Rows:
        def __init__(self, buf, lane):
            ref = S[buf]
            ssem, rsem = shared(ref.at[pl.ds(0, 3)]), sem()
            self.copies = [
                remote(
                    S["ab"].at[pl.ds(dev * wc, wc), pl.ds(lane, nc)], ref.at[ch], (dp, dev),
                    ssem, rsem,
                )
                for dev in (yp, diag, sib)
            ]
            self.arrived = total(ref.at[pl.ds(0, 3)], rsem)
            ref[ch] = S["ab"][pl.ds(ch * wc, wc), lane : lane + nc]

        def start(self):
            for c in self.copies:
                c.start()

        def wait(self):
            self.arrived.wait()

    b_rows = Rows("sbr", nc)
    a_rows = Rows("sar", 0)
    neck_in.start()
    b_rows.start()
    ld_wv.wait()
    wv, acc = S["wv"], S["acc"]

    def conv_part(side, p, first):
        x = jnp.concatenate([xg[2 * side, p], xg[2 * side + 1, p]], axis=1)
        for tap, di, dj in plane_taps(p):
            res = dot_nn(x, wv[tap, pl.ds(side * 2 * cb, 2 * cb), :])
            k = group_of(di, dj)
            if first:
                acc[k] = res
            else:
                acc[k] += res
    for p in PLANES:
        crops[p].near()
        conv_part(half, p, p == PLANES[0])
    for p in PLANES[:-1]:
        crops[p].forward()
        cross_x.send(yp, other, p)
        crops[p].far()
        conv_part(other, p, False)
    for tile in g.tiles:
        at = pl.ds(tile[0], tile[1])
        inner = acc[1, at] + shift_tile(acc[3, at], tile, -1, 0)
        acc[2, at] = shift_tile(acc[2, at], tile, -1, 0) + shift_tile(inner, tile, 0, -1)
    p = PLANES[-1]
    crops[p].forward()
    cross_x.send(yp, other, p)
    crops[p].far()
    conv_part(other, p, False)
    acc[0] = acc[0] + acc[2]

    st = S["st"]
    st_send, st_recv = sem(), [sem(), sem()]

    before = []

    def exchange(phase, first, second, cols):
        st[phase, dp, 0:1, 0:cols] = first
        st[phase, dp, 1:2, 0:cols] = second
        ssem, rsem = st_send, st_recv[phase % 2]
        if before:
            before.pop().wait()
        mine = st.at[phase, dp, :, pl.ds(0, cols)]
        for peer in dp_peers:
            pltpu.make_async_remote_copy(
                src_ref=mine, dst_ref=mine, send_sem=ssem, recv_sem=rsem,
                device_id=(peer, ch), device_id_type=MESH,
            ).start()
        some = st.at[phase, pl.ds(0, n - 1), :, pl.ds(0, cols)]

        before.append(total(some, ssem))

        def finish():
            total(some, rsem).wait()
            return st[phase, :, :, 0:cols]

        return finish

    def norm_start(phase, ref):
        cols = ref.shape[-1]
        mean = jnp.sum(ref[...], axis=0, keepdims=True) * (1.0 / R)
        dev = ref[...] - mean
        return exchange(phase, mean, jnp.sum(dev * dev, axis=0, keepdims=True), cols)

    def norm_finish(finish):
        v = finish()
        tot = jnp.sum(v, axis=0)
        mean = tot[0:1] * (1.0 / n)
        off = v - mean[None]
        spread = jnp.sum(off * off, axis=0)[0:1]
        var = (tot[1:2] + R * spread) * (1.0 / g.total_rows)
        return mean, lax.rsqrt(var + EPSILON)

    def sums_finish(finish):
        tot = jnp.sum(finish(), axis=0)
        return tot[0:1], tot[1:2]
    fin = norm_start(0, acc.at[0])
    for c in ld_p:
        c.wait()
    gain1 = S["pw"][0:1, pl.ds(ch * wc, wc)]
    bias1 = S["pw"][1:2, pl.ds(ch * wc, wc)]
    neck_in.forward()
    neck_in.near()
    neck_in.far()
    b_rows.wait()
    rows_b = jnp.concatenate([S["sbr"][k] for k in range(4)], axis=1)
    for k in range(4):
        S["cmat"][k] = dot_nn(rows_b, S["nin"][k]).astype(BF16)
    mean1, inv1 = norm_finish(fin)
    wg = S["wg"]
    for t0 in range(0, R, 256):
        at = pl.ds(t0, 256)
        normed = (acc[0, at] - mean1) * inv1
        S["n1"][at] = normed
        S["nb"][at] = normed.astype(BF16)
        wg[ch, at] = mish_parts(normed * gain1 + bias1)[0].astype(BF16)

    summed = []

    def reduce_chan(k, pair):
        send, recv = S["rs_send" + k], S["rs_recv" + k]
        ys, yr, keep = S["rs_ys" + k], S["rs_yr" + k], S["rs_keep"]
        parts = [pl.ds(0, R // 2), pl.ds(R // 2, R // 2)]
        s0, sy, r1 = shared(send), shared(ys), sem()
        summed.append(r1)
        c0 = [remote(send.at[0, at], recv.at[0, at], (dp, sib), s0) for at in parts]
        c1 = [remote(send.at[1, at], recv.at[1, at], (dp, sib), s0, r1) for at in parts]
        cy = [remote(ys.at[at], yr.at[at], (dp, yp), sy) for at in parts]
        summed.extend(c.dst_sem for c in (*c0, *cy))
        for at, far, near in zip(parts, c0, c1, strict=True):
            part = pair(at, diag, sib).astype(BF16)
            send[0, at] = part[:, :nc]
            far.start()
            send[1, at] = part[:, nc:]
            near.start()
        for at, near, far in zip(parts, c0, cy, strict=True):
            part = pair(at, yp, ch)
            keep[1, at] = part[:, nc:]
            near.wait_recv()
            ys[at] = (part[:, :nc] + recv[0, at].astype(F32)).astype(BF16)
            far.start()
        total(recv.at[1], r1).wait()
        keep[1] += recv[1].astype(F32)

        def finish():
            for at, far in zip(parts, cy, strict=True):
                far.wait_recv()
                keep[1, at] += yr[at].astype(F32)

        return finish

    def neck_pair(at, d0, d1):
        return dot_nn(
            wg[ch, at], jnp.concatenate([S["cmat"][d0], S["cmat"][d1]], axis=1)
        )
    n_mate = [remote(S["nb"].at[at], S["nz"].at[at], mate) for at in (upper, lower)]
    n_mate[0].start()
    rs_fin = reduce_chan("f", neck_pair)
    for c in ld_c:
        c.wait()
    gb_g = Gather(S["gb"])
    ga_g = Gather(S["ga"])
    wide_g = Gather(wg)
    cross_x.hand_on()
    for t0 in range(0, R, 256):
        at = pl.ds(t0, 256)
        S["s1"][at] = mish_parts(S["n1"][at] * gain1 + bias1)[1]
    rs_fin()
    a_rows.start()
    z2 = S["rs_keep"].at[1]
    fin = norm_start(1, z2)
    n_mate[1].start()
    gain2 = S["pn"][0, 0:1, pl.ds(ch * nc, nc)]
    bias2 = S["pn"][0, 1:2, pl.ds(ch * nc, nc)]
    gain3 = S["pn"][1, 0:1, pl.ds(ch * nc, nc)]
    bias3 = S["pn"][1, 1:2, pl.ds(ch * nc, nc)]
    mean2, inv2 = norm_finish(fin)
    fg = S["fg"]
    for t0 in range(0, R, 256):
        at = pl.ds(t0, 256)
        normed = (z2[at] - mean2) * inv2
        S["n2"][at] = normed
        fg[ch, at] = mish_parts(normed * gain2 + bias2)[0].astype(BF16)
    first_g = Gather(fg)
    first_g.start()
    ld_wn.wait()
    wn, yb = S["wn"], S["yb"]

    def neck_part(side, first):
        x = jnp.concatenate([fg[2 * side], fg[2 * side + 1]], axis=1)
        w = wn[pl.ds(side * 2 * nc, 2 * nc), :]
        if first:
            yb[...] = dot_nn(x, w)
        else:
            yb[...] += dot_nn(x, w)

    first_g.near()
    neck_part(half, True)
    for t0 in range(0, R, 256):
        at = pl.ds(t0, 256)
        S["s2"][at] = mish_parts(S["n2"][at] * gain2 + bias2)[1]
    first_g.forward()
    first_g.far()
    gb_g.start()
    ga_g.start()
    neck_part(other, False)
    z3 = S["n3"]
    for tile in g.tiles:
        at = pl.ds(tile[0], tile[1])
        cols = []
        for s in range(3):
            cols.append(
                yb[at, (3 + s) * nc : (4 + s) * nc]
                + shift_tile(yb[at, s * nc : (s + 1) * nc], tile, -1, 0)
                + shift_tile(yb[at, (6 + s) * nc : (7 + s) * nc], tile, 1, 0)
            )
        z3[at] = (
            cols[1] + shift_tile(cols[0], tile, 0, -1) + shift_tile(cols[2], tile, 0, 1)
        )
    fin = norm_start(2, z3)
    cross_f = Cross("fz", fg)
    cross_f.send(ch, half)
    cross_f.send(yp, other)
    mean3, inv3 = norm_finish(fin)
    q_tot = jnp.zeros((1, nc), F32)
    qn_tot = jnp.zeros((1, nc), F32)
    for t0 in range(0, R, 256):
        at = pl.ds(t0, 256)
        normed = (z3[at] - mean3) * inv3
        slope = mish_parts(normed * gain3 + bias3)[1]
        q = S["gb"][ch, at].astype(F32) * slope
        z3[at] = normed
        S["s3"][at] = q
        q_tot += jnp.sum(q, axis=0, keepdims=True)
        qn_tot += jnp.sum(q * normed, axis=0, keepdims=True)
    fin = exchange(3, qn_tot, q_tot, nc)

    def grad_in(q, normed, gain, inv, qn_sum, q_sum):
        return gain * inv * (
            q - q_sum * (1.0 / g.total_rows) - normed * (qn_sum * (1.0 / g.total_rows))
        )

    stage_sems = {}
    plans = reductions(g)

    class Halving:
        def __init__(self, name, item, *results):
            self.name, self.item, self.results = name, item, results
            self.plan = halving_plan(plans[name][3])
            self.copies = []
            self.alone = S[f"h_{name}_s0"].shape[0] == 1
            if name not in stage_sems:
                stages = range(len(self.plan))
                stage_sems[name] = (
                    [sem()] * len(self.plan)
                    if self.alone
                    else [shared(S[f"h_{name}_s{i}"].at[:, :, 0]) for i in stages]
                )
            for i, (bit, high, low) in enumerate(self.plan):
                own = lax.rem(lax.div(dp, 1 << bit), 2)
                peer = dp + (1 - 2 * own) * (1 << bit)
                send = S[f"h_{name}_s{i}"]
                recv = S[f"h_{name}_r{i}"]
                self.copies.append(
                    remote(
                        send.at[item, :, 1 - own], recv.at[item], (peer, ch), stage_sems[name][i]
                    )
                )

        def start(self, stage=0):
            self.copies[stage].start()

        def step(self, stage):
            bit, high, low = self.plan[stage]
            own = lax.rem(lax.div(dp, 1 << bit), 2)
            send = S[f"h_{self.name}_s{stage}"]
            recv = S[f"h_{self.name}_r{stage}"]
            self.copies[stage].wait_recv()
            if self.alone:
                self.copies[stage].wait_send()
            both = send[self.item, :, own].astype(F32) + recv[self.item].astype(F32)
            if stage + 1 < len(self.plan):
                after = S[f"h_{self.name}_s{stage + 1}"]
                after[self.item] = both.astype(BF16).reshape(after.shape[1:])
                self.start(stage + 1)
            else:
                width = self.results[0].shape[-1]
                for k, ref in enumerate(self.results):
                    ref[...] = both[0, 0, :, k * width : (k + 1) * width].astype(ref.dtype)

    def put_rows(name, value):
        ref = S[f"h_{name}_s0"]
        _, high, _, low, rows, cols = ref.shape
        value = value.astype(BF16)
        for e in range(n):
            r, c = e % (n // 4), e // (n // 4)
            ref[0, e // (2 * low), e // low % 2, e % low] = value[
                r * rows : (r + 1) * rows, c * cols : (c + 1) * cols
            ]

    quarter = n // 4
    at_home = lax.div(dp, quarter) == ch

    class Deliver:
        def __init__(self, name):
            self.src, self.dst = S[f"p_{name}"], S[f"g_{name}"]
            target = (ch * quarter + lax.rem(dp, quarter), lax.div(dp, quarter))
            self.copy = pltpu.make_async_remote_copy(
                src_ref=self.src, dst_ref=self.dst, send_sem=sem(), recv_sem=sem(),
                device_id=target, device_id_type=MESH,
            )

        def start(self):
            @pl.when(at_home)
            def _():
                self.dst[...] = self.src[...]

            @pl.when(jnp.logical_not(at_home))
            def _():
                self.copy.start()

        def finish(self):
            @pl.when(jnp.logical_not(at_home))
            def _():
                self.copy.wait_recv()
                self.copy.wait_send()

    def put(name, item, first_block, value):
        ref = S[f"h_{name}_s0"]
        _, high, _, low, rows, cols = ref.shape
        at = first_block // (2 * low)
        count = value.shape[0] // (rows * 2 * low)
        ref[item, at : at + count] = value.astype(BF16).reshape(count, 2, low, rows, cols)

    for t0 in range(0, R, 256):
        at = pl.ds(t0, 256)
        yb[at, 0:nc] = mish_parts(z3[at] * gain3 + bias3)[0]
    gb_g.forward()
    gb_g.near()
    gb_g.far()
    u = S["u"]
    u[...] = dot_nt(
        jnp.concatenate([S["gb"][k] for k in range(4)], axis=1),
        jnp.concatenate([S["sbr"][k] for k in range(4)], axis=1),
    )
    qn3, q3 = sums_finish(fin)
    cg = S["cg"]

    def tap_shifts(dst, tile, v):
        at = pl.ds(tile[0], tile[1])
        for r in range(3):
            vi = shift_tile(v, tile, 1 - r, 0)
            for s in range(3):
                t = r * 3 + s
                dst[at, t * nc : (t + 1) * nc] = shift_tile(vi, tile, 0, 1 - s).astype(BF16)

    for tile in g.tiles:
        at = pl.ds(tile[0], tile[1])
        v = grad_in(S["s3"][at], z3[at], gain3, inv3, qn3, q3)
        tap_shifts(cg, tile, v.astype(BF16).astype(F32))
    to_mate = remote(cg.at[:, pl.ds(4 * nc, nc)], S["cz"], mate)
    to_mate.start()

    rows = g.ch // n
    reuse = [*load_sems, ab_sem, wn_sem, ga_sem, gb_sem]
    ld_m = [
        local(src, S[name], one)
        for (src, name), one in zip(
            (
                (m_down, "m_down"), (m_a, "m_a"), (m_b, "m_b"), (m_in, "m_in"),
                (m_conv, "m_conv"),
                (w_down.at[:, pl.ds(dp * rows, rows)], "k_down"),
                (w_a.at[pl.ds(dp * 2 * rows, 2 * rows)], "k_a"),
                (w_b.at[pl.ds(dp * 2 * rows, 2 * rows)], "k_b"),
                (w_in.at[pl.ds(dp * rows, rows)], "k_in"),
                (w_conv.at[:, pl.ds(dp * rows, rows)], "k_conv"),
            ),
            reuse,
            strict=True,
        )
    ]

    def back_pair(at, d0, d1):
        w = jnp.concatenate([wn[pl.ds(d0 * nc, nc), :], wn[pl.ds(d1 * nc, nc), :]], axis=0)
        return dot_nt(cg[at], w)

    cross_f.hand_on()
    rs_fin = reduce_chan("b", back_pair)
    ga_g.forward()
    ga_g.near()
    ga_g.far()
    a_rows.wait()
    u[...] += dot_nt(
        jnp.concatenate([S["ga"][k] for k in range(4)], axis=1),
        jnp.concatenate([S["sar"][k] for k in range(4)], axis=1),
    )
    h_a = Halving("a", 0, S["p_a"])
    put_rows("a", dot_tn(wg[ch], jnp.concatenate([S["ga"][k] for k in range(4)], axis=1)))
    h_a.start()
    deliveries = []
    done = {}

    def on(what):
        h = h_down[what] if isinstance(what, int) else what
        stage = done.setdefault((h.name, h.item), 0)
        if stage >= len(h.plan):
            return
        h.step(stage)
        done[h.name, h.item] += 1
        if h.name in ("a", "b", "in") and stage == len(h.plan) - 1:
            deliveries.append(Deliver(h.name))
            deliveries[-1].start()

    starts = [sum(CONV_SPLIT[:k]) * nc for k in range(len(CONV_SPLIT) + 1)]
    h_conv = [
        Halving(f"c{k}", 0, S["g_conv"].at[:, pl.ds(starts[k], starts[k + 1] - starts[k])])
        for k in range(len(CONV_SPLIT))
    ]
    def sq(value):
        v = value * value
        while v.ndim > 2:
            v = jnp.sum(v, axis=0)
        v = jnp.sum(v, axis=0, keepdims=True)
        out = v[:, 0:128]
        for k in range(128, v.shape[1], 128):
            out = out + v[:, k : k + 128]
        return out

    layers = ("down", "a", "b", "in", "conv")
    lane = lax.broadcasted_iota(jnp.int32, (1, 128), 1)

    def add_square(i, value):
        total_sq = jnp.sum(sq(value), axis=1, keepdims=True)
        S["squares"][...] = jnp.where(lane == i, total_sq, S["squares"][...])

    S["squares"][...] = jnp.zeros((1, 128), F32)
    for c in ld_m:
        c.wait()
    for i, name in enumerate(layers):
        add_square(i, S["k_" + name][...].astype(F32))
    rs_fin()
    q_tot = jnp.zeros((1, nc), F32)
    qn_tot = jnp.zeros((1, nc), F32)
    q2r = S["rs_keep"].at[1]
    for t0 in range(0, R, 256):
        at = pl.ds(t0, 256)
        q = q2r[at] * S["s2"][at]
        q2r[at] = q
        q_tot += jnp.sum(q, axis=0, keepdims=True)
        qn_tot += jnp.sum(q * S["n2"][at], axis=0, keepdims=True)
    fin = exchange(4, qn_tot, q_tot, nc)
    to_mate.wait_recv()
    for tile in g.tiles:
        tap_shifts(S["cgz"], tile, S["cz"][pl.ds(tile[0], tile[1])].astype(F32))
    cross_f.finish()
    mine = jnp.concatenate([fg[pbit], fg[pbit + 2]], axis=1)
    theirs = jnp.concatenate([S["fz"][0], S["fz"][1]], axis=1)
    for k, h in enumerate(h_conv):
        cols = slice(starts[k], starts[k + 1])
        put(h.name, 0, 0, dot_tn(mine, cg[:, cols]) + dot_tn(theirs, S["cgz"][:, cols]))
        h.start()


    on(h_a)
    qn2, q2 = sums_finish(fin)
    ng = S["ng"]
    for t0 in range(0, R, 256):
        at = pl.ds(t0, 256)
        ng[ch, at] = grad_in(q2r[at], S["n2"][at], gain2, inv2, qn2, q2).astype(BF16)
    neck_g = Gather(ng)
    neck_g.start()
    def wide_part(side):
        return dot_nt(
            jnp.concatenate([ng[2 * side], ng[2 * side + 1]], axis=1),
            jnp.concatenate([S["cmat"][2 * side], S["cmat"][2 * side + 1]], axis=1),
        )
    neck_g.near()
    u[...] += wide_part(half)
    on(h_a)
    on(h_conv[0])
    neck_g.forward()
    on(h_conv[1])
    neck_g.far()
    wide_g.start()
    u[...] += wide_part(other)
    q_tot = jnp.zeros((1, wc), F32)
    qn_tot = jnp.zeros((1, wc), F32)
    for t0 in range(0, R, 256):
        at = pl.ds(t0, 256)
        q = u[at] * S["s1"][at]
        u[at] = q
        q_tot += jnp.sum(q, axis=0, keepdims=True)
        qn_tot += jnp.sum(q * S["n1"][at], axis=0, keepdims=True)
    fin = exchange(5, qn_tot, q_tot, wc)
    for t0 in range(0, R, 256):
        at = pl.ds(t0, 256)
        S["qs"][at] = (u[at] - q_tot * (1.0 / R) - S["n1"][at] * (qn_tot * (1.0 / R))).astype(BF16)
    hw = wc // 2
    halves = [pl.ds(h * hw, hw) for h in range(2)]
    g_mate = [remote(S["qs"].at[:, halves[h]], S["gz"].at[h], mate) for h in range(2)]
    for c in g_mate:
        c.start()

    ng_whole = jnp.concatenate([ng[k] for k in range(4)], axis=1)
    h_b = Halving("b", 0, S["p_b"])
    cols = []
    for k in range(4):
        back = dot_nt(
            ng_whole,
            jnp.concatenate([S["nin"][c, k * nc : (k + 1) * nc] for c in range(4)], axis=1),
        )
        cols.append((S["gb"][k].astype(F32) + back).astype(BF16))
    put_rows("b", dot_tn(wg[ch], jnp.concatenate(cols, axis=1)))
    on(h_conv[2])
    h_b.start()
    h_in = Halving("in", 0, S["p_in"])
    qn1, q1 = sums_finish(fin)
    gsh, gzs = S["gsh"], S["gzs"]

    for one in (*crops.values(), neck_in, first_g, gb_g, ga_g):
        free.extend((one.to_sib.dst_sem, one.to_far.dst_sem, one.onward.dst_sem))
    free.extend(summed)

    def row_shifts(dst, tile, cols, v):
        at = pl.ds(tile[0], tile[1])
        dst[1, at, cols] = shift_tile(v, tile, 0, 1).astype(BF16)
        v = shift_tile(v, tile, 1, 0)
        dst[2, at, cols] = v.astype(BF16)
        dst[3, at, cols] = shift_tile(v, tile, 0, 1).astype(BF16)

    for tile in g.tiles:
        at = pl.ds(tile[0], tile[1])
        v = grad_in(u[at], S["n1"][at], gain1, inv1, qn1, q1)
        gsh[0, at] = v.astype(BF16)
    for tile in g.tiles:
        at = pl.ds(tile[0], tile[1])
        row_shifts(gsh, tile, slice(0, wc), gsh[0, at].astype(F32))

    where = {tap: (tap, p, k) for tap, p, k in
             ((t, p, group_of(di, dj)) for p in PLANES for t, di, dj in plane_taps(p))}

    def split_job():
        pb = S["pb"]
        split = dot_nn(
            jnp.concatenate([wg[k] for k in range(4)], axis=1), S["ab"][...]
        )
        o_big[0] = split[:br, :nc].astype(BF16)
        o_small[0] = split[br:, :nc].astype(BF16)
        part = split[:, nc:].astype(BF16)
        pb[...] = part
        block = (part.astype(F32) + yb[:, 0:nc]).astype(BF16)
        o_big[1] = block[:br]
        o_small[1] = block[br:]

    def in_job():
        put_rows("in", dot_tn(S["pb"][...], jnp.concatenate([ng[k] for k in range(4)], axis=1)))
        h_in.start()

    taps = [(tap, p, group_of(di, dj)) for p in PLANES for tap, di, dj in plane_taps(p)]
    parts = []
    for h in range(2):
        for p in (PLANES[::-1] if h == 0 else PLANES):
            of_plane = [(tap, k) for tap, q, k in taps if q == p]
            parts += [(h, p, of_plane[i : i + 2]) for i in range(0, len(of_plane), 2)]
    h_down = []
    counts = {1: 0, 2: 0}
    for h, p, two in parts:
        results = [S["g_down"].at[tap, :, halves[h]] for tap, _ in two]
        h_down.append(Halving(f"d{len(two)}", counts[len(two)], *results))
        counts[len(two)] += 1

    def down_part(i):
        h, p, two = parts[i]
        mine = jnp.concatenate([xg[pbit, p], xg[pbit + 2, p]], axis=1)
        theirs = jnp.concatenate([S["xz"][0, p], S["xz"][1, p]], axis=1)
        cols = slice(h * hw, (h + 1) * hw)
        own = jnp.concatenate([gsh[k, :, cols] for _, k in two], axis=1)
        far = jnp.concatenate([gzs[k, :, cols] for _, k in two], axis=1)
        put(h_down[i].name, h_down[i].item, 0, dot_tn(mine, own) + dot_tn(theirs, far))
        h_down[i].start()

    cs, cr, cys, cyr = S["cs"], S["cr"], S["cys"], S["cyr"]
    cs_sem, cys_sem = shared(cs), shared(cys)
    c_sib = {
        p: [remote(cs.at[p, k], cr.at[p, k], (dp, sib), cs_sem) for k in range(2)] for p in PLANES
    }
    c_far = {p: remote(cys.at[p], cyr.at[p], (dp, yp), cys_sem) for p in PLANES}

    def crop_pair(p, d0, d1):
        left, right = [], []
        for tap, di, dj in plane_taps(p):
            left.append(gsh[group_of(di, dj)])
            right.append(
                jnp.concatenate(
                    [wv[tap, pl.ds(d0 * cb, cb), :], wv[tap, pl.ds(d1 * cb, cb), :]], axis=0
                )
            )
        return dot_nt(jnp.concatenate(left, axis=1), jnp.concatenate(right, axis=1))

    def crop_near(p):
        part = crop_pair(p, diag, sib).astype(BF16)
        cs[p, 0] = part[:, :cb]
        c_sib[p][0].start()
        cs[p, 1] = part[:, cb:]
        c_sib[p][1].start()

    def crop_own(p):
        acc[p] = crop_pair(p, yp, ch)

    def crop_send(p):
        c_sib[p][0].wait_recv()
        cys[p] = (acc[p, :, :cb] + cr[p, 0].astype(F32)).astype(BF16)
        c_far[p].start()
        c_sib[p][1].wait_recv()
        acc[p, :, cb:] += cr[p, 1].astype(F32)

    def crop_end(p):
        pr, pc = p // 2, p % 2
        c_far[p].wait_recv()
        v = acc[p, :, cb:] + cyr[p].astype(F32)
        o_gbig[:, pr, pl.ds(pc, g.hb, stride=2), :] = v[:br].reshape(-1, g.hb, cb)
        o_gsmall[:, pr, pl.ds(pc, g.hs, stride=2), :] = v[br:].reshape(-1, g.hs, cb)


    def job(kind, key=None):
        if kind == "d":
            down_part(key)
        elif kind == "near":
            crop_near(key)
        elif kind == "own":
            crop_own(key)
        elif kind == "send":
            crop_send(key)
        elif kind == "end":
            crop_end(key)
        elif kind == "wide":
            wide_g.forward()
            wide_g.near()
        else:
            wide_g.far()
            split_job()
            in_job()

    def receive(h):
        g_mate[h].wait_recv()
        cols = slice(h * hw, (h + 1) * hw)
        theirs = st[5, mate[0], :, cols] * (1.0 / R)
        scale = gain1[:, cols] * inv1[:, cols]
        shift = theirs[1:2] - q1[:, cols] * (1.0 / g.total_rows)
        slope = theirs[0:1] - qn1[:, cols] * (1.0 / g.total_rows)
        for tile in g.tiles:
            at = pl.ds(tile[0], tile[1])
            v = S["gz"][h, at].astype(F32) + shift + S["nz"][at, cols].astype(F32) * slope
            v = (scale * v).astype(BF16)
            gzs[0, at, cols] = v
            row_shifts(gzs, tile, cols, v.astype(F32))

    def both(*pairs):
        for i, *ready in pairs:
            job("d", i)
            for k in ready:
                on(k)

    job("near", 0)
    job("own", 0)
    job("near", 1)
    job("own", 1)
    n_mate[0].wait_recv()
    n_mate[1].wait_recv()
    job("send", 0)
    receive(0)
    cross_x.finish()
    both((0,), (1,))
    job("send", 1)
    on(h_a)
    on(h_b)
    both((2, 0),)
    job("wide")
    both((3,), (4, 1))
    job("split")
    job("near", 2)
    on(2)
    on(3)
    receive(1)
    both((5, 4), (6,))
    job("own", 2)
    job("send", 2)
    on(h_b)
    job("near", 3)
    both((7, 5),)
    on(h_in)
    both((8, 6), (9,))
    job("own", 3)
    on(h_a)
    on(7)
    job("send", 3)
    on(h_in)
    on(8)
    on(h_b)
    on(9)
    on(h_in)
    for h in h_conv:
        on(h)
    add_square(9, S["g_conv"][...])
    job("end", 0)
    job("end", 1)
    for i in range(0, 5):
        on(i)
    job("end", 2)
    for i in range(5, 10):
        on(i)
    job("end", 3)
    for _ in range(bits_of(n)):
        for h in (*h_conv, h_a, h_b, h_in, *h_down):
            on(h)
    for d in deliveries:
        d.finish()
    for i, name in enumerate(layers):
        if name in ("a", "b", "in"):
            add_square(5 + i, S["g_" + name][...].astype(F32))

    grads = {
        "down": S["g_down"][...],
        "a": S["g_a"][...].astype(F32),
        "b": S["g_b"][...].astype(F32),
        "in": S["g_in"][...].astype(F32),
    }
    g_conv = S["g_conv"]
    nm = S["nm"]
    add_square(5, S["g_down"][...])
    place = nm.at[dp * 4 + ch]
    place[...] = S["squares"][...]
    ssem, rsem = sem(), sem()
    everyone(
        lambda peer: pltpu.make_async_remote_copy(
            src_ref=place, dst_ref=place, send_sem=ssem, recv_sem=rsem,
            device_id=peer, device_id_type=MESH,
        ).start()
    )
    some = nm.at[pl.ds(0, 4 * n - 1)]
    total(some, rsem).wait()
    roots = jnp.sqrt(jnp.sum(nm[...], axis=0))
    norms = [jnp.sum(jnp.where(lane == k, roots, 0.0), axis=1, keepdims=True) for k in range(10)]
    row = lax.broadcasted_iota(jnp.int32, (2, 5), 0)
    col = lax.broadcasted_iota(jnp.int32, (2, 5), 1)
    table = jnp.zeros((2, 5), F32)
    for k in range(10):
        table = jnp.where((row == k // 5) & (col == k % 5), norms[k], table)
    o_ln[...] = table
    o_wn[0:1] = qn1
    o_wn[1:2] = q1
    o_nn[0, 0:1] = qn2
    o_nn[0, 1:2] = q2
    o_nn[1, 0:1] = qn3
    o_nn[1, 1:2] = q3

    def update(rate, weight, grad, moment):
        after = MOMENTUM * moment + rate * (grad + DECAY * weight)
        return weight - after, after

    for i, name in enumerate(layers):
        wnorm = norms[i]
        rate = TRUST * wnorm / (norms[5 + i] + DECAY * wnorm)
        o_new, o_next = {
            "down": (o_ndown, o_mdown), "a": (o_na, o_ma), "b": (o_nb, o_mb),
            "in": (o_nin, o_min), "conv": (o_nconv, o_mconv),
        }[name]
        if name == "down":
            for t in range(9):
                new, after = update(
                    rate, S["k_down"][t].astype(F32), S["g_down"][t], S["m_down"][t]
                )
                o_new[t] = new
                o_next[t] = after
        elif name == "conv":
            for t in range(9):
                new, after = update(
                    rate,
                    S["k_conv"][t].astype(F32),
                    g_conv[:, t * nc : (t + 1) * nc],
                    S["m_conv"][t],
                )
                o_new[t] = new
                o_next[t] = after
        else:
            new, after = update(rate, S["k_" + name][...].astype(F32), grads[name], S["m_" + name][...])
            o_new[...] = new
            o_next[...] = after
    for c in pending:
        c.wait_send()
    total(some, ssem).wait()
    before.pop().wait()
    for c in drain:
        c.wait()
    assert used[0] <= sems.shape[0], used[0]


def hand_over(*refs):
    count = len(refs) // 2
    copies = [
        pltpu.make_async_copy(refs[k], refs[count + k], refs[-1].at[k]) for k in range(count)
    ]
    for c in copies:
        c.start()
    for c in copies:
        c.wait()


def per_device(
    big_crops, small_crops, conv_down, split_a, split_b, neck_in, neck_conv, norm_wide, norm_neck,
    cot_big, cot_small, mom_down, mom_a, mom_b, mom_in, mom_conv,
):
    n = lax.axis_size("dp")
    g = Geometry(big_crops.shape, small_crops.shape, conv_down.shape, neck_conv.shape, n)

    def taps_first(w):
        return jnp.transpose(w, (1, 2, 0, 3)).reshape(9, w.shape[0], w.shape[3])

    def taps_back(w):
        return jnp.transpose(w.reshape(3, 3, w.shape[1], w.shape[2]), (2, 0, 1, 3))

    args = (
        big_crops.reshape(g.nb * g.hb * 2, 2 * g.hb, g.cb),
        small_crops.reshape(g.ns * g.hs * 2, 2 * g.hs, g.cb),
        taps_first(conv_down), split_a, split_b, neck_in, taps_first(neck_conv),
        norm_wide, norm_neck,
        cot_big.reshape(2, g.big_rows, g.nc), cot_small.reshape(2, g.small_rows, g.nc),
        taps_first(mom_down), mom_a, mom_b, mom_in, taps_first(mom_conv),
    )
    sds = jax.ShapeDtypeStruct
    up = [
        sds((9, g.ch // n, g.wc), F32), sds(mom_a.shape, F32), sds(mom_b.shape, F32),
        sds(mom_in.shape, F32), sds((9, g.ch // n, g.nc), F32),
    ]
    out_shape = [
        sds((2, g.big_rows, g.nc), BF16), sds((2, g.small_rows, g.nc), BF16),
        sds((g.nb * g.hb, 2, 2 * g.hb, g.cb), F32), sds((g.ns * g.hs, 2, 2 * g.hs, g.cb), F32),
        *up, *up,
        sds((2, g.wc), F32), sds((2, 2, g.nc), F32), sds((2, 5), F32),
    ]
    anywhere = pl.BlockSpec(memory_space=pl.ANY)
    vmem = pl.BlockSpec(memory_space=pltpu.VMEM)
    plan = scratch_plan(g)
    res = pl.pallas_call(
        functools.partial(mega, g, tuple(plan)),
        out_shape=[pltpu.VMEM(o.shape, o.dtype) for o in out_shape],
        in_specs=[anywhere] * 16,
        out_specs=[vmem] * 17,
        scratch_shapes=[pltpu.VMEM(shape, dtype) for shape, dtype in plan.values()]
        + [pltpu.SemaphoreType.DMA((count_sems(g),))],
        compiler_params=pltpu.CompilerParams(
            collective_id=0, has_side_effects=True, vmem_limit_bytes=58 * 2**20
        ),
    )(*args)
    res = pl.pallas_call(
        hand_over,
        out_shape=out_shape,
        in_specs=[anywhere] * 17,
        out_specs=[anywhere] * 17,
        scratch_shapes=[pltpu.SemaphoreType.DMA((17,))],
        compiler_params=pltpu.CompilerParams(vmem_limit_bytes=2**20),
    )(*res)
    res = list(res)
    res[0] = res[0].reshape(cot_big.shape)
    res[1] = res[1].reshape(cot_small.shape)
    res[2] = res[2].reshape(big_crops.shape)
    res[3] = res[3].reshape(small_crops.shape)
    for k in (4, 8, 9, 13):
        res[k] = taps_back(res[k])
    return tuple(res)


def solution(mesh):
    in_specs = (
        P("dp", None, None, "chan"),
        P("dp", None, None, "chan"),
        P(None, None, None, "chan"),
        P(None, "chan"),
        P(None, "chan"),
        P(None, "chan"),
        P(None, None, None, "chan"),
        P(),
        P(),
        P(None, "dp", None, None, "chan"),
        P(None, "dp", None, None, "chan"),
        P("dp", None, None, "chan"),
        P("dp", "chan"),
        P("dp", "chan"),
        P("dp", "chan"),
        P("dp", None, None, "chan"),
    )
    out_specs = (
        P(None, "dp", None, None, "chan"),
        P(None, "dp", None, None, "chan"),
        P("dp", None, None, "chan"),
        P("dp", None, None, "chan"),
        P("dp", None, None, "chan"),
        P("dp", "chan"),
        P("dp", "chan"),
        P("dp", "chan"),
        P("dp", None, None, "chan"),
        P("dp", None, None, "chan"),
        P("dp", "chan"),
        P("dp", "chan"),
        P("dp", "chan"),
        P("dp", None, None, "chan"),
        P(None, "chan"),
        P(None, None, "chan"),
        P(),
    )
    return jax.shard_map(
        per_device, mesh=mesh, in_specs=in_specs, out_specs=out_specs, check_vma=False
    )
```
